32 devices in a mesh: group: 2 (over y), tile: 4 (over z), list: 4 (over x, core).
Axes of the slice: x: 2, y: 2, z: 4, core: 2. Of those that a mesh axis runs over, the one named last changes fastest.
Arguments:
- probes: float32 [8192, 256], P(('group', 'tile', 'list')), parts along dimension 0, may hold values from -6 to 6
- right_bases: bfloat16 [8, 1, 96, 1024], P(('group', 'tile'), None, 'list'), parts along dimension 0, may hold values from -0.1875 to 0.1875
- left_bases: bfloat16 [8, 1, 96, 1024], P(('group', 'tile'), None, 'list'), parts along dimension 0, may hold values from -0.625 to 0.625
- near_tiles: bfloat16 [8, 1024, 3, 1024], P(('group', 'tile'), None, None, 'list'), parts along dimension 0, may hold values from -0.109375 to 0.109375
- tile_ranks: int32 [8, 1], P(('group', 'tile')), parts along dimension 0, may hold values from 32 to 96
- column_rows: int32 [4, 1], P('tile'), may hold values from 0 to 3, as said below
- row_columns: int32 [4, 1], P('tile'), may hold values from 0 to 3, as said below
Outputs:
- product: float32 [8192, 256], P(('group', 'tile', 'list')), parts along dimension 0
The draws below stay inside these ranges and needn't reach their ends.
There are 2 independent parts, one for each index of `group`. The reference program is written for one: setup_inputs(seed, part) draws one part's arguments, and reference() takes and returns one part's arrays. A program takes and returns all parts, laid end to end along the dimension named above; an argument that names none is the same for every part. Nothing has to cross between parts.
Inputs may be any that keep to these rules, and one draw needn't show every extreme that they name: `column_rows`: each row j lists 1 distinct tile rows. Tile (i, j) is listed in row j here exactly when j is listed in row i of row_columns. A listed tile may lie beside the diagonal; its low-rank term then adds to the dense tile. `row_columns`: each row i lists 1 distinct tile columns, matching column_rows.
All inputs are finite; a program needn't handle non-finite values.
Results may differ from the reference program's by a relative error of at most 0.0048.
Values may be sent and summed in bfloat16 or wider, within the bound.
No kernel may reach another device: no remote copies, remote signals or barrier semaphores. Data moves between devices by JAX's collectives and lax.ppermute only.
A program may use at most 64 MiB of HBM per device.

```python
import jax
import jax.numpy as jnp
from jax import lax

TILE = 1024
PROBES = 256
RMAX = 96
RMIN = 32
NT = 4
KT = 1
N = 4096


def pattern_parts(key):
    from_label = jax.random.permutation(jax.random.fold_in(key, 13), NT).astype(jnp.int32)
    to_label = from_label
    counting = jnp.arange(NT, dtype=jnp.int32)
    from_inverse = jnp.zeros((NT,), jnp.int32).at[from_label].set(counting)
    to_inverse = from_inverse
    magnitude = jnp.arange(KT, dtype=jnp.int32) + 1
    signs = jax.random.randint(jax.random.fold_in(key, 23), (KT,), 0, 2).astype(jnp.int32) * 2 - 1
    offsets = (magnitude * signs + NT) % NT
    order = jax.random.permutation(jax.random.fold_in(key, 19), KT).astype(jnp.int32)
    offsets = offsets[order]
    return (from_label, to_label, from_inverse, to_inverse, offsets)


def draw_column_rows(key, part):
    from_label, to_label, from_inverse, to_inverse, offsets = pattern_parts(key)
    return to_inverse[(from_label[:, None] + offsets[None, :]) % NT].astype(jnp.int32)


def draw_row_columns(key, part):
    from_label, to_label, from_inverse, to_inverse, offsets = pattern_parts(key)
    return from_inverse[(to_label[:, None] - offsets[None, :] + NT) % NT].astype(jnp.int32)


def draw_tile_ranks(key, part):
    entries = NT * KT
    values = jax.random.randint(jax.random.fold_in(key, 3), (entries,), RMIN, RMAX + 1)
    top_slot = jax.random.randint(jax.random.fold_in(key, 5), (), 0, entries)
    low_slot = (top_slot + 1 + jax.random.randint(jax.random.fold_in(key, 7), (), 0, entries - 1)) % entries
    values = values.at[top_slot].set(RMAX).at[low_slot].set(RMIN)
    return values.reshape(NT, KT).astype(jnp.int32)


def block_scale(key, dims, shards, smallest, high):
    gain, own = 1.0, jax.random.fold_in(key, 6)
    for axis_at, parts in shards:
        steps = jnp.exp(jax.random.uniform(jax.random.fold_in(own, axis_at), (parts,), jnp.float32, smallest / len(shards), high / len(shards)))
        gain = gain * jnp.repeat(steps, dims[axis_at] // parts).reshape([-1 if axis == axis_at else 1 for axis in range(len(dims))])
    return gain


def centred(stream_key, shape, spread, bound, split=(), kind=jnp.bfloat16):
    level = block_scale(stream_key, shape, split, -0.22, 0.18) if split else 1.0
    array = jax.random.normal(stream_key, shape, jnp.float32) * spread * level
    return jnp.minimum(jnp.maximum(array, -bound), bound).astype(kind)


def setup_inputs(seed: int = 0, part: int = 0) -> dict:
    arg_keys = jax.random.split(jax.random.key(seed), 8)
    part_keys = jax.random.split(jax.random.fold_in(arg_keys[7], part), 8)
    probes = centred(part_keys[0], (N, PROBES), 1.0, 6.0, ((0, 16),), jnp.float32)
    right_bases = centred(part_keys[1], (NT, KT, RMAX, TILE), TILE ** -0.5, 0.1875, ((0, 4), (2, 4)))
    left_bases = centred(part_keys[2], (NT, KT, RMAX, TILE), (KT * RMAX) ** -0.5, 0.625, ((0, 4), (2, 4)))
    near_tiles = centred(part_keys[3], (NT, TILE, 3, TILE), (3 * TILE) ** -0.5, 0.109375, ((0, 4), (3, 4)))
    tile_ranks = draw_tile_ranks(jax.random.fold_in(jax.random.fold_in(arg_keys[7], part), 71), part)
    column_rows = draw_column_rows(jax.random.fold_in(arg_keys[7], 71), part)
    row_columns = draw_row_columns(jax.random.fold_in(arg_keys[7], 71), part)
    return {"probes": probes, "right_bases": right_bases, "left_bases": left_bases, "near_tiles": near_tiles, "tile_ranks": tile_ranks, "column_rows": column_rows, "row_columns": row_columns}


def image_of(operand, right_bases, left_bases, near_tiles, tile_ranks, column_rows, row_columns):
    blocks = operand.reshape(NT, TILE, PROBES)
    rank_level = jnp.arange(RMAX, dtype=jnp.int32)

    def column_terms(col_index):
        flattened = right_bases[col_index].reshape(KT * RMAX, TILE)
        values = jnp.dot(flattened, blocks[col_index], preferred_element_type=jnp.float32)
        values = values.reshape(KT, RMAX, PROBES)
        rank_mask = rank_level[None, :] < tile_ranks[col_index][:, None]
        return jnp.where(rank_mask[:, :, None], values, 0.0).astype(jnp.bfloat16)

    coefficients = lax.map(column_terms, jnp.arange(NT, dtype=jnp.int32))
    empty = jnp.zeros((1, TILE, PROBES), operand.dtype)
    padded = jnp.concatenate([empty, blocks, empty], axis=0)

    def row_terms(row_index):
        sources = row_columns[row_index]
        matches = column_rows[sources] == row_index
        slot_index = jnp.argmax(matches, axis=1).astype(jnp.int32)
        selected = coefficients[sources, slot_index].reshape(KT * RMAX, PROBES)
        far_sum = jnp.dot(left_bases[row_index].reshape(KT * RMAX, TILE).T, selected, preferred_element_type=jnp.float32)
        window = lax.dynamic_slice_in_dim(padded, row_index, 3, 0).reshape(3 * TILE, PROBES)
        near_sum = jnp.dot(near_tiles[row_index].reshape(TILE, 3 * TILE), window, preferred_element_type=jnp.float32)
        return near_sum + far_sum

    rows_all = lax.map(row_terms, jnp.arange(NT, dtype=jnp.int32))
    return rows_all.reshape(N, PROBES)


def reference(probes, right_bases, left_bases, near_tiles, tile_ranks, column_rows, row_columns):
    probe_bf = probes.astype(jnp.bfloat16)
    first_pass = image_of(probe_bf, right_bases, left_bases, near_tiles, tile_ranks, column_rows, row_columns).astype(jnp.bfloat16)
    return image_of(first_pass, right_bases, left_bases, near_tiles, tile_ranks, column_rows, row_columns)
```

```python
import functools

import jax
import jax.numpy as jnp
from jax import lax
from jax.experimental import pallas as pl
from jax.experimental.pallas import tpu as pltpu
from jax.sharding import PartitionSpec as P

BF = jnp.bfloat16
F32 = jnp.float32


def shifted(block, axis, distance):
    devices = range(lax.axis_size(axis))
    route = [(i - distance, i) for i in devices if i - distance in devices]
    return lax.ppermute(block, axis, route)


def image_part(operand, right_bases, left_bases, near_tiles, tile_ranks, column_rows, row_columns):
    tile_slots = right_bases.shape[1]
    rank_part = right_bases.shape[2]
    tile_rows = right_bases.shape[3]
    probe_count = operand.shape[1]
    tile_count = lax.axis_size("tile")
    right_flat = right_bases.reshape(tile_slots * rank_part, tile_rows)
    left_flat = left_bases.reshape(tile_slots * rank_part, tile_rows)
    dense_flat = near_tiles.reshape(tile_rows, -1)
    values = jnp.dot(
        right_flat,
        lax.all_gather(operand, "list", axis=0, tiled=True),
        preferred_element_type=F32,
    )
    rank_level = lax.axis_index("list") * rank_part + lax.iota(jnp.int32, rank_part)
    rank_mask = rank_level[None, :] < tile_ranks[0][:, None]
    coefficients = jnp.where(
        rank_mask[:, :, None], values.reshape(tile_slots, rank_part, probe_count), 0.0
    ).astype(BF)
    targets = (column_rows[0][None, :] == lax.iota(jnp.int32, tile_count)[:, None]).astype(BF)
    outgoing = jnp.einsum(
        "dk,krp->drp", targets, coefficients, preferred_element_type=F32
    ).astype(BF)
    sources = (row_columns[0][:, None] == lax.iota(jnp.int32, tile_count)[None, :]).astype(BF)
    chosen = jnp.einsum(
        "kj,jrp->krp",
        sources,
        lax.all_to_all(outgoing, "tile", split_axis=0, concat_axis=0, tiled=True),
        preferred_element_type=F32,
    ).astype(BF)
    chosen = chosen.reshape(tile_slots * rank_part, -1)
    far_sum = lax.dot_general(
        left_flat, chosen, (((0,), (0,)), ((), ())), preferred_element_type=F32
    )
    arrived = {}
    for offset in (1, -1):
        arrived[offset] = shifted(operand, "tile", offset)
    stacked = jnp.concatenate([arrived[1], operand, arrived[-1]], axis=0)
    near_sum = jnp.dot(dense_flat, stacked, preferred_element_type=F32)
    partial_image = near_sum + far_sum
    return lax.psum_scatter(partial_image, "list", scatter_dimension=0, tiled=True)


def many_slots(probes, right_bases, left_bases, near_tiles, tile_ranks, column_rows, row_columns):
    rest = (right_bases, left_bases, near_tiles, tile_ranks, column_rows, row_columns)
    first_pass = image_part(probes.astype(BF), *rest).astype(BF)
    return image_part(first_pass, *rest)


VMEM = pl.BlockSpec(memory_space=pltpu.VMEM)
SMEM = pl.BlockSpec(memory_space=pltpu.SMEM)


def image_kernel(tile_count, near_ref, left_ref, blocks_ref, right_ref, columns_ref, out_ref):
    me = lax.axis_index("tile")
    rows = near_ref.shape[2]
    parts = out_ref.shape[0]
    source = columns_ref[0, 0]
    coefficients = jnp.dot(
        right_ref[source], blocks_ref[source], preferred_element_type=F32
    ).astype(BF)
    above = jnp.where(me > 0, blocks_ref[jnp.maximum(me - 1, 0)], 0)
    below = jnp.where(me < tile_count - 1, blocks_ref[jnp.minimum(me + 1, tile_count - 1)], 0)
    own = blocks_ref[me]
    for part in range(parts):
        cut = slice(part * rows, (part + 1) * rows)
        total = lax.dot_general(
            left_ref[:, cut], coefficients, (((0,), (0,)), ((), ())), preferred_element_type=F32
        )
        for side, block in enumerate((above, own, below)):
            total += jnp.dot(near_ref[side, cut, :], block, preferred_element_type=F32)
        out_ref[part] = total.astype(out_ref.dtype)


def image(near, left, blocks, right, row_columns):
    tile_count, rows, probes = blocks.shape
    parts = near.shape[1] // rows
    flops = 2 * near.size * probes
    return pl.pallas_call(
        functools.partial(image_kernel, tile_count),
        out_shape=jax.ShapeDtypeStruct((parts, rows, probes), BF),
        in_specs=[VMEM, VMEM, VMEM, VMEM, SMEM],
        out_specs=VMEM,
        compiler_params=pltpu.CompilerParams(vmem_limit_bytes=40 * 2**20),
        cost_estimate=pl.CostEstimate(
            flops=flops, bytes_accessed=2 * near.size, transcendentals=0
        ),
    )(near, left, blocks, right, row_columns)


def one_slot(probes, right_bases, left_bases, near_tiles, tile_ranks, column_rows, row_columns):
    rank_part, tile_rows = right_bases.shape[2:]
    rows, probe_count = probes.shape
    list_count = lax.axis_size("list")
    ranks = rank_part * list_count
    me = lax.axis_index("list")
    bases = jnp.stack([right_bases[0, 0], left_bases[0, 0]])
    bases = lax.all_gather(bases, "list", axis=0)
    left = bases[:, 1].reshape(ranks, tile_rows)
    right = lax.dynamic_slice_in_dim(bases[:, 0], me * rows, rows, 2).reshape(ranks, rows)
    keep = lax.iota(jnp.int32, ranks) < tile_ranks[0, 0]
    right = jnp.where(keep[:, None], right, 0)
    near = near_tiles[0].transpose(1, 0, 2)
    block = probes.astype(BF)
    blocks = lax.all_gather(jnp.concatenate([block, right]), "tile", axis=0)
    right, blocks = blocks[:, rows:], blocks[:, :rows]
    partial = image(near, left, blocks, right, row_columns)
    arrived = lax.all_to_all(partial, "list", 0, 0, tiled=True)
    first_pass = jnp.sum(arrived.astype(F32), axis=0).astype(BF)
    blocks = lax.all_gather(first_pass, "tile", axis=0)
    partial = image(near, left, blocks, right, row_columns)
    arrived = lax.all_to_all(partial, "list", 0, 0, tiled=True)
    return jnp.sum(arrived.astype(F32), axis=0)


def local(probes, right_bases, left_bases, near_tiles, tile_ranks, column_rows, row_columns):
    small = right_bases.shape[1] == 1 and lax.axis_size("tile") <= 4
    form = one_slot if small else many_slots
    return form(
        probes, right_bases, left_bases, near_tiles, tile_ranks, column_rows, row_columns
    )


def solution(mesh):
    placed = (
        P(("group", "tile", "list"), None),
        P(("group", "tile"), None, "list", None),
        P(("group", "tile"), None, "list", None),
        P(("group", "tile"), None, None, "list"),
        P(("group", "tile"), None),
        P("tile", None),
        P("tile", None),
    )
    return jax.shard_map(
        local,
        mesh=mesh,
        in_specs=placed,
        out_specs=P(("group", "tile", "list"), None),
        check_vma=False,
    )
```

```python
import functools

import jax
import jax.numpy as jnp
from jax import lax
from jax.experimental import pallas as pl
from jax.experimental.pallas import tpu as pltpu
from jax.sharding import PartitionSpec as P

BF = jnp.bfloat16
F32 = jnp.float32


def shifted(block, axis, distance):
    devices = range(lax.axis_size(axis))
    route = [(i - distance, i) for i in devices if i - distance in devices]
    return lax.ppermute(block, axis, route)


def image_part(operand, right_bases, left_bases, near_tiles, tile_ranks, column_rows, row_columns):
    tile_slots = right_bases.shape[1]
    rank_part = right_bases.shape[2]
    tile_rows = right_bases.shape[3]
    probe_count = operand.shape[1]
    tile_count = lax.axis_size("tile")
    right_flat = right_bases.reshape(tile_slots * rank_part, tile_rows)
    left_flat = left_bases.reshape(tile_slots * rank_part, tile_rows)
    dense_flat = near_tiles.reshape(tile_rows, -1)
    values = jnp.dot(
        right_flat,
        lax.all_gather(operand, "list", axis=0, tiled=True),
        preferred_element_type=F32,
    )
    rank_level = lax.axis_index("list") * rank_part + lax.iota(jnp.int32, rank_part)
    rank_mask = rank_level[None, :] < tile_ranks[0][:, None]
    coefficients = jnp.where(
        rank_mask[:, :, None], values.reshape(tile_slots, rank_part, probe_count), 0.0
    ).astype(BF)
    targets = (column_rows[0][None, :] == lax.iota(jnp.int32, tile_count)[:, None]).astype(BF)
    outgoing = jnp.einsum(
        "dk,krp->drp", targets, coefficients, preferred_element_type=F32
    ).astype(BF)
    sources = (row_columns[0][:, None] == lax.iota(jnp.int32, tile_count)[None, :]).astype(BF)
    chosen = jnp.einsum(
        "kj,jrp->krp",
        sources,
        lax.all_to_all(outgoing, "tile", split_axis=0, concat_axis=0, tiled=True),
        preferred_element_type=F32,
    ).astype(BF)
    chosen = chosen.reshape(tile_slots * rank_part, -1)
    far_sum = lax.dot_general(
        left_flat, chosen, (((0,), (0,)), ((), ())), preferred_element_type=F32
    )
    arrived = {}
    for offset in (1, -1):
        arrived[offset] = shifted(operand, "tile", offset)
    stacked = jnp.concatenate([arrived[1], operand, arrived[-1]], axis=0)
    near_sum = jnp.dot(dense_flat, stacked, preferred_element_type=F32)
    partial_image = near_sum + far_sum
    return lax.psum_scatter(partial_image, "list", scatter_dimension=0, tiled=True)


def many_slots(probes, right_bases, left_bases, near_tiles, tile_ranks, column_rows, row_columns):
    rest = (right_bases, left_bases, near_tiles, tile_ranks, column_rows, row_columns)
    first_pass = image_part(probes.astype(BF), *rest).astype(BF)
    return image_part(first_pass, *rest)


VMEM = pl.BlockSpec(memory_space=pltpu.VMEM)
SMEM = pl.BlockSpec(memory_space=pltpu.SMEM)


def chosen_coefficients(tile_count, columns_ref, coefficient_refs):
    distance = lax.rem(lax.axis_index("tile") - columns_ref[0, 0] + tile_count, tile_count)
    chosen = coefficient_refs[0][...]
    for step in range(1, tile_count):
        chosen = jnp.where(distance == step, coefficient_refs[step][...], chosen)
    return chosen


def row_part(near_ref, left_ref, block_refs, coefficients, start):
    rows = near_ref.shape[2]
    cut = pl.ds(pl.multiple_of(start, rows), rows)
    total = lax.dot_general(
        left_ref[:, cut], coefficients, (((0,), (0,)), ((), ())), preferred_element_type=F32
    )
    for side, block_ref in enumerate(block_refs):
        total += jnp.dot(near_ref[side, cut, :], block_ref[...], preferred_element_type=F32)
    return total


def first_kernel(tile_count, rank_part, near_ref, left_ref, right_ref, ranks_ref, columns_ref, *refs):
    block_refs, coefficient_refs, (keep_ref, send_ref) = refs[:3], refs[3:-2], refs[-2:]
    rows = near_ref.shape[2]
    groups, rank_rows = right_ref.shape[:2]
    me = lax.axis_index("list")
    coefficients = chosen_coefficients(tile_count, columns_ref, coefficient_refs)
    sums = [jnp.zeros((rank_rows, rows), F32)] * groups
    for turn in range(groups):
        part = me ^ turn
        total = row_part(near_ref, left_ref, block_refs, coefficients, part * rows)
        out_ref = send_ref if turn % 2 else keep_ref
        out_ref[turn // 2, :rows, :] = total.astype(out_ref.dtype)
        rounded = total.astype(BF)
        cut = pl.ds(pl.multiple_of(part * rows, rows), rows)
        for group in range(groups):
            sums[group] += jnp.dot(
                right_ref[me ^ group, :, cut], rounded, preferred_element_type=F32
            )
    slot = lax.broadcasted_iota(jnp.int32, (rank_rows, rows), 0)
    for turn in range(groups):
        level = (me ^ turn) * rank_part + slot
        out_ref = send_ref if turn % 2 else keep_ref
        out_ref[turn // 2, rows:, :] = jnp.where(
            level < ranks_ref[0, 0], sums[turn], 0.0
        ).astype(out_ref.dtype)


def second_kernel(tile_count, near_ref, left_ref, columns_ref, *refs):
    block_refs, coefficient_refs, (keep_ref, send_ref) = refs[:3], refs[3:-2], refs[-2:]
    rows = near_ref.shape[2]
    me = lax.axis_index("list")
    coefficients = chosen_coefficients(tile_count, columns_ref, coefficient_refs)
    for turn in range(2 * keep_ref.shape[0]):
        total = row_part(near_ref, left_ref, block_refs, coefficients, (me ^ turn) * rows)
        out_ref = send_ref if turn % 2 else keep_ref
        out_ref[turn // 2] = total.astype(out_ref.dtype)


def call(kernel, out_rows, near, operands, smem):
    rows = near.shape[2]
    half = near.shape[1] // rows // 2
    shape = (half, out_rows, operands[-1].shape[-1])
    return pl.pallas_call(
        kernel,
        out_shape=(jax.ShapeDtypeStruct(shape, F32), jax.ShapeDtypeStruct(shape, SEND)),
        in_specs=[SMEM if index in smem else VMEM for index in range(len(operands) + 1)],
        out_specs=(VMEM, VMEM),
        compiler_params=pltpu.CompilerParams(vmem_limit_bytes=40 * 2**20),
        cost_estimate=pl.CostEstimate(
            flops=2 * near.size * shape[2], bytes_accessed=2 * near.size, transcendentals=0
        ),
    )(near, *operands)


SEND = F32


def rotated(block, axis, distance):
    count = lax.axis_size(axis)
    return lax.ppermute(block, axis, [(i, (i + distance) % count) for i in range(count)])


def swapped(block, axis, bit):
    return lax.ppermute(block, axis, [(i, i ^ bit) for i in range(lax.axis_size(axis))])


def wrapped(block, axis):
    last = lax.axis_size(axis) - 1
    return lax.ppermute(block, axis, [(0, last), (last, 0)])


def list_sum(keep, send):
    pair = keep + swapped(send, "list", 1)
    return pair[0] + swapped(pair[1].astype(BF), "list", 2)


def one_slot(probes, right_bases, left_bases, near_tiles, tile_ranks, column_rows, row_columns):
    rank_part, tile_rows = right_bases.shape[2:]
    rows = probes.shape[0]
    tile_count = lax.axis_size("tile")
    rank_rows = -(-rank_part // 16) * 16
    padding = jnp.zeros((rank_rows - rank_part, tile_rows), BF)
    own_right = jnp.concatenate([right_bases[0, 0], padding])
    left = jnp.concatenate([left_bases[0, 0], padding])
    near = near_tiles[0].transpose(1, 0, 2)
    block = probes.astype(BF)
    above, below = shifted(block, "tile", 1), shifted(block, "tile", -1)
    column = lax.all_gather(block, "list", axis=0, tiled=True)
    right = lax.all_gather(own_right, "list", axis=0)
    values = jnp.dot(own_right, column, preferred_element_type=F32)
    level = lax.axis_index("list") * rank_part + lax.iota(jnp.int32, rank_rows)
    own = jnp.where((level < tile_ranks[0, 0])[:, None], values, 0.0).astype(BF)
    coefficients = [own] + [rotated(own, "tile", step) for step in range(1, tile_count)]
    keep, send = call(
        functools.partial(first_kernel, tile_count, rank_part),
        rows + rank_rows,
        near,
        (left, right, tile_ranks, row_columns, above, block, below, *coefficients),
        (3, 4),
    )
    both = list_sum(keep, send).astype(BF)
    above, below = shifted(both, "tile", 1), shifted(both, "tile", -1)
    own = both[rows:]
    ends = wrapped(own, "tile")
    me = lax.axis_index("tile")
    coefficients = [own]
    coefficients.append(jnp.where(me == 0, ends, above[rows:]))
    coefficients += [rotated(own, "tile", step) for step in range(2, tile_count - 1)]
    coefficients.append(jnp.where(me == tile_count - 1, ends, below[rows:]))
    keep, send = call(
        functools.partial(second_kernel, tile_count),
        rows,
        near,
        (left, row_columns, above[:rows], both[:rows], below[:rows], *coefficients),
        (2,),
    )
    return list_sum(keep, send)


def local(probes, right_bases, left_bases, near_tiles, tile_ranks, column_rows, row_columns):
    few = lax.axis_size("tile") == 4 and lax.axis_size("list") == 4
    small = right_bases.shape[1] == 1 and few
    form = one_slot if small else many_slots
    return form(
        probes, right_bases, left_bases, near_tiles, tile_ranks, column_rows, row_columns
    )


def solution(mesh):
    placed = (
        P(("group", "tile", "list"), None),
        P(("group", "tile"), None, "list", None),
        P(("group", "tile"), None, "list", None),
        P(("group", "tile"), None, None, "list"),
        P(("group", "tile"), None),
        P("tile", None),
        P("tile", None),
    )
    return jax.shard_map(
        local,
        mesh=mesh,
        in_specs=placed,
        out_specs=P(("group", "tile", "list"), None),
        check_vma=False,
    )
```

```python
import functools

import jax
import jax.numpy as jnp
from jax import lax
from jax.experimental import pallas as pl
from jax.experimental.pallas import tpu as pltpu
from jax.sharding import PartitionSpec as P

BF = jnp.bfloat16
F32 = jnp.float32


def shifted(block, axis, distance):
    devices = range(lax.axis_size(axis))
    route = [(i - distance, i) for i in devices if i - distance in devices]
    return lax.ppermute(block, axis, route)


def image_part(operand, right_bases, left_bases, near_tiles, tile_ranks, column_rows, row_columns):
    tile_slots = right_bases.shape[1]
    rank_part = right_bases.shape[2]
    tile_rows = right_bases.shape[3]
    probe_count = operand.shape[1]
    tile_count = lax.axis_size("tile")
    right_flat = right_bases.reshape(tile_slots * rank_part, tile_rows)
    left_flat = left_bases.reshape(tile_slots * rank_part, tile_rows)
    dense_flat = near_tiles.reshape(tile_rows, -1)
    values = jnp.dot(
        right_flat,
        lax.all_gather(operand, "list", axis=0, tiled=True),
        preferred_element_type=F32,
    )
    rank_level = lax.axis_index("list") * rank_part + lax.iota(jnp.int32, rank_part)
    rank_mask = rank_level[None, :] < tile_ranks[0][:, None]
    coefficients = jnp.where(
        rank_mask[:, :, None], values.reshape(tile_slots, rank_part, probe_count), 0.0
    ).astype(BF)
    targets = (column_rows[0][None, :] == lax.iota(jnp.int32, tile_count)[:, None]).astype(BF)
    outgoing = jnp.einsum(
        "dk,krp->drp", targets, coefficients, preferred_element_type=F32
    ).astype(BF)
    sources = (row_columns[0][:, None] == lax.iota(jnp.int32, tile_count)[None, :]).astype(BF)
    chosen = jnp.einsum(
        "kj,jrp->krp",
        sources,
        lax.all_to_all(outgoing, "tile", split_axis=0, concat_axis=0, tiled=True),
        preferred_element_type=F32,
    ).astype(BF)
    chosen = chosen.reshape(tile_slots * rank_part, -1)
    far_sum = lax.dot_general(
        left_flat, chosen, (((0,), (0,)), ((), ())), preferred_element_type=F32
    )
    arrived = {}
    for offset in (1, -1):
        arrived[offset] = shifted(operand, "tile", offset)
    stacked = jnp.concatenate([arrived[1], operand, arrived[-1]], axis=0)
    near_sum = jnp.dot(dense_flat, stacked, preferred_element_type=F32)
    partial_image = near_sum + far_sum
    return lax.psum_scatter(partial_image, "list", scatter_dimension=0, tiled=True)


def many_slots(probes, right_bases, left_bases, near_tiles, tile_ranks, column_rows, row_columns):
    rest = (right_bases, left_bases, near_tiles, tile_ranks, column_rows, row_columns)
    first_pass = image_part(probes.astype(BF), *rest).astype(BF)
    return image_part(first_pass, *rest)


VMEM = pl.BlockSpec(memory_space=pltpu.VMEM)


def kernel_call(kernel, outs, operands, flops=0):
    return pl.pallas_call(
        kernel,
        out_shape=tuple(jax.ShapeDtypeStruct(shape, kind) for shape, kind in outs),
        in_specs=[VMEM] * len(operands),
        out_specs=tuple(VMEM for _ in outs),
        compiler_params=pltpu.CompilerParams(vmem_limit_bytes=40 * 2**20),
        cost_estimate=pl.CostEstimate(
            flops=flops, bytes_accessed=2 * operands[0].size, transcendentals=0
        ),
    )(*operands)


def prepare_kernel(probes_ref, right_ref, left_ref, block_ref, parts_ref, padded_ref):
    ranks = right_ref.shape[0]
    rows = probes_ref.shape[0]
    block_ref[...] = probes_ref[...].astype(BF)
    parts_ref[...] = jnp.zeros_like(parts_ref)
    padded_ref[...] = jnp.zeros_like(padded_ref)
    padded_ref[:ranks, :] = left_ref[...]
    for part in range(parts_ref.shape[0]):
        parts_ref[part, :ranks, :] = right_ref[:, part * rows : (part + 1) * rows]


def kept_levels(group, rank_part, ranks_ref, shape):
    slot = lax.broadcasted_iota(jnp.int32, shape, 0)
    return (group * rank_part + slot < ranks_ref[...]) & (slot < rank_part)


def coefficient_kernel(rank_part, parts_ref, own_ref, across_ref, pair_ref, ranks_ref, out_ref):
    me = lax.axis_index("list")
    blocks = (own_ref[...], pair_ref[0], across_ref[...], pair_ref[1])
    total = jnp.zeros(out_ref.shape, F32)
    for turn, block in enumerate(blocks):
        total += jnp.dot(parts_ref[me ^ turn], block, preferred_element_type=F32)
    keep = kept_levels(me, rank_part, ranks_ref, out_ref.shape)
    out_ref[...] = jnp.where(keep, total, 0.0).astype(out_ref.dtype)


def partner(tile, turn, count):
    if turn == 2:
        return lax.rem(tile + count + 2 * lax.rem(tile, 2) - 1, count)
    return tile ^ (turn if turn < 2 else 2)


def tile_swap(block, turn):
    count = lax.axis_size("tile")
    if turn == 2:
        route = [(i, (i + count + 2 * (i % 2) - 1) % count) for i in range(count)]
    else:
        route = [(i, i ^ (1 if turn == 1 else 2)) for i in range(count)]
    return lax.ppermute(block, "tile", route)


def list_swap(block, bit):
    return lax.ppermute(block, "list", [(i, i ^ bit) for i in range(lax.axis_size("list"))])


def across(block):
    cut = block.shape[0] // 2
    return jnp.concatenate([list_swap(block[:cut], 2), list_swap(block[cut:], 2)])


def far_and_near(rows, columns_ref, block_refs, coefficient_refs):
    count = lax.axis_size("tile")
    tile = lax.axis_index("tile")
    chosen = coefficient_refs[0][...]
    for turn in (1, 2, 3):
        listed = columns_ref[...] == partner(tile, turn, count)
        chosen = jnp.where(listed, coefficient_refs[turn][...], chosen)
    odd = lax.rem(tile, 2)
    inside = (tile > 0) & (tile < count - 1)
    blocks = [
        (1, block_refs[0][:rows, :]),
        (2 - 2 * odd, block_refs[1][:rows, :]),
        (2 * odd, jnp.where(inside, block_refs[2][:rows, :], 0)),
    ]
    return chosen, blocks


def row_part(near_ref, left_ref, blocks, coefficients, part):
    rows = near_ref.shape[2]
    cut = pl.ds(pl.multiple_of(part * rows, rows), rows)
    total = lax.dot_general(
        left_ref[:, cut], coefficients, (((0,), (0,)), ((), ())), preferred_element_type=F32
    )
    for side, block in blocks:
        total += jnp.dot(near_ref[side, cut, :], block, preferred_element_type=F32)
    return total


def first_kernel(rank_part, near_ref, left_ref, columns_ref, ranks_ref, *refs):
    right_refs, block_refs, coefficient_refs = refs[:3], refs[3:6], refs[6:10]
    keep_ref, send_ref = refs[10:]
    rows = near_ref.shape[2]
    me = lax.axis_index("list")
    right = (right_refs[0], right_refs[2].at[0], right_refs[1], right_refs[2].at[1])
    coefficients, blocks = far_and_near(rows, columns_ref, block_refs, coefficient_refs)
    shape = coefficients.shape
    sums = [jnp.zeros(shape, F32)] * 4
    for turn in (1, 3, 0, 2):
        part = me ^ turn
        total = row_part(near_ref, left_ref, blocks, coefficients, part)
        out_ref = send_ref if turn % 2 else keep_ref
        out_ref[turn // 2, :rows, :] = total.astype(out_ref.dtype)
        rounded = total.astype(BF)
        for group in range(4):
            sums[group] += jnp.dot(right[group][part], rounded, preferred_element_type=F32)
    for turn in range(4):
        keep = kept_levels(me ^ turn, rank_part, ranks_ref, shape)
        out_ref = send_ref if turn % 2 else keep_ref
        out_ref[turn // 2, rows:, :] = jnp.where(keep, sums[turn], 0.0).astype(out_ref.dtype)


def second_kernel(near_ref, left_ref, columns_ref, *refs):
    block_refs, coefficient_refs, (keep_ref, send_ref) = refs[:3], refs[3:7], refs[7:]
    rows = near_ref.shape[2]
    me = lax.axis_index("list")
    coefficients, blocks = far_and_near(rows, columns_ref, block_refs, coefficient_refs)
    for turn in (1, 3, 0, 2):
        out_ref = send_ref if turn % 2 else keep_ref
        total = row_part(near_ref, left_ref, blocks, coefficients, me ^ turn)
        out_ref[turn // 2] = total.astype(out_ref.dtype)


def list_sum(keep, send):
    pair = keep + list_swap(send, 1)
    return pair[0] + across(pair[1].astype(BF))


def one_slot(probes, right_bases, left_bases, near_tiles, tile_ranks, column_rows, row_columns):
    rank_part, tile_rows = right_bases.shape[2:]
    rows, probe_count = probes.shape
    slots = -(-rank_part // 16) * 16
    near = near_tiles[0].transpose(1, 0, 2)
    flops = 2 * near.size * probe_count
    block, right, left = kernel_call(
        prepare_kernel,
        [
            ((rows, probe_count), BF),
            ((tile_rows // rows, slots, rows), BF),
            ((slots, tile_rows), BF),
        ],
        (probes, right_bases[0, 0], left_bases[0, 0]),
    )
    block_across = across(block)
    right_across = list_swap(right, 2)
    beside = [block, tile_swap(block, 1), tile_swap(block, 2)]
    block_pair = list_swap(jnp.stack([block, block_across]), 1)
    (own,) = kernel_call(
        functools.partial(coefficient_kernel, rank_part),
        [((slots, probe_count), BF)],
        (right, block, block_across, block_pair, tile_ranks),
    )
    coefficients = [own] + [tile_swap(own, turn) for turn in (1, 2, 3)]
    right_pair = list_swap(jnp.stack([right, right_across]), 1)
    shape = (2, rows + slots, probe_count)
    keep, send = kernel_call(
        functools.partial(first_kernel, rank_part),
        [(shape, F32), (shape, F32)],
        (
            near,
            left,
            row_columns,
            tile_ranks,
            right,
            right_across,
            right_pair,
            *beside,
            *coefficients,
        ),
        flops,
    )
    both = list_sum(keep, send).astype(BF)
    beside = [both, tile_swap(both, 1), tile_swap(both, 2)]
    coefficients = [message[rows:] for message in beside] + [tile_swap(both[rows:], 3)]
    shape = (2, rows, probe_count)
    keep, send = kernel_call(
        second_kernel,
        [(shape, F32), (shape, F32)],
        (near, left, row_columns, *beside, *coefficients),
        flops,
    )
    return list_sum(keep, send)


def local(probes, right_bases, left_bases, near_tiles, tile_ranks, column_rows, row_columns):
    few = lax.axis_size("tile") == 4 and lax.axis_size("list") == 4
    small = right_bases.shape[1] == 1 and few
    form = one_slot if small else many_slots
    return form(
        probes, right_bases, left_bases, near_tiles, tile_ranks, column_rows, row_columns
    )


def solution(mesh):
    placed = (
        P(("group", "tile", "list"), None),
        P(("group", "tile"), None, "list", None),
        P(("group", "tile"), None, "list", None),
        P(("group", "tile"), None, None, "list"),
        P(("group", "tile"), None),
        P("tile", None),
        P("tile", None),
    )
    return jax.shard_map(
        local,
        mesh=mesh,
        in_specs=placed,
        out_specs=P(("group", "tile", "list"), None),
        check_vma=False,
    )
```

```python
import functools

import jax
import jax.numpy as jnp
from jax import lax
from jax.experimental import pallas as pl
from jax.experimental.pallas import tpu as pltpu
from jax.sharding import PartitionSpec as P

BF = jnp.bfloat16
F32 = jnp.float32


def shifted(block, axis, distance):
    devices = range(lax.axis_size(axis))
    route = [(i - distance, i) for i in devices if i - distance in devices]
    return lax.ppermute(block, axis, route)


def image_part(operand, right_bases, left_bases, near_tiles, tile_ranks, column_rows, row_columns):
    tile_slots = right_bases.shape[1]
    rank_part = right_bases.shape[2]
    tile_rows = right_bases.shape[3]
    probe_count = operand.shape[1]
    tile_count = lax.axis_size("tile")
    right_flat = right_bases.reshape(tile_slots * rank_part, tile_rows)
    left_flat = left_bases.reshape(tile_slots * rank_part, tile_rows)
    dense_flat = near_tiles.reshape(tile_rows, -1)
    values = jnp.dot(
        right_flat,
        lax.all_gather(operand, "list", axis=0, tiled=True),
        preferred_element_type=F32,
    )
    rank_level = lax.axis_index("list") * rank_part + lax.iota(jnp.int32, rank_part)
    rank_mask = rank_level[None, :] < tile_ranks[0][:, None]
    coefficients = jnp.where(
        rank_mask[:, :, None], values.reshape(tile_slots, rank_part, probe_count), 0.0
    ).astype(BF)
    targets = (column_rows[0][None, :] == lax.iota(jnp.int32, tile_count)[:, None]).astype(BF)
    outgoing = jnp.einsum(
        "dk,krp->drp", targets, coefficients, preferred_element_type=F32
    ).astype(BF)
    sources = (row_columns[0][:, None] == lax.iota(jnp.int32, tile_count)[None, :]).astype(BF)
    chosen = jnp.einsum(
        "kj,jrp->krp",
        sources,
        lax.all_to_all(outgoing, "tile", split_axis=0, concat_axis=0, tiled=True),
        preferred_element_type=F32,
    ).astype(BF)
    chosen = chosen.reshape(tile_slots * rank_part, -1)
    far_sum = lax.dot_general(
        left_flat, chosen, (((0,), (0,)), ((), ())), preferred_element_type=F32
    )
    arrived = {}
    for offset in (1, -1):
        arrived[offset] = shifted(operand, "tile", offset)
    stacked = jnp.concatenate([arrived[1], operand, arrived[-1]], axis=0)
    near_sum = jnp.dot(dense_flat, stacked, preferred_element_type=F32)
    partial_image = near_sum + far_sum
    return lax.psum_scatter(partial_image, "list", scatter_dimension=0, tiled=True)


def many_slots(probes, right_bases, left_bases, near_tiles, tile_ranks, column_rows, row_columns):
    rest = (right_bases, left_bases, near_tiles, tile_ranks, column_rows, row_columns)
    first_pass = image_part(probes.astype(BF), *rest).astype(BF)
    return image_part(first_pass, *rest)


VMEM = pl.BlockSpec(memory_space=pltpu.VMEM)


def kernel_call(kernel, outs, operands, flops=0):
    return pl.pallas_call(
        kernel,
        out_shape=tuple(jax.ShapeDtypeStruct(shape, kind) for shape, kind in outs),
        in_specs=[VMEM] * len(operands),
        out_specs=tuple(VMEM for _ in outs),
        compiler_params=pltpu.CompilerParams(vmem_limit_bytes=40 * 2**20),
        cost_estimate=pl.CostEstimate(
            flops=flops, bytes_accessed=2 * operands[0].size, transcendentals=0
        ),
    )(*operands)


def bases_kernel(right_ref, left_ref, parts_ref, padded_ref):
    ranks = right_ref.shape[0]
    rows = parts_ref.shape[2]
    parts_ref[...] = jnp.zeros_like(parts_ref)
    padded_ref[...] = jnp.zeros_like(padded_ref)
    padded_ref[:ranks, :] = left_ref[...]
    for part in range(parts_ref.shape[0]):
        parts_ref[part, :ranks, :] = right_ref[:, part * rows : (part + 1) * rows]


def kept_levels(group, rank_part, ranks_ref, shape):
    slot = lax.broadcasted_iota(jnp.int32, shape, 0)
    return (group * rank_part + slot < ranks_ref[...]) & (slot < rank_part)


def coefficient_kernel(rank_part, parts_ref, own_ref, across_ref, pair_ref, ranks_ref, out_ref):
    me = lax.axis_index("list")
    blocks = (own_ref[...], pair_ref[0], across_ref[...], pair_ref[1])
    total = jnp.zeros(out_ref.shape, F32)
    for turn, block in enumerate(blocks):
        total += jnp.dot(parts_ref[me ^ turn], block, preferred_element_type=F32)
    keep = kept_levels(me, rank_part, ranks_ref, out_ref.shape)
    out_ref[...] = jnp.where(keep, total, 0.0).astype(out_ref.dtype)


def tile_swap(block, turn):
    count = lax.axis_size("tile")
    route = [(i, i ^ turn) for i in range(count)]
    if turn == 0:
        route = [(i, min(max(i - 1 + 2 * (i % 2), 0), count - 1)) for i in range(count)]
    return lax.ppermute(block, "tile", route)


def list_swap(block, bit):
    return lax.ppermute(block, "list", [(i, i ^ bit) for i in range(lax.axis_size("list"))])


def far_and_near(rows, columns_ref, block_refs, coefficient_refs):
    count = lax.axis_size("tile")
    tile = lax.axis_index("tile")
    chosen = coefficient_refs[0][...]
    for turn in (1, 2, 3):
        listed = columns_ref[...] == tile ^ turn
        chosen = jnp.where(listed, coefficient_refs[turn][...], chosen)
    odd = lax.rem(tile, 2)
    inside = (tile > 0) & (tile < count - 1)
    blocks = [
        (1, block_refs[0][:rows, :]),
        (2 - 2 * odd, block_refs[1][:rows, :]),
        (2 * odd, jnp.where(inside, block_refs[2][:rows, :], 0)),
    ]
    return chosen, blocks


def row_part(near_ref, left_ref, blocks, coefficients, part):
    rows = near_ref.shape[2]
    cut = pl.ds(pl.multiple_of(part * rows, rows), rows)
    total = lax.dot_general(
        left_ref[:, cut], coefficients, (((0,), (0,)), ((), ())), preferred_element_type=F32
    )
    for side, block in blocks:
        total += jnp.dot(near_ref[side, cut, :], block, preferred_element_type=F32)
    return total


def first_kernel(rank_part, near_ref, left_ref, columns_ref, ranks_ref, *refs):
    right_refs, block_refs, coefficient_refs = refs[:3], refs[3:6], refs[6:10]
    keep_ref, send_ref = refs[10:]
    rows = near_ref.shape[2]
    me = lax.axis_index("list")
    right = (right_refs[0], right_refs[2].at[0], right_refs[1], right_refs[2].at[1])
    coefficients, blocks = far_and_near(rows, columns_ref, block_refs, coefficient_refs)
    shape = coefficients.shape
    sums = jnp.zeros((4 * shape[0], shape[1]), F32)
    for turn in (1, 3, 0, 2):
        part = me ^ turn
        total = row_part(near_ref, left_ref, blocks, coefficients, part)
        out_ref = send_ref if turn % 2 else keep_ref
        out_ref[turn // 2, :rows, :] = total.astype(out_ref.dtype)
        rounded = total.astype(BF)
        stacked = jnp.concatenate([group_ref[part] for group_ref in right])
        sums += jnp.dot(stacked, rounded, preferred_element_type=F32)
    for turn in range(4):
        keep = kept_levels(me ^ turn, rank_part, ranks_ref, shape)
        out_ref = send_ref if turn % 2 else keep_ref
        group_sum = sums[turn * shape[0] : (turn + 1) * shape[0]]
        out_ref[turn // 2, rows:, :] = jnp.where(keep, group_sum, 0.0).astype(out_ref.dtype)


def second_kernel(near_ref, left_ref, columns_ref, *refs):
    block_refs, coefficient_refs, (keep_ref, send_ref) = refs[:3], refs[3:7], refs[7:]
    rows = near_ref.shape[2]
    me = lax.axis_index("list")
    coefficients, blocks = far_and_near(rows, columns_ref, block_refs, coefficient_refs)
    for turn in (1, 3, 0, 2):
        out_ref = send_ref if turn % 2 else keep_ref
        total = row_part(near_ref, left_ref, blocks, coefficients, me ^ turn)
        out_ref[turn // 2] = total.astype(out_ref.dtype)


def list_sum(keep, send):
    pair = keep + list_swap(send, 1)
    return pair[0] + list_swap(pair[1].astype(BF), 2)


def one_slot(probes, right_bases, left_bases, near_tiles, tile_ranks, column_rows, row_columns):
    rank_part, tile_rows = right_bases.shape[2:]
    rows, probe_count = probes.shape
    slots = -(-rank_part // 16) * 16
    near = near_tiles[0].transpose(1, 0, 2)
    flops = 2 * near.size * probe_count
    right, left = kernel_call(
        bases_kernel,
        [((tile_rows // rows, slots, rows), BF), ((slots, tile_rows), BF)],
        (right_bases[0, 0], left_bases[0, 0]),
    )
    block = probes.astype(BF)
    block_across = list_swap(block, 2)
    beside = [block, tile_swap(block, 1), tile_swap(block, 0)]
    block_across, beside[1] = lax.optimization_barrier((block_across, beside[1]))
    block_pair = list_swap(jnp.stack([block, block_across]), 1)
    (own,) = kernel_call(
        functools.partial(coefficient_kernel, rank_part),
        [((slots, probe_count), BF)],
        (right, block, block_across, block_pair, tile_ranks),
    )
    coefficients = [own] + [tile_swap(own, turn) for turn in (1, 2, 3)]
    right, _ = lax.optimization_barrier((right, block_across))
    right_across = list_swap(right, 2)
    right_pair = list_swap(jnp.stack([right, right_across]), 1)
    shape = (2, rows + slots, probe_count)
    keep, send = kernel_call(
        functools.partial(first_kernel, rank_part),
        [(shape, F32), (shape, F32)],
        (
            near,
            left,
            row_columns,
            tile_ranks,
            right,
            right_across,
            right_pair,
            *beside,
            *coefficients,
        ),
        flops,
    )
    both = list_sum(keep, send).astype(BF)
    beside = [both, tile_swap(both, 1), tile_swap(both[:rows], 0)]
    coefficients = [message[rows:] for message in beside[:2]]
    coefficients += [tile_swap(both[rows:], turn) for turn in (2, 3)]
    shape = (2, rows, probe_count)
    keep, send = kernel_call(
        second_kernel,
        [(shape, F32), (shape, F32)],
        (near, left, row_columns, *beside, *coefficients),
        flops,
    )
    return list_sum(keep, send)


def local(probes, right_bases, left_bases, near_tiles, tile_ranks, column_rows, row_columns):
    few = lax.axis_size("tile") == 4 and lax.axis_size("list") == 4
    small = right_bases.shape[1] == 1 and few
    form = one_slot if small else many_slots
    return form(
        probes, right_bases, left_bases, near_tiles, tile_ranks, column_rows, row_columns
    )


def solution(mesh):
    placed = (
        P(("group", "tile", "list"), None),
        P(("group", "tile"), None, "list", None),
        P(("group", "tile"), None, "list", None),
        P(("group", "tile"), None, None, "list"),
        P(("group", "tile"), None),
        P("tile", None),
        P("tile", None),
    )
    return jax.shard_map(
        local,
        mesh=mesh,
        in_specs=placed,
        out_specs=P(("group", "tile", "list"), None),
        check_vma=False,
    )
```

```python
import functools

import jax
import jax.numpy as jnp
from jax import lax
from jax.experimental import pallas as pl
from jax.experimental.pallas import tpu as pltpu
from jax.sharding import PartitionSpec as P

BF = jnp.bfloat16
F32 = jnp.float32


def shifted(block, axis, distance):
    devices = range(lax.axis_size(axis))
    route = [(i - distance, i) for i in devices if i - distance in devices]
    return lax.ppermute(block, axis, route)


def image_part(operand, right_bases, left_bases, near_tiles, tile_ranks, column_rows, row_columns):
    tile_slots = right_bases.shape[1]
    rank_part = right_bases.shape[2]
    tile_rows = right_bases.shape[3]
    probe_count = operand.shape[1]
    tile_count = lax.axis_size("tile")
    right_flat = right_bases.reshape(tile_slots * rank_part, tile_rows)
    left_flat = left_bases.reshape(tile_slots * rank_part, tile_rows)
    dense_flat = near_tiles.reshape(tile_rows, -1)
    values = jnp.dot(
        right_flat,
        lax.all_gather(operand, "list", axis=0, tiled=True),
        preferred_element_type=F32,
    )
    rank_level = lax.axis_index("list") * rank_part + lax.iota(jnp.int32, rank_part)
    rank_mask = rank_level[None, :] < tile_ranks[0][:, None]
    coefficients = jnp.where(
        rank_mask[:, :, None], values.reshape(tile_slots, rank_part, probe_count), 0.0
    ).astype(BF)
    targets = (column_rows[0][None, :] == lax.iota(jnp.int32, tile_count)[:, None]).astype(BF)
    outgoing = jnp.einsum(
        "dk,krp->drp", targets, coefficients, preferred_element_type=F32
    ).astype(BF)
    sources = (row_columns[0][:, None] == lax.iota(jnp.int32, tile_count)[None, :]).astype(BF)
    chosen = jnp.einsum(
        "kj,jrp->krp",
        sources,
        lax.all_to_all(outgoing, "tile", split_axis=0, concat_axis=0, tiled=True),
        preferred_element_type=F32,
    ).astype(BF)
    chosen = chosen.reshape(tile_slots * rank_part, -1)
    far_sum = lax.dot_general(
        left_flat, chosen, (((0,), (0,)), ((), ())), preferred_element_type=F32
    )
    arrived = {}
    for offset in (1, -1):
        arrived[offset] = shifted(operand, "tile", offset)
    stacked = jnp.concatenate([arrived[1], operand, arrived[-1]], axis=0)
    near_sum = jnp.dot(dense_flat, stacked, preferred_element_type=F32)
    partial_image = near_sum + far_sum
    return lax.psum_scatter(partial_image, "list", scatter_dimension=0, tiled=True)


def many_slots(probes, right_bases, left_bases, near_tiles, tile_ranks, column_rows, row_columns):
    rest = (right_bases, left_bases, near_tiles, tile_ranks, column_rows, row_columns)
    first_pass = image_part(probes.astype(BF), *rest).astype(BF)
    return image_part(first_pass, *rest)


VMEM = pl.BlockSpec(memory_space=pltpu.VMEM)


def kernel_call(kernel, outs, operands, flops=0):
    return pl.pallas_call(
        kernel,
        out_shape=tuple(jax.ShapeDtypeStruct(shape, kind) for shape, kind in outs),
        in_specs=[VMEM] * len(operands),
        out_specs=tuple(VMEM for _ in outs),
        compiler_params=pltpu.CompilerParams(vmem_limit_bytes=16 * 2**20),
        cost_estimate=pl.CostEstimate(
            flops=flops, bytes_accessed=2 * operands[0].size, transcendentals=0
        ),
    )(*operands)


def coefficient_sums(right_parts, operands, group_rows, rank_part, ranks_ref, keep_ref, send_ref):
    me = lax.axis_index("list")
    total = jnp.zeros((4 * group_rows, operands[0].shape[1]), F32)
    for right, operand in zip(right_parts, operands):
        total += jnp.dot(right, operand, preferred_element_type=F32)
    slot = lax.broadcasted_iota(jnp.int32, (group_rows, total.shape[1]), 0)
    for turn in range(4):
        level = (me ^ turn) * rank_part + slot
        keep = (level < ranks_ref[...]) & (slot < rank_part)
        out_ref = send_ref if turn % 2 else keep_ref
        out_ref[turn // 2] = jnp.where(
            keep, total[turn * group_rows : (turn + 1) * group_rows], 0.0
        )


def coefficient_kernel(even_ref, odd_ref, block_ref, ranks_ref, parts_ref, keep_ref, send_ref):
    me = lax.axis_index("list")
    ranks = even_ref.shape[1]
    rows = block_ref.shape[0]
    slots = keep_ref.shape[1]
    parts_ref[...] = jnp.zeros_like(parts_ref)
    groups = (even_ref.at[0], odd_ref.at[0], even_ref.at[1], odd_ref.at[1])
    for part in range(parts_ref.shape[0]):
        for turn, group_ref in enumerate(groups):
            parts_ref[part, turn * slots : turn * slots + ranks, :] = group_ref[
                :, part * rows : (part + 1) * rows
            ]
    coefficient_sums(
        [parts_ref[me]], [block_ref[...]], slots, ranks, ranks_ref, keep_ref, send_ref
    )


def tile_swap(block, turn):
    count = lax.axis_size("tile")
    route = [(i, i ^ turn) for i in range(count)]
    if turn == 0:
        route = [(i, min(max(i - 1 + 2 * (i % 2), 0), count - 1)) for i in range(count)]
    return lax.ppermute(block, "tile", route)


def list_swap(block, bit):
    return lax.ppermute(block, "list", [(i, i ^ bit) for i in range(lax.axis_size("list"))])


def far_and_near(columns_ref, block_refs, coefficient_refs):
    count = lax.axis_size("tile")
    tile = lax.axis_index("tile")
    own_ref, second_ref, pair_ref = coefficient_refs
    slots = own_ref.shape[0]
    chosen = own_ref[...]
    others = (pair_ref[:slots, :], second_ref[...], pair_ref[slots:, :])
    for turn, other in enumerate(others):
        chosen = jnp.where(columns_ref[...] == tile ^ (turn + 1), other, chosen)
    odd = lax.rem(tile, 2)
    inside = (tile > 0) & (tile < count - 1)
    blocks = [
        (1, block_refs[0][...]),
        (2 - 2 * odd, block_refs[1][...]),
        (2 * odd, jnp.where(inside, block_refs[2][...], 0)),
    ]
    return chosen, blocks


def row_part(near_ref, left_ref, blocks, coefficients, part):
    rows = near_ref.shape[2]
    cut = pl.ds(pl.multiple_of(part * rows, rows), rows)
    total = lax.dot_general(
        left_ref[:, cut], coefficients, (((0,), (0,)), ((), ())), preferred_element_type=F32
    )
    for side, block in blocks:
        total += jnp.dot(near_ref[side, cut, :], block, preferred_element_type=F32)
    return total


def image_kernel(near_ref, left_ref, columns_ref, *refs):
    block_refs, coefficient_refs, (keep_ref, send_ref) = refs[:3], refs[3:6], refs[6:]
    me = lax.axis_index("list")
    coefficients, blocks = far_and_near(columns_ref, block_refs, coefficient_refs)
    totals = []
    for turn in (1, 3, 0, 2):
        out_ref = send_ref if turn % 2 else keep_ref
        total = row_part(near_ref, left_ref, blocks, coefficients, me ^ turn)
        out_ref[turn // 2] = total
        totals.append((me ^ turn, total.astype(BF)))
    return totals


def first_kernel(rank_part, near_ref, left_ref, columns_ref, ranks_ref, parts_ref, *refs):
    totals = image_kernel(near_ref, left_ref, columns_ref, *refs[:8])
    coefficient_sums(
        [parts_ref[part] for part, _ in totals],
        [total for _, total in totals],
        parts_ref.shape[1] // 4,
        rank_part,
        ranks_ref,
        *refs[8:],
    )


def second_kernel(*refs):
    image_kernel(*refs)


def list_sum(keep, send, kind=F32, after=()):
    pair = keep + list_swap(send, 1)
    pair, *_ = lax.optimization_barrier((pair, *after))
    return pair[0] + list_swap(pair[1].astype(kind), 2)


def one_slot(probes, right_bases, left_bases, near_tiles, tile_ranks, column_rows, row_columns):
    rank_part, tile_rows = right_bases.shape[2:]
    rows, probe_count = probes.shape
    slots = -(-rank_part // 16) * 16
    near = near_tiles[0].transpose(1, 0, 2)
    flops = 2 * near.size * probe_count
    right = right_bases[0, 0]
    right = jnp.stack([right, list_swap(right, 2)])
    right_pair = list_swap(right, 1)
    left = jnp.pad(left_bases[0, 0], ((0, slots - rank_part), (0, 0)))
    block = probes.astype(BF)
    beside = [block, tile_swap(block, 1), tile_swap(block, 0)]
    image_sums = [((2, rows, probe_count), F32)] * 2
    small_sums = [((2, slots, probe_count), F32)] * 2
    parts, keep, send = kernel_call(
        coefficient_kernel,
        [((tile_rows // rows, 4 * slots, rows), BF), *small_sums],
        (right, right_pair, block, tile_ranks),
        8 * flops,
    )
    own = list_sum(keep, send, after=beside).astype(BF)
    second = tile_swap(own, 2)
    coefficients = own, second, tile_swap(jnp.concatenate([own, second]), 1)
    keep, send, small_keep, small_send = kernel_call(
        functools.partial(first_kernel, rank_part),
        image_sums + small_sums,
        (near, left, row_columns, tile_ranks, parts, *beside, *coefficients),
        flops,
    )
    own = list_sum(small_keep, small_send).astype(BF)
    second = tile_swap(own, 2)
    block = list_sum(keep, send, BF).astype(BF)
    message = tile_swap(jnp.concatenate([block, own, second]), 1)
    beside = [block, message[:rows], tile_swap(block, 0)]
    coefficients = own, second, message[rows:]
    keep, send = kernel_call(
        second_kernel,
        image_sums,
        (near, left, row_columns, *beside, *coefficients),
        flops,
    )
    return list_sum(keep, send, BF)


def local(probes, right_bases, left_bases, near_tiles, tile_ranks, column_rows, row_columns):
    few = lax.axis_size("tile") == 4 and lax.axis_size("list") == 4
    small = right_bases.shape[1] == 1 and few
    form = one_slot if small else many_slots
    return form(
        probes, right_bases, left_bases, near_tiles, tile_ranks, column_rows, row_columns
    )


def solution(mesh):
    placed = (
        P(("group", "tile", "list"), None),
        P(("group", "tile"), None, "list", None),
        P(("group", "tile"), None, "list", None),
        P(("group", "tile"), None, None, "list"),
        P(("group", "tile"), None),
        P("tile", None),
        P("tile", None),
    )
    return jax.shard_map(
        local,
        mesh=mesh,
        in_specs=placed,
        out_specs=P(("group", "tile", "list"), None),
        check_vma=False,
    )
```

```python
import functools

import jax
import jax.numpy as jnp
from jax import lax
from jax.experimental import pallas as pl
from jax.experimental.pallas import tpu as pltpu
from jax.sharding import PartitionSpec as P

BF = jnp.bfloat16
F32 = jnp.float32


def shifted(block, axis, distance):
    devices = range(lax.axis_size(axis))
    route = [(i - distance, i) for i in devices if i - distance in devices]
    return lax.ppermute(block, axis, route)


def image_part(operand, right_bases, left_bases, near_tiles, tile_ranks, column_rows, row_columns):
    tile_slots = right_bases.shape[1]
    rank_part = right_bases.shape[2]
    tile_rows = right_bases.shape[3]
    probe_count = operand.shape[1]
    tile_count = lax.axis_size("tile")
    right_flat = right_bases.reshape(tile_slots * rank_part, tile_rows)
    left_flat = left_bases.reshape(tile_slots * rank_part, tile_rows)
    dense_flat = near_tiles.reshape(tile_rows, -1)
    values = jnp.dot(
        right_flat,
        lax.all_gather(operand, "list", axis=0, tiled=True),
        preferred_element_type=F32,
    )
    rank_level = lax.axis_index("list") * rank_part + lax.iota(jnp.int32, rank_part)
    rank_mask = rank_level[None, :] < tile_ranks[0][:, None]
    coefficients = jnp.where(
        rank_mask[:, :, None], values.reshape(tile_slots, rank_part, probe_count), 0.0
    ).astype(BF)
    targets = (column_rows[0][None, :] == lax.iota(jnp.int32, tile_count)[:, None]).astype(BF)
    outgoing = jnp.einsum(
        "dk,krp->drp", targets, coefficients, preferred_element_type=F32
    ).astype(BF)
    sources = (row_columns[0][:, None] == lax.iota(jnp.int32, tile_count)[None, :]).astype(BF)
    chosen = jnp.einsum(
        "kj,jrp->krp",
        sources,
        lax.all_to_all(outgoing, "tile", split_axis=0, concat_axis=0, tiled=True),
        preferred_element_type=F32,
    ).astype(BF)
    chosen = chosen.reshape(tile_slots * rank_part, -1)
    far_sum = lax.dot_general(
        left_flat, chosen, (((0,), (0,)), ((), ())), preferred_element_type=F32
    )
    arrived = {}
    for offset in (1, -1):
        arrived[offset] = shifted(operand, "tile", offset)
    stacked = jnp.concatenate([arrived[1], operand, arrived[-1]], axis=0)
    near_sum = jnp.dot(dense_flat, stacked, preferred_element_type=F32)
    partial_image = near_sum + far_sum
    return lax.psum_scatter(partial_image, "list", scatter_dimension=0, tiled=True)


def many_slots(probes, right_bases, left_bases, near_tiles, tile_ranks, column_rows, row_columns):
    rest = (right_bases, left_bases, near_tiles, tile_ranks, column_rows, row_columns)
    first_pass = image_part(probes.astype(BF), *rest).astype(BF)
    return image_part(first_pass, *rest)


VMEM = pl.BlockSpec(memory_space=pltpu.VMEM)


def kernel_call(kernel, outs, operands, flops=0):
    return pl.pallas_call(
        kernel,
        out_shape=tuple(jax.ShapeDtypeStruct(shape, kind) for shape, kind in outs),
        in_specs=[VMEM] * len(operands),
        out_specs=tuple(VMEM for _ in outs),
        compiler_params=pltpu.CompilerParams(vmem_limit_bytes=16 * 2**20),
        cost_estimate=pl.CostEstimate(
            flops=flops, bytes_accessed=2 * operands[0].size, transcendentals=0
        ),
    )(*operands)


def stacked(pieces):
    return jnp.concatenate([piece.astype(F32) for piece in pieces]).astype(BF)


def under_rank(values, group, rank_part, ranks_ref):
    level = group * rank_part + lax.broadcasted_iota(jnp.int32, values.shape, 0)
    return jnp.where(level < ranks_ref[...], values, 0.0)


def coefficient_kernel(own_ref, across_ref, block_ref, other_ref, ranks_ref, out_ref):
    me = lax.axis_index("list")
    ranks = own_ref.shape[0]
    rows = block_ref.shape[0]
    total = 0.0
    for part, operand_ref in ((me, block_ref), (me ^ 1, other_ref)):
        cut = pl.ds(pl.multiple_of(part * rows, rows), rows)
        bases = stacked([own_ref[:, cut], across_ref[:, cut]])
        total += jnp.dot(bases, operand_ref[...], preferred_element_type=F32)
    halves = [
        under_rank(total[index * ranks : (index + 1) * ranks], group, ranks, ranks_ref)
        for index, group in enumerate((me, me ^ 2))
    ]
    out_ref[...] = jnp.concatenate(halves).astype(out_ref.dtype)


def tile_swap(block, turn):
    count = lax.axis_size("tile")
    route = [(i, i ^ turn) for i in range(count)]
    if turn == 0:
        route = [(i, min(max(i - 1 + 2 * (i % 2), 0), count - 1)) for i in range(count)]
    return lax.ppermute(block, "tile", route)


def list_swap(block, bit):
    return lax.ppermute(block, "list", [(i, i ^ bit) for i in range(lax.axis_size("list"))])


def image_kernel(near_ref, left_ref, across_ref, columns_ref, *refs):
    block_refs, coefficient_refs, (keep_ref, send_ref) = refs[:3], refs[3:7], refs[7:]
    count = lax.axis_size("tile")
    tile = lax.axis_index("tile")
    me = lax.axis_index("list")
    rows = near_ref.shape[2]
    chosen = coefficient_refs[0][...]
    for turn in (1, 2, 3):
        listed = columns_ref[...] == tile ^ turn
        chosen = jnp.where(listed, coefficient_refs[turn][...], chosen)
    odd = lax.rem(tile, 2)
    inside = (tile > 0) & (tile < count - 1)
    blocks = [
        (1, block_refs[0][...]),
        (2 - 2 * odd, block_refs[1][...]),
        (2 * odd, jnp.where(inside, block_refs[2][...], 0)),
    ]
    totals = []
    for turn in (1, 3, 0, 2):
        part = me ^ turn
        cut = pl.ds(pl.multiple_of(part * rows, rows), rows)
        left = stacked([left_ref[:, cut], across_ref[:, cut]])
        total = lax.dot_general(
            left, chosen, (((0,), (0,)), ((), ())), preferred_element_type=F32
        )
        for side, block in blocks:
            total += jnp.dot(near_ref[side, cut, :], block, preferred_element_type=F32)
        out_ref = send_ref if turn % 2 else keep_ref
        out_ref[turn // 2, :rows, :] = total
        totals.append((cut, total.astype(BF)))
    return totals


def first_kernel(near_ref, left_ref, across_ref, columns_ref, ranks_ref, even_ref, odd_ref, *refs):
    totals = image_kernel(near_ref, left_ref, across_ref, columns_ref, *refs)
    keep_ref, send_ref = refs[7:]
    me = lax.axis_index("list")
    ranks = even_ref.shape[1]
    rows = near_ref.shape[2]
    sums = 0.0
    for cut, total in totals:
        bases = stacked([ref[index, :, cut] for ref in (even_ref, odd_ref) for index in range(2)])
        sums += jnp.dot(bases, total, preferred_element_type=F32)
    for index, turn in enumerate((0, 2, 1, 3)):
        values = sums[index * ranks : (index + 1) * ranks]
        out_ref = send_ref if turn % 2 else keep_ref
        out_ref[turn // 2, rows:, :] = under_rank(values, me ^ turn, ranks, ranks_ref)


def second_kernel(*refs):
    image_kernel(*refs)


def tile_swaps(own):
    return [own] + [tile_swap(own, turn) for turn in (1, 2, 3)]


def one_slot(probes, right_bases, left_bases, near_tiles, tile_ranks, column_rows, row_columns):
    rows, probe_count = probes.shape
    rank_part = right_bases.shape[2]
    near = near_tiles[0].transpose(1, 0, 2)
    flops = 2 * near.size * probe_count
    right, left = right_bases[0, 0], left_bases[0, 0]
    right_across = list_swap(right, 2)
    block = probes.astype(BF)
    beside = [block, tile_swap(block, 1), tile_swap(block, 0)]
    (own,) = kernel_call(
        coefficient_kernel,
        [((2 * rank_part, probe_count), BF)],
        (right, right_across, block, list_swap(block, 1), tile_ranks),
        8 * flops,
    )
    coefficients = tile_swaps(own)
    right = jnp.stack([right, right_across])
    bases = (near, left, list_swap(left, 2), row_columns)
    keep, send = kernel_call(
        first_kernel,
        [((2, rows + rank_part, probe_count), F32)] * 2,
        (*bases, tile_ranks, right, list_swap(right, 1), *beside, *coefficients),
        flops,
    )
    pair = keep + list_swap(send, 1)
    coefficients = tile_swaps(pair[:, rows:].reshape(-1, probe_count).astype(BF))
    block = (pair[0, :rows] + list_swap(pair[1, :rows].astype(BF), 2)).astype(BF)
    block, *coefficients[2:] = lax.optimization_barrier((block, *coefficients[2:]))
    beside = [block, tile_swap(block, 1), tile_swap(block, 0)]
    keep, send = kernel_call(
        second_kernel,
        [((2, rows, probe_count), F32)] * 2,
        (*bases, *beside, *coefficients),
        flops,
    )
    pair = keep + list_swap(send, 1)
    return pair[0] + list_swap(pair[1].astype(BF), 2)


def local(probes, right_bases, left_bases, near_tiles, tile_ranks, column_rows, row_columns):
    few = lax.axis_size("tile") == 4 and lax.axis_size("list") == 4
    small = right_bases.shape[1] == 1 and few
    form = one_slot if small else many_slots
    return form(
        probes, right_bases, left_bases, near_tiles, tile_ranks, column_rows, row_columns
    )


def solution(mesh):
    placed = (
        P(("group", "tile", "list"), None),
        P(("group", "tile"), None, "list", None),
        P(("group", "tile"), None, "list", None),
        P(("group", "tile"), None, None, "list"),
        P(("group", "tile"), None),
        P("tile", None),
        P("tile", None),
    )
    return jax.shard_map(
        local,
        mesh=mesh,
        in_specs=placed,
        out_specs=P(("group", "tile", "list"), None),
        check_vma=False,
    )
```

```python
import functools

import jax
import jax.numpy as jnp
from jax import lax
from jax.experimental import pallas as pl
from jax.experimental.pallas import tpu as pltpu
from jax.sharding import PartitionSpec as P

BF = jnp.bfloat16
F32 = jnp.float32


def shifted(block, axis, distance):
    devices = range(lax.axis_size(axis))
    route = [(i - distance, i) for i in devices if i - distance in devices]
    return lax.ppermute(block, axis, route)


def image_part(operand, right_bases, left_bases, near_tiles, tile_ranks, column_rows, row_columns):
    tile_slots = right_bases.shape[1]
    rank_part = right_bases.shape[2]
    tile_rows = right_bases.shape[3]
    probe_count = operand.shape[1]
    tile_count = lax.axis_size("tile")
    right_flat = right_bases.reshape(tile_slots * rank_part, tile_rows)
    left_flat = left_bases.reshape(tile_slots * rank_part, tile_rows)
    dense_flat = near_tiles.reshape(tile_rows, -1)
    values = jnp.dot(
        right_flat,
        lax.all_gather(operand, "list", axis=0, tiled=True),
        preferred_element_type=F32,
    )
    rank_level = lax.axis_index("list") * rank_part + lax.iota(jnp.int32, rank_part)
    rank_mask = rank_level[None, :] < tile_ranks[0][:, None]
    coefficients = jnp.where(
        rank_mask[:, :, None], values.reshape(tile_slots, rank_part, probe_count), 0.0
    ).astype(BF)
    targets = (column_rows[0][None, :] == lax.iota(jnp.int32, tile_count)[:, None]).astype(BF)
    outgoing = jnp.einsum(
        "dk,krp->drp", targets, coefficients, preferred_element_type=F32
    ).astype(BF)
    sources = (row_columns[0][:, None] == lax.iota(jnp.int32, tile_count)[None, :]).astype(BF)
    chosen = jnp.einsum(
        "kj,jrp->krp",
        sources,
        lax.all_to_all(outgoing, "tile", split_axis=0, concat_axis=0, tiled=True),
        preferred_element_type=F32,
    ).astype(BF)
    chosen = chosen.reshape(tile_slots * rank_part, -1)
    far_sum = lax.dot_general(
        left_flat, chosen, (((0,), (0,)), ((), ())), preferred_element_type=F32
    )
    arrived = {}
    for offset in (1, -1):
        arrived[offset] = shifted(operand, "tile", offset)
    stacked = jnp.concatenate([arrived[1], operand, arrived[-1]], axis=0)
    near_sum = jnp.dot(dense_flat, stacked, preferred_element_type=F32)
    partial_image = near_sum + far_sum
    return lax.psum_scatter(partial_image, "list", scatter_dimension=0, tiled=True)


def many_slots(probes, right_bases, left_bases, near_tiles, tile_ranks, column_rows, row_columns):
    rest = (right_bases, left_bases, near_tiles, tile_ranks, column_rows, row_columns)
    first_pass = image_part(probes.astype(BF), *rest).astype(BF)
    return image_part(first_pass, *rest)


VMEM = pl.BlockSpec(memory_space=pltpu.VMEM)


def kernel_call(kernel, outs, operands, flops=0):
    return pl.pallas_call(
        kernel,
        out_shape=tuple(jax.ShapeDtypeStruct(shape, kind) for shape, kind in outs),
        in_specs=[VMEM] * len(operands),
        out_specs=tuple(VMEM for _ in outs),
        compiler_params=pltpu.CompilerParams(vmem_limit_bytes=16 * 2**20),
        cost_estimate=pl.CostEstimate(
            flops=flops, bytes_accessed=2 * operands[0].size, transcendentals=0
        ),
    )(*operands)


def stacked(pieces):
    return jnp.concatenate([piece.astype(F32) for piece in pieces]).astype(BF)


def under_rank(values, group, rank_part, ranks_ref):
    level = group * rank_part + lax.broadcasted_iota(jnp.int32, values.shape, 0)
    return jnp.where(level < ranks_ref[...], values, 0.0)


def coefficient_kernel(bases_ref, across_ref, block_ref, other_ref, ranks_ref, out_ref):
    me = lax.axis_index("list")
    ranks = bases_ref.shape[1]
    rows = block_ref.shape[0]
    total = 0.0
    for part, operand_ref in ((me, block_ref), (me ^ 1, other_ref)):
        cut = pl.ds(pl.multiple_of(part * rows, rows), rows)
        bases = stacked([bases_ref[0, :, cut], across_ref[0, :, cut]])
        total += jnp.dot(bases, operand_ref[...], preferred_element_type=F32)
    halves = [
        under_rank(total[index * ranks : (index + 1) * ranks], group, ranks, ranks_ref)
        for index, group in enumerate((me, me ^ 2))
    ]
    out_ref[...] = jnp.concatenate(halves).astype(out_ref.dtype)


def tile_swap(block, turn):
    count = lax.axis_size("tile")
    route = [(i, i ^ turn) for i in range(count)]
    if turn == 0:
        route = [(i, min(max(i - 1 + 2 * (i % 2), 0), count - 1)) for i in range(count)]
    return lax.ppermute(block, "tile", route)


def list_swap(block, bit):
    return lax.ppermute(block, "list", [(i, i ^ bit) for i in range(lax.axis_size("list"))])


def image_kernel(turns, near_ref, bases_ref, across_ref, columns_ref, *refs):
    block_refs, coefficient_refs, out_ref = refs[:3], refs[3:7], refs[7]
    count = lax.axis_size("tile")
    tile = lax.axis_index("tile")
    me = lax.axis_index("list")
    rows = near_ref.shape[2]
    chosen = coefficient_refs[0][...]
    for turn in (1, 2, 3):
        listed = columns_ref[...] == tile ^ turn
        chosen = jnp.where(listed, coefficient_refs[turn][...], chosen)
    odd = lax.rem(tile, 2)
    inside = (tile > 0) & (tile < count - 1)
    blocks = [
        (1, block_refs[0][...]),
        (2 - 2 * odd, block_refs[1][...]),
        (2 * odd, jnp.where(inside, block_refs[2][...], 0)),
    ]
    totals = []
    for index, turn in enumerate(turns):
        part = me ^ turn
        cut = pl.ds(pl.multiple_of(part * rows, rows), rows)
        left = stacked([bases_ref[1, :, cut], across_ref[1, :, cut]])
        total = lax.dot_general(
            left, chosen, (((0,), (0,)), ((), ())), preferred_element_type=F32
        )
        for side, block in blocks:
            total += jnp.dot(near_ref[side, cut, :], block, preferred_element_type=F32)
        out_ref[index] = total
        totals.append((cut, total.astype(BF)))
    return totals


def right_products(totals, bases_ref, across_ref, pair_ref):
    sums = 0.0
    for cut, total in totals:
        groups = [bases_ref[0, :, cut], across_ref[0, :, cut], pair_ref[0, :, cut], pair_ref[1, :, cut]]
        sums += jnp.dot(stacked(groups), total, preferred_element_type=F32)
    return sums


def sent_kernel(near_ref, bases_ref, across_ref, columns_ref, *refs):
    operands, pair_ref, out_ref, sums_ref = refs[:7], *refs[7:]
    totals = image_kernel(
        (1, 3), near_ref, bases_ref, across_ref, columns_ref, *operands, out_ref
    )
    sums_ref[...] = right_products(totals, bases_ref, across_ref, pair_ref)


def kept_kernel(near_ref, bases_ref, across_ref, columns_ref, *refs):
    operands, (pair_ref, ranks_ref, sums_ref), outs = refs[:7], refs[7:10], refs[10:]
    totals = image_kernel(
        (0, 2), near_ref, bases_ref, across_ref, columns_ref, *operands, outs[0]
    )
    sums = sums_ref[...] + right_products(totals, bases_ref, across_ref, pair_ref)
    me = lax.axis_index("list")
    ranks = bases_ref.shape[1]
    for index, turn in enumerate((0, 2, 1, 3)):
        values = sums[index * ranks : (index + 1) * ranks]
        start = index % 2 * ranks
        outs[1 + index // 2][start : start + ranks, :] = under_rank(
            values, me ^ turn, ranks, ranks_ref
        )


def second_kernel(turns, *refs):
    image_kernel(turns, *refs)


def one_slot(probes, right_bases, left_bases, near_tiles, tile_ranks, column_rows, row_columns):
    rows, probe_count = probes.shape
    rank_part = right_bases.shape[2]
    near = near_tiles[0].transpose(1, 0, 2)
    flops = 2 * near.size * probe_count
    halves = ((2, rows, probe_count), F32)
    small = ((2 * rank_part, probe_count), F32)

    bases = jnp.stack([right_bases[0, 0], left_bases[0, 0]])
    bases_across = list_swap(bases, 2)
    block = probes.astype(BF)
    beside = [block, tile_swap(block, 1), tile_swap(block, 0)]
    (own,) = kernel_call(
        coefficient_kernel,
        [((2 * rank_part, probe_count), BF)],
        (bases, bases_across, block, list_swap(block, 1), tile_ranks),
        8 * flops,
    )
    coefficients = [own] + [tile_swap(own, turn) for turn in (1, 2, 3)]
    right = jnp.stack([bases[0], bases_across[0]])
    right, _ = lax.optimization_barrier((right, own))
    right_pair = list_swap(right, 1)

    fixed = (near, bases, bases_across, row_columns)
    operands = (*fixed, *beside, *coefficients, right_pair)
    send, sums = kernel_call(
        sent_kernel, [halves, ((4 * rank_part, probe_count), F32)], operands, flops
    )
    arrived = list_swap(send, 1)
    keep, small_keep, small_send = kernel_call(
        kept_kernel, [halves, small, small], (*operands, tile_ranks, sums), flops
    )
    own = (small_keep + list_swap(small_send, 1)).astype(BF)
    pair = keep + arrived
    second, third = tile_swap(own, 2), tile_swap(own, 3)
    block = (pair[0] + list_swap(pair[1].astype(BF), 2)).astype(BF)
    message = jnp.concatenate([block, own])
    message, second, third = lax.optimization_barrier((message, second, third))
    message = tile_swap(message, 1)
    beside = [block, message[:rows], tile_swap(block, 0)]
    coefficients = [own, message[rows:], second, third]

    operands = (*fixed, *beside, *coefficients)
    (send,) = kernel_call(
        functools.partial(second_kernel, (1, 3)), [halves], operands, flops
    )
    arrived = list_swap(send, 1)
    (keep,) = kernel_call(
        functools.partial(second_kernel, (0, 2)), [halves], operands, flops
    )
    pair = keep + arrived
    return pair[0] + list_swap(pair[1].astype(BF), 2)


def local(probes, right_bases, left_bases, near_tiles, tile_ranks, column_rows, row_columns):
    few = lax.axis_size("tile") == 4 and lax.axis_size("list") == 4
    small = right_bases.shape[1] == 1 and few
    form = one_slot if small else many_slots
    return form(
        probes, right_bases, left_bases, near_tiles, tile_ranks, column_rows, row_columns
    )


def solution(mesh):
    placed = (
        P(("group", "tile", "list"), None),
        P(("group", "tile"), None, "list", None),
        P(("group", "tile"), None, "list", None),
        P(("group", "tile"), None, None, "list"),
        P(("group", "tile"), None),
        P("tile", None),
        P("tile", None),
    )
    return jax.shard_map(
        local,
        mesh=mesh,
        in_specs=placed,
        out_specs=P(("group", "tile", "list"), None),
        check_vma=False,
    )
```

```python
import functools

import jax
import jax.numpy as jnp
from jax import lax
from jax.experimental import pallas as pl
from jax.experimental.pallas import tpu as pltpu
from jax.sharding import PartitionSpec as P

BF = jnp.bfloat16
F32 = jnp.float32


def shifted(block, axis, distance):
    devices = range(lax.axis_size(axis))
    route = [(i - distance, i) for i in devices if i - distance in devices]
    return lax.ppermute(block, axis, route)


def image_part(operand, right_bases, left_bases, near_tiles, tile_ranks, column_rows, row_columns):
    tile_slots = right_bases.shape[1]
    rank_part = right_bases.shape[2]
    tile_rows = right_bases.shape[3]
    probe_count = operand.shape[1]
    tile_count = lax.axis_size("tile")
    right_flat = right_bases.reshape(tile_slots * rank_part, tile_rows)
    left_flat = left_bases.reshape(tile_slots * rank_part, tile_rows)
    dense_flat = near_tiles.reshape(tile_rows, -1)
    values = jnp.dot(
        right_flat,
        lax.all_gather(operand, "list", axis=0, tiled=True),
        preferred_element_type=F32,
    )
    rank_level = lax.axis_index("list") * rank_part + lax.iota(jnp.int32, rank_part)
    rank_mask = rank_level[None, :] < tile_ranks[0][:, None]
    coefficients = jnp.where(
        rank_mask[:, :, None], values.reshape(tile_slots, rank_part, probe_count), 0.0
    ).astype(BF)
    targets = (column_rows[0][None, :] == lax.iota(jnp.int32, tile_count)[:, None]).astype(BF)
    outgoing = jnp.einsum(
        "dk,krp->drp", targets, coefficients, preferred_element_type=F32
    ).astype(BF)
    sources = (row_columns[0][:, None] == lax.iota(jnp.int32, tile_count)[None, :]).astype(BF)
    chosen = jnp.einsum(
        "kj,jrp->krp",
        sources,
        lax.all_to_all(outgoing, "tile", split_axis=0, concat_axis=0, tiled=True),
        preferred_element_type=F32,
    ).astype(BF)
    chosen = chosen.reshape(tile_slots * rank_part, -1)
    far_sum = lax.dot_general(
        left_flat, chosen, (((0,), (0,)), ((), ())), preferred_element_type=F32
    )
    arrived = {}
    for offset in (1, -1):
        arrived[offset] = shifted(operand, "tile", offset)
    stacked = jnp.concatenate([arrived[1], operand, arrived[-1]], axis=0)
    near_sum = jnp.dot(dense_flat, stacked, preferred_element_type=F32)
    partial_image = near_sum + far_sum
    return lax.psum_scatter(partial_image, "list", scatter_dimension=0, tiled=True)


def many_slots(probes, right_bases, left_bases, near_tiles, tile_ranks, column_rows, row_columns):
    rest = (right_bases, left_bases, near_tiles, tile_ranks, column_rows, row_columns)
    first_pass = image_part(probes.astype(BF), *rest).astype(BF)
    return image_part(first_pass, *rest)


VMEM = pl.BlockSpec(memory_space=pltpu.VMEM)


def kernel_call(kernel, outs, operands, flops=0):
    return pl.pallas_call(
        kernel,
        out_shape=tuple(jax.ShapeDtypeStruct(shape, kind) for shape, kind in outs),
        in_specs=[VMEM] * len(operands),
        out_specs=tuple(VMEM for _ in outs),
        compiler_params=pltpu.CompilerParams(vmem_limit_bytes=16 * 2**20),
        cost_estimate=pl.CostEstimate(
            flops=flops, bytes_accessed=2 * operands[0].size, transcendentals=0
        ),
    )(*operands)


def stacked(pieces):
    return jnp.concatenate([piece.astype(F32) for piece in pieces]).astype(BF)


def under_rank(values, group, rank_part, ranks_ref):
    level = group * rank_part + lax.broadcasted_iota(jnp.int32, values.shape, 0)
    return jnp.where(level < ranks_ref[...], values, 0.0)


def coefficient_kernel(bases_ref, across_ref, block_ref, other_ref, ranks_ref, out_ref):
    me = lax.axis_index("list")
    ranks = bases_ref.shape[1]
    rows = block_ref.shape[0]
    total = 0.0
    for part, operand_ref in ((me, block_ref), (me ^ 1, other_ref)):
        cut = pl.ds(pl.multiple_of(part * rows, rows), rows)
        bases = stacked([bases_ref[0, :, cut], across_ref[0, :, cut]])
        total += jnp.dot(bases, operand_ref[...], preferred_element_type=F32)
    halves = [
        under_rank(total[index * ranks : (index + 1) * ranks], group, ranks, ranks_ref)
        for index, group in enumerate((me, me ^ 2))
    ]
    out_ref[...] = jnp.concatenate(halves).astype(out_ref.dtype)


def tile_swap(block, turn):
    return lax.ppermute(block, "tile", [(i, i ^ turn) for i in range(lax.axis_size("tile"))])


def middle_swap(block):
    tiles, parts = lax.axis_size("tile"), lax.axis_size("list")
    route = []
    for tile in range(tiles):
        for part in range(parts):
            to = (tile - 1 + 2 * (tile % 2), part)
            if tile in (0, tiles - 1):
                to = (tile, part ^ 1)
            route.append((tile * parts + part, to[0] * parts + to[1]))
    return lax.ppermute(block, ("tile", "list"), route)


def list_swap(block, bit):
    return lax.ppermute(block, "list", [(i, i ^ bit) for i in range(lax.axis_size("list"))])


def image_kernel(turns, near_ref, bases_ref, across_ref, columns_ref, *refs):
    block_refs, coefficient_refs, out_ref = refs[:3], refs[3:7], refs[7]
    count = lax.axis_size("tile")
    tile = lax.axis_index("tile")
    me = lax.axis_index("list")
    rows = near_ref.shape[2]
    chosen = coefficient_refs[0][...]
    slots = chosen.shape[0]
    for turn in (1, 2, 3):
        other_ref = coefficient_refs[turn]
        other = other_ref[other_ref.shape[0] - slots :, :]
        chosen = jnp.where(columns_ref[...] == tile ^ turn, other, chosen)
    odd = lax.rem(tile, 2)
    inside = (tile > 0) & (tile < count - 1)
    blocks = [
        (1, block_refs[0][...]),
        (2 - 2 * odd, block_refs[1][:rows, :]),
        (2 * odd, jnp.where(inside, block_refs[2][...], 0)),
    ]
    totals = []
    for index, turn in enumerate(turns):
        part = me ^ turn
        cut = pl.ds(pl.multiple_of(part * rows, rows), rows)
        left = stacked([bases_ref[1, :, cut], across_ref[1, :, cut]])
        total = lax.dot_general(
            left, chosen, (((0,), (0,)), ((), ())), preferred_element_type=F32
        )
        for side, block in blocks:
            total += jnp.dot(near_ref[side, cut, :], block, preferred_element_type=F32)
        out_ref[index] = total
        totals.append((cut, total.astype(BF)))
    return totals


def right_products(totals, bases_ref, across_ref, pair_ref):
    sums = 0.0
    for cut, total in totals:
        groups = [bases_ref[0, :, cut], across_ref[0, :, cut], pair_ref[0, :, cut], pair_ref[1, :, cut]]
        sums += jnp.dot(stacked(groups), total, preferred_element_type=F32)
    return sums


def sent_kernel(near_ref, bases_ref, across_ref, columns_ref, *refs):
    operands, pair_ref, out_ref, sums_ref = refs[:7], *refs[7:]
    totals = image_kernel(
        (1, 3), near_ref, bases_ref, across_ref, columns_ref, *operands, out_ref
    )
    sums_ref[...] = right_products(totals, bases_ref, across_ref, pair_ref)


def kept_kernel(near_ref, bases_ref, across_ref, columns_ref, *refs):
    operands, (pair_ref, ranks_ref, sums_ref), outs = refs[:7], refs[7:10], refs[10:]
    totals = image_kernel(
        (0, 2), near_ref, bases_ref, across_ref, columns_ref, *operands, outs[0]
    )
    sums = sums_ref[...] + right_products(totals, bases_ref, across_ref, pair_ref)
    me = lax.axis_index("list")
    ranks = bases_ref.shape[1]
    for index, turn in enumerate((0, 2, 1, 3)):
        values = sums[index * ranks : (index + 1) * ranks]
        start = index % 2 * ranks
        outs[1 + index // 2][start : start + ranks, :] = under_rank(
            values, me ^ turn, ranks, ranks_ref
        )


def second_kernel(turns, *refs):
    image_kernel(turns, *refs)


def one_slot(probes, right_bases, left_bases, near_tiles, tile_ranks, column_rows, row_columns):
    rows, probe_count = probes.shape
    rank_part = right_bases.shape[2]
    near = near_tiles[0].transpose(1, 0, 2)
    flops = 2 * near.size * probe_count
    halves = ((2, rows, probe_count), F32)
    small = ((2 * rank_part, probe_count), F32)

    bases = jnp.stack([right_bases[0, 0], left_bases[0, 0]])
    bases, probes = lax.optimization_barrier((bases, probes))
    bases_across = list_swap(bases, 2)
    block = probes.astype(BF)
    beside = [block, tile_swap(block, 1), middle_swap(block)]
    (own,) = kernel_call(
        coefficient_kernel,
        [((2 * rank_part, probe_count), BF)],
        (bases, bases_across, block, list_swap(block, 1), tile_ranks),
        8 * flops,
    )
    coefficients = [own] + [tile_swap(own, turn) for turn in (1, 2, 3)]
    right = jnp.stack([bases[0], bases_across[0]])
    right, _ = lax.optimization_barrier((right, own))
    right_pair = list_swap(right, 1)

    fixed = (near, bases, bases_across, row_columns)
    operands = (*fixed, *beside, *coefficients, right_pair)
    send, sums = kernel_call(
        sent_kernel, [halves, ((4 * rank_part, probe_count), F32)], operands, flops
    )
    arrived = list_swap(send, 1)
    keep, small_keep, small_send = kernel_call(
        kept_kernel, [halves, small, small], (*operands, tile_ranks, sums), flops
    )
    own = (small_keep + list_swap(small_send, 1)).astype(BF)
    pair = keep + arrived
    second, third = tile_swap(own, 2), tile_swap(own, 3)
    block = (pair[0] + list_swap(pair[1].astype(BF), 2)).astype(BF)
    message = jnp.concatenate([block, own])
    message, second, third = lax.optimization_barrier((message, second, third))
    message = tile_swap(message, 1)
    beside = [block, message, middle_swap(block)]
    coefficients = [own, message, second, third]

    operands = (*fixed, *beside, *coefficients)
    (send,) = kernel_call(
        functools.partial(second_kernel, (1, 3)), [halves], operands, flops
    )
    arrived = list_swap(send, 1)
    (keep,) = kernel_call(
        functools.partial(second_kernel, (0, 2)), [halves], operands, flops
    )
    pair = keep + arrived
    return pair[0] + list_swap(pair[1].astype(BF), 2)


def local(probes, right_bases, left_bases, near_tiles, tile_ranks, column_rows, row_columns):
    few = lax.axis_size("tile") == 4 and lax.axis_size("list") == 4
    small = right_bases.shape[1] == 1 and few
    form = one_slot if small else many_slots
    return form(
        probes, right_bases, left_bases, near_tiles, tile_ranks, column_rows, row_columns
    )


def solution(mesh):
    placed = (
        P(("group", "tile", "list"), None),
        P(("group", "tile"), None, "list", None),
        P(("group", "tile"), None, "list", None),
        P(("group", "tile"), None, None, "list"),
        P(("group", "tile"), None),
        P("tile", None),
        P("tile", None),
    )
    return jax.shard_map(
        local,
        mesh=mesh,
        in_specs=placed,
        out_specs=P(("group", "tile", "list"), None),
        check_vma=False,
    )
```

```python
import functools

import jax
import jax.numpy as jnp
from jax import lax
from jax.experimental import pallas as pl
from jax.experimental.pallas import tpu as pltpu
from jax.sharding import PartitionSpec as P

BF = jnp.bfloat16
F32 = jnp.float32


def shifted(block, axis, distance):
    devices = range(lax.axis_size(axis))
    route = [(i - distance, i) for i in devices if i - distance in devices]
    return lax.ppermute(block, axis, route)


def image_part(operand, right_bases, left_bases, near_tiles, tile_ranks, column_rows, row_columns):
    tile_slots = right_bases.shape[1]
    rank_part = right_bases.shape[2]
    tile_rows = right_bases.shape[3]
    probe_count = operand.shape[1]
    tile_count = lax.axis_size("tile")
    right_flat = right_bases.reshape(tile_slots * rank_part, tile_rows)
    left_flat = left_bases.reshape(tile_slots * rank_part, tile_rows)
    dense_flat = near_tiles.reshape(tile_rows, -1)
    values = jnp.dot(
        right_flat,
        lax.all_gather(operand, "list", axis=0, tiled=True),
        preferred_element_type=F32,
    )
    rank_level = lax.axis_index("list") * rank_part + lax.iota(jnp.int32, rank_part)
    rank_mask = rank_level[None, :] < tile_ranks[0][:, None]
    coefficients = jnp.where(
        rank_mask[:, :, None], values.reshape(tile_slots, rank_part, probe_count), 0.0
    ).astype(BF)
    targets = (column_rows[0][None, :] == lax.iota(jnp.int32, tile_count)[:, None]).astype(BF)
    outgoing = jnp.einsum(
        "dk,krp->drp", targets, coefficients, preferred_element_type=F32
    ).astype(BF)
    sources = (row_columns[0][:, None] == lax.iota(jnp.int32, tile_count)[None, :]).astype(BF)
    chosen = jnp.einsum(
        "kj,jrp->krp",
        sources,
        lax.all_to_all(outgoing, "tile", split_axis=0, concat_axis=0, tiled=True),
        preferred_element_type=F32,
    ).astype(BF)
    chosen = chosen.reshape(tile_slots * rank_part, -1)
    far_sum = lax.dot_general(
        left_flat, chosen, (((0,), (0,)), ((), ())), preferred_element_type=F32
    )
    arrived = {}
    for offset in (1, -1):
        arrived[offset] = shifted(operand, "tile", offset)
    stacked = jnp.concatenate([arrived[1], operand, arrived[-1]], axis=0)
    near_sum = jnp.dot(dense_flat, stacked, preferred_element_type=F32)
    partial_image = near_sum + far_sum
    return lax.psum_scatter(partial_image, "list", scatter_dimension=0, tiled=True)


def many_slots(probes, right_bases, left_bases, near_tiles, tile_ranks, column_rows, row_columns):
    rest = (right_bases, left_bases, near_tiles, tile_ranks, column_rows, row_columns)
    first_pass = image_part(probes.astype(BF), *rest).astype(BF)
    return image_part(first_pass, *rest)


VMEM = pl.BlockSpec(memory_space=pltpu.VMEM)


def kernel_call(kernel, outs, operands, flops=0):
    return pl.pallas_call(
        kernel,
        out_shape=tuple(jax.ShapeDtypeStruct(shape, kind) for shape, kind in outs),
        in_specs=[VMEM] * len(operands),
        out_specs=tuple(VMEM for _ in outs),
        compiler_params=pltpu.CompilerParams(vmem_limit_bytes=16 * 2**20),
        cost_estimate=pl.CostEstimate(
            flops=flops, bytes_accessed=2 * operands[0].size, transcendentals=0
        ),
    )(*operands)


def stacked(pieces):
    return jnp.concatenate([piece.astype(F32) for piece in pieces]).astype(BF)


def under_rank(values, group, rank_part, ranks_ref):
    level = group * rank_part + lax.broadcasted_iota(jnp.int32, values.shape, 0)
    return jnp.where(level < ranks_ref[...], values, 0.0)


def coefficient_kernel(bases_ref, across_ref, block_ref, other_ref, ranks_ref, out_ref):
    me = lax.axis_index("list")
    ranks = bases_ref.shape[1]
    rows = block_ref.shape[0]
    total = 0.0
    for part, operand_ref in ((me, block_ref), (me ^ 1, other_ref)):
        cut = pl.ds(pl.multiple_of(part * rows, rows), rows)
        bases = stacked([bases_ref[0, :, cut], across_ref[0, :, cut]])
        total += jnp.dot(bases, operand_ref[...], preferred_element_type=F32)
    halves = [
        under_rank(total[index * ranks : (index + 1) * ranks], group, ranks, ranks_ref)
        for index, group in enumerate((me, me ^ 2))
    ]
    out_ref[...] = jnp.concatenate(halves).astype(out_ref.dtype)


def tile_swap(block, turn):
    return lax.ppermute(block, "tile", [(i, i ^ turn) for i in range(lax.axis_size("tile"))])


def middle_swap(block):
    tiles, parts = lax.axis_size("tile"), lax.axis_size("list")
    route = []
    for tile in range(tiles):
        for part in range(parts):
            to = (tile - 1 + 2 * (tile % 2), part)
            if tile in (0, tiles - 1):
                to = (tile, part ^ 1)
            route.append((tile * parts + part, to[0] * parts + to[1]))
    return lax.ppermute(block, ("tile", "list"), route)


def list_swap(block, bit):
    return lax.ppermute(block, "list", [(i, i ^ bit) for i in range(lax.axis_size("list"))])


def image_kernel(turns, near_ref, bases_ref, across_ref, columns_ref, *refs):
    block_refs, coefficients_ref, out_ref = refs[:3], refs[3], refs[4]
    count = lax.axis_size("tile")
    tile = lax.axis_index("tile")
    me = lax.axis_index("list")
    rows = near_ref.shape[2]
    chosen = coefficients_ref[0]
    for column in range(1, count):
        chosen = jnp.where(columns_ref[...] == column, coefficients_ref[column], chosen)
    odd = lax.rem(tile, 2)
    inside = (tile > 0) & (tile < count - 1)
    blocks = [
        (1, block_refs[0][...]),
        (2 - 2 * odd, block_refs[1][...]),
        (2 * odd, jnp.where(inside, block_refs[2][...], 0)),
    ]
    totals = []
    for index, turn in enumerate(turns):
        part = me ^ turn
        cut = pl.ds(pl.multiple_of(part * rows, rows), rows)
        left = stacked([bases_ref[1, :, cut], across_ref[1, :, cut]])
        total = lax.dot_general(
            left, chosen, (((0,), (0,)), ((), ())), preferred_element_type=F32
        )
        for side, block in blocks:
            total += jnp.dot(near_ref[side, cut, :], block, preferred_element_type=F32)
        out_ref[index] = total
        totals.append((cut, total.astype(BF)))
    return totals


def right_products(totals, bases_ref, across_ref, pair_ref):
    sums = 0.0
    for cut, total in totals:
        groups = [bases_ref[0, :, cut], across_ref[0, :, cut], pair_ref[0, :, cut], pair_ref[1, :, cut]]
        sums += jnp.dot(stacked(groups), total, preferred_element_type=F32)
    return sums


def sent_kernel(near_ref, bases_ref, across_ref, columns_ref, *refs):
    operands, pair_ref, out_ref, sums_ref = refs[:4], *refs[4:]
    totals = image_kernel(
        (1, 3), near_ref, bases_ref, across_ref, columns_ref, *operands, out_ref
    )
    sums_ref[...] = right_products(totals, bases_ref, across_ref, pair_ref)


def kept_kernel(near_ref, bases_ref, across_ref, columns_ref, *refs):
    operands, (pair_ref, ranks_ref, sums_ref), outs = refs[:4], refs[4:7], refs[7:]
    totals = image_kernel(
        (0, 2), near_ref, bases_ref, across_ref, columns_ref, *operands, outs[0]
    )
    sums = sums_ref[...] + right_products(totals, bases_ref, across_ref, pair_ref)
    me = lax.axis_index("list")
    ranks = bases_ref.shape[1]
    for index, turn in enumerate((0, 2, 1, 3)):
        values = sums[index * ranks : (index + 1) * ranks]
        start = index % 2 * ranks
        outs[1 + index // 2][start : start + ranks, :] = under_rank(
            values, me ^ turn, ranks, ranks_ref
        )


def second_kernel(turns, *refs):
    image_kernel(turns, *refs)


def over_tiles(own):
    copies = jnp.broadcast_to(own, (lax.axis_size("tile"), *own.shape))
    return lax.all_to_all(copies, "tile", 0, 0, tiled=True)


def one_slot(probes, right_bases, left_bases, near_tiles, tile_ranks, column_rows, row_columns):
    rows, probe_count = probes.shape
    rank_part = right_bases.shape[2]
    near = near_tiles[0].transpose(1, 0, 2)
    flops = 2 * near.size * probe_count
    halves = ((2, rows, probe_count), F32)
    small = ((2 * rank_part, probe_count), F32)

    bases = jnp.stack([right_bases[0, 0], left_bases[0, 0]])
    bases, probes = lax.optimization_barrier((bases, probes))
    bases_across = list_swap(bases, 2)
    block = probes.astype(BF)
    beside = [block, tile_swap(block, 1), middle_swap(block)]
    (own,) = kernel_call(
        coefficient_kernel,
        [((2 * rank_part, probe_count), BF)],
        (bases, bases_across, block, list_swap(block, 1), tile_ranks),
        8 * flops,
    )
    coefficients = over_tiles(own)
    right = jnp.stack([bases[0], bases_across[0]])
    right, _ = lax.optimization_barrier((right, own))
    right_pair = list_swap(right, 1)

    fixed = (near, bases, bases_across, row_columns)
    operands = (*fixed, *beside, coefficients, right_pair)
    send, sums = kernel_call(
        sent_kernel, [halves, ((4 * rank_part, probe_count), F32)], operands, flops
    )
    arrived = list_swap(send, 1)
    keep, small_keep, small_send = kernel_call(
        kept_kernel, [halves, small, small], (*operands, tile_ranks, sums), flops
    )
    own = (small_keep + list_swap(small_send, 1)).astype(BF)
    pair = keep + arrived
    own, pair = lax.optimization_barrier((own, pair))
    coefficients = over_tiles(own)
    block = (pair[0] + list_swap(pair[1].astype(BF), 2)).astype(BF)
    block, coefficients = lax.optimization_barrier((block, coefficients))
    beside = [block, tile_swap(block, 1), middle_swap(block)]

    operands = (*fixed, *beside, coefficients)
    (send,) = kernel_call(
        functools.partial(second_kernel, (1, 3)), [halves], operands, flops
    )
    arrived = list_swap(send, 1)
    (keep,) = kernel_call(
        functools.partial(second_kernel, (0, 2)), [halves], operands, flops
    )
    pair = keep + arrived
    return pair[0] + list_swap(pair[1].astype(BF), 2)


def local(probes, right_bases, left_bases, near_tiles, tile_ranks, column_rows, row_columns):
    few = lax.axis_size("tile") == 4 and lax.axis_size("list") == 4
    small = right_bases.shape[1] == 1 and few
    form = one_slot if small else many_slots
    return form(
        probes, right_bases, left_bases, near_tiles, tile_ranks, column_rows, row_columns
    )


def solution(mesh):
    placed = (
        P(("group", "tile", "list"), None),
        P(("group", "tile"), None, "list", None),
        P(("group", "tile"), None, "list", None),
        P(("group", "tile"), None, None, "list"),
        P(("group", "tile"), None),
        P("tile", None),
        P("tile", None),
    )
    return jax.shard_map(
        local,
        mesh=mesh,
        in_specs=placed,
        out_specs=P(("group", "tile", "list"), None),
        check_vma=False,
    )
```

```python
import functools

import jax
import jax.numpy as jnp
from jax import lax
from jax.experimental import pallas as pl
from jax.experimental.pallas import tpu as pltpu
from jax.sharding import PartitionSpec as P

BF = jnp.bfloat16
F32 = jnp.float32


def shifted(block, axis, distance):
    devices = range(lax.axis_size(axis))
    route = [(i - distance, i) for i in devices if i - distance in devices]
    return lax.ppermute(block, axis, route)


def image_part(operand, right_bases, left_bases, near_tiles, tile_ranks, column_rows, row_columns):
    tile_slots = right_bases.shape[1]
    rank_part = right_bases.shape[2]
    tile_rows = right_bases.shape[3]
    probe_count = operand.shape[1]
    tile_count = lax.axis_size("tile")
    right_flat = right_bases.reshape(tile_slots * rank_part, tile_rows)
    left_flat = left_bases.reshape(tile_slots * rank_part, tile_rows)
    dense_flat = near_tiles.reshape(tile_rows, -1)
    values = jnp.dot(
        right_flat,
        lax.all_gather(operand, "list", axis=0, tiled=True),
        preferred_element_type=F32,
    )
    rank_level = lax.axis_index("list") * rank_part + lax.iota(jnp.int32, rank_part)
    rank_mask = rank_level[None, :] < tile_ranks[0][:, None]
    coefficients = jnp.where(
        rank_mask[:, :, None], values.reshape(tile_slots, rank_part, probe_count), 0.0
    ).astype(BF)
    targets = (column_rows[0][None, :] == lax.iota(jnp.int32, tile_count)[:, None]).astype(BF)
    outgoing = jnp.einsum(
        "dk,krp->drp", targets, coefficients, preferred_element_type=F32
    ).astype(BF)
    sources = (row_columns[0][:, None] == lax.iota(jnp.int32, tile_count)[None, :]).astype(BF)
    chosen = jnp.einsum(
        "kj,jrp->krp",
        sources,
        lax.all_to_all(outgoing, "tile", split_axis=0, concat_axis=0, tiled=True),
        preferred_element_type=F32,
    ).astype(BF)
    chosen = chosen.reshape(tile_slots * rank_part, -1)
    far_sum = lax.dot_general(
        left_flat, chosen, (((0,), (0,)), ((), ())), preferred_element_type=F32
    )
    arrived = {}
    for offset in (1, -1):
        arrived[offset] = shifted(operand, "tile", offset)
    stacked = jnp.concatenate([arrived[1], operand, arrived[-1]], axis=0)
    near_sum = jnp.dot(dense_flat, stacked, preferred_element_type=F32)
    partial_image = near_sum + far_sum
    return lax.psum_scatter(partial_image, "list", scatter_dimension=0, tiled=True)


def many_slots(probes, right_bases, left_bases, near_tiles, tile_ranks, column_rows, row_columns):
    rest = (right_bases, left_bases, near_tiles, tile_ranks, column_rows, row_columns)
    first_pass = image_part(probes.astype(BF), *rest).astype(BF)
    return image_part(first_pass, *rest)


VMEM = pl.BlockSpec(memory_space=pltpu.VMEM)


def kernel_call(kernel, outs, operands, flops=0):
    return pl.pallas_call(
        kernel,
        out_shape=tuple(jax.ShapeDtypeStruct(shape, kind) for shape, kind in outs),
        in_specs=[VMEM] * len(operands),
        out_specs=tuple(VMEM for _ in outs),
        compiler_params=pltpu.CompilerParams(vmem_limit_bytes=16 * 2**20),
        cost_estimate=pl.CostEstimate(
            flops=flops, bytes_accessed=2 * operands[0].size, transcendentals=0
        ),
    )(*operands)


def stacked(pieces):
    return jnp.concatenate([piece.astype(F32) for piece in pieces]).astype(BF)


def under_rank(sums, turns, rank_part, ranks_ref):
    me = lax.axis_index("list")
    groups = []
    for index, turn in enumerate(turns):
        values = sums[index * rank_part : (index + 1) * rank_part]
        level = (me ^ turn) * rank_part + lax.broadcasted_iota(jnp.int32, values.shape, 0)
        groups.append(jnp.where(level < ranks_ref[...], values, 0.0))
    return groups


def basis_groups(side, cut, refs):
    pieces = [ref[side, :, cut] for ref in refs[:2]]
    return stacked(pieces + [ref[index, :, cut] for ref in refs[2:] for index in range(2)])


def coefficient_kernel(bases_ref, across_ref, block_ref, beside_ref, ranks_ref, out_ref):
    me = lax.axis_index("list")
    rows = block_ref.shape[0]
    total = 0.0
    for part, operand_ref in ((me, block_ref), (me ^ 1, beside_ref)):
        cut = pl.ds(pl.multiple_of(part * rows, rows), rows)
        bases = basis_groups(0, cut, (bases_ref, across_ref))
        total += jnp.dot(bases, operand_ref[...], preferred_element_type=F32)
    groups = under_rank(total, (0, 2), bases_ref.shape[1], ranks_ref)
    out_ref[...] = jnp.concatenate(groups).astype(out_ref.dtype)


def tile_swap(block, turn):
    return lax.ppermute(block, "tile", [(i, i ^ turn) for i in range(lax.axis_size("tile"))])


def middle_swap(block):
    tiles, parts = lax.axis_size("tile"), lax.axis_size("list")
    route = []
    for tile in range(tiles):
        for part in range(parts):
            to = (tile - 1 + 2 * (tile % 2), part)
            if tile in (0, tiles - 1):
                to = (tile, part ^ 1)
            route.append((tile * parts + part, to[0] * parts + to[1]))
    return lax.ppermute(block, ("tile", "list"), route)


def far_swap(block):
    tiles, parts = lax.axis_size("tile"), lax.axis_size("list")
    route = [
        (tile * parts + part, (tile ^ (2 + part % 2)) * parts + part)
        for tile in range(tiles)
        for part in range(parts)
    ]
    return lax.ppermute(block, ("tile", "list"), route)


def list_swap(block, bit):
    return lax.ppermute(block, "list", [(i, i ^ bit) for i in range(lax.axis_size("list"))])


def near_choice(columns, tile, me, refs):
    chosen = refs[0][...]
    for turn in (1, 2, 3):
        chosen = jnp.where(columns == tile ^ turn, refs[turn][...], chosen)
    return chosen


def far_choice(columns, tile, me, refs):
    own_ref, message_ref, far_ref = refs
    half = own_ref.shape[0] // 2
    first = jnp.where(columns == tile, own_ref[:half, :], 0)
    first = jnp.where(columns == tile ^ 1, message_ref[message_ref.shape[0] - half :, :], first)
    far = columns == tile ^ (2 + lax.rem(me, 2))
    return jnp.concatenate(
        [jnp.where(far, far_ref[:half, :], first), jnp.where(far, far_ref[half:, :], 0)]
    )


def image_kernel(choice, turns, near_ref, columns_ref, bases_refs, *refs):
    block_refs, coefficient_refs, out_ref = refs[:3], refs[3:-1], refs[-1]
    count = lax.axis_size("tile")
    tile = lax.axis_index("tile")
    me = lax.axis_index("list")
    rows = near_ref.shape[2]
    chosen = choice(columns_ref[...], tile, me, coefficient_refs)
    odd = lax.rem(tile, 2)
    inside = (tile > 0) & (tile < count - 1)
    blocks = [
        (1, block_refs[0][...]),
        (2 - 2 * odd, block_refs[1][:rows, :]),
        (2 * odd, jnp.where(inside, block_refs[2][...], 0)),
    ]
    totals = []
    for index, turn in enumerate(turns):
        part = me ^ turn
        cut = pl.ds(pl.multiple_of(part * rows, rows), rows)
        left = basis_groups(1, cut, bases_refs)
        total = lax.dot_general(
            left, chosen, (((0,), (0,)), ((), ())), preferred_element_type=F32
        )
        for side, block in blocks:
            total += jnp.dot(near_ref[side, cut, :], block, preferred_element_type=F32)
        out_ref[index] = total
        totals.append((cut, total.astype(BF)))
    return totals


def right_products(totals, bases_refs):
    return sum(
        jnp.dot(basis_groups(0, cut, bases_refs), total, preferred_element_type=F32)
        for cut, total in totals
    )


def sent_kernel(near_ref, columns_ref, bases_ref, across_ref, other_ref, *refs):
    bases_refs = (bases_ref, across_ref)
    totals = image_kernel(near_choice, (1, 3), near_ref, columns_ref, bases_refs, *refs[:-1])
    refs[-1][...] = right_products(totals, (*bases_refs, other_ref))


def kept_kernel(near_ref, columns_ref, bases_ref, across_ref, other_ref, *refs):
    operands, (ranks_ref, sums_ref, out_ref, own_ref, send_ref) = refs[:-5], refs[-5:]
    bases_refs = (bases_ref, across_ref)
    totals = image_kernel(
        near_choice, (0, 2), near_ref, columns_ref, bases_refs, *operands, out_ref
    )
    sums = sums_ref[...] + right_products(totals, (*bases_refs, other_ref))
    groups = under_rank(sums, (0, 2, 1, 3), bases_ref.shape[1], ranks_ref)
    own_ref[...] = jnp.concatenate(groups)
    send_ref[...] = jnp.concatenate(groups[2:] + groups[:2])


def second_kernel(turns, near_ref, columns_ref, bases_ref, across_ref, other_ref, *refs):
    bases_refs = (bases_ref, across_ref, other_ref)
    image_kernel(far_choice, turns, near_ref, columns_ref, bases_refs, *refs)


def one_slot(probes, right_bases, left_bases, near_tiles, tile_ranks, column_rows, row_columns):
    rows, probe_count = probes.shape
    rank_part = right_bases.shape[2]
    near = near_tiles[0].transpose(1, 0, 2)
    flops = 2 * near.size * probe_count
    halves = ((2, rows, probe_count), F32)
    ranks = 4 * rank_part

    bases = jnp.stack([right_bases[0, 0], left_bases[0, 0]])
    bases, probes = lax.optimization_barrier((bases, probes))
    across = list_swap(bases, 2)
    block = probes.astype(BF)
    beside = [block, tile_swap(block, 1), middle_swap(block)]
    (own,) = kernel_call(
        coefficient_kernel,
        [((ranks // 2, probe_count), BF)],
        (bases, across, block, list_swap(block, 1), tile_ranks),
        8 * flops,
    )
    coefficients = [own] + [tile_swap(own, turn) for turn in (1, 2, 3)]
    right, _ = lax.optimization_barrier((jnp.stack([bases[0], across[0]]), own))
    fixed = (near, row_columns, bases, across)
    operands = (*fixed, list_swap(right, 1), *beside, *coefficients)
    send, sums = kernel_call(sent_kernel, [halves, ((ranks, probe_count), F32)], operands, flops)
    arrived = list_swap(send, 1)
    keep, own, send = kernel_call(
        kept_kernel,
        [halves] + [((ranks, probe_count), F32)] * 2,
        (*operands, tile_ranks, sums),
        flops,
    )
    own = (own + list_swap(send, 1)).astype(BF)
    pair = keep + arrived
    held, held_across, pair = lax.optimization_barrier((bases, across, pair))
    left = list_swap(jnp.stack([held[1], held_across[1]]), 1)
    far = far_swap(own)
    block = (pair[0] + list_swap(pair[1].astype(BF), 2)).astype(BF)
    message, far = lax.optimization_barrier((jnp.concatenate([block, own[: ranks // 2]]), far))
    message = tile_swap(message, 1)
    beside = [block, message, middle_swap(block)]

    operands = (*fixed, left, *beside, own, message, far)
    (send,) = kernel_call(
        functools.partial(second_kernel, (1, 3)), [halves], operands, flops
    )
    arrived = list_swap(send, 1)
    (keep,) = kernel_call(
        functools.partial(second_kernel, (0, 2)), [halves], operands, flops
    )
    pair = keep + arrived
    return pair[0] + list_swap(pair[1].astype(BF), 2)


def local(probes, right_bases, left_bases, near_tiles, tile_ranks, column_rows, row_columns):
    few = lax.axis_size("tile") == 4 and lax.axis_size("list") == 4
    small = right_bases.shape[1] == 1 and few
    form = one_slot if small else many_slots
    return form(
        probes, right_bases, left_bases, near_tiles, tile_ranks, column_rows, row_columns
    )


def solution(mesh):
    placed = (
        P(("group", "tile", "list"), None),
        P(("group", "tile"), None, "list", None),
        P(("group", "tile"), None, "list", None),
        P(("group", "tile"), None, None, "list"),
        P(("group", "tile"), None),
        P("tile", None),
        P("tile", None),
    )
    return jax.shard_map(
        local,
        mesh=mesh,
        in_specs=placed,
        out_specs=P(("group", "tile", "list"), None),
        check_vma=False,
    )
```

```python
import functools

import jax
import jax.numpy as jnp
from jax import lax
from jax.experimental import pallas as pl
from jax.experimental.pallas import tpu as pltpu
from jax.sharding import PartitionSpec as P

BF = jnp.bfloat16
F32 = jnp.float32


def shifted(block, axis, distance):
    devices = range(lax.axis_size(axis))
    route = [(i - distance, i) for i in devices if i - distance in devices]
    return lax.ppermute(block, axis, route)


def image_part(operand, right_bases, left_bases, near_tiles, tile_ranks, column_rows, row_columns):
    tile_slots = right_bases.shape[1]
    rank_part = right_bases.shape[2]
    tile_rows = right_bases.shape[3]
    probe_count = operand.shape[1]
    tile_count = lax.axis_size("tile")
    right_flat = right_bases.reshape(tile_slots * rank_part, tile_rows)
    left_flat = left_bases.reshape(tile_slots * rank_part, tile_rows)
    dense_flat = near_tiles.reshape(tile_rows, -1)
    values = jnp.dot(
        right_flat,
        lax.all_gather(operand, "list", axis=0, tiled=True),
        preferred_element_type=F32,
    )
    rank_level = lax.axis_index("list") * rank_part + lax.iota(jnp.int32, rank_part)
    rank_mask = rank_level[None, :] < tile_ranks[0][:, None]
    coefficients = jnp.where(
        rank_mask[:, :, None], values.reshape(tile_slots, rank_part, probe_count), 0.0
    ).astype(BF)
    targets = (column_rows[0][None, :] == lax.iota(jnp.int32, tile_count)[:, None]).astype(BF)
    outgoing = jnp.einsum(
        "dk,krp->drp", targets, coefficients, preferred_element_type=F32
    ).astype(BF)
    sources = (row_columns[0][:, None] == lax.iota(jnp.int32, tile_count)[None, :]).astype(BF)
    chosen = jnp.einsum(
        "kj,jrp->krp",
        sources,
        lax.all_to_all(outgoing, "tile", split_axis=0, concat_axis=0, tiled=True),
        preferred_element_type=F32,
    ).astype(BF)
    chosen = chosen.reshape(tile_slots * rank_part, -1)
    far_sum = lax.dot_general(
        left_flat, chosen, (((0,), (0,)), ((), ())), preferred_element_type=F32
    )
    arrived = {}
    for offset in (1, -1):
        arrived[offset] = shifted(operand, "tile", offset)
    stacked = jnp.concatenate([arrived[1], operand, arrived[-1]], axis=0)
    near_sum = jnp.dot(dense_flat, stacked, preferred_element_type=F32)
    partial_image = near_sum + far_sum
    return lax.psum_scatter(partial_image, "list", scatter_dimension=0, tiled=True)


def many_slots(probes, right_bases, left_bases, near_tiles, tile_ranks, column_rows, row_columns):
    rest = (right_bases, left_bases, near_tiles, tile_ranks, column_rows, row_columns)
    first_pass = image_part(probes.astype(BF), *rest).astype(BF)
    return image_part(first_pass, *rest)


VMEM = pl.BlockSpec(memory_space=pltpu.VMEM)


def list_swap_in_pieces(block, bit, pieces):
    return jnp.concatenate([list_swap(piece, bit) for piece in jnp.split(block, pieces)])


def kernel_call(kernel, outs, operands, flops=0):
    return pl.pallas_call(
        kernel,
        out_shape=tuple(jax.ShapeDtypeStruct(shape, kind) for shape, kind in outs),
        in_specs=[VMEM] * len(operands),
        out_specs=tuple(VMEM for _ in outs),
        compiler_params=pltpu.CompilerParams(vmem_limit_bytes=16 * 2**20),
        cost_estimate=pl.CostEstimate(
            flops=flops, bytes_accessed=2 * operands[0].size, transcendentals=0
        ),
    )(*operands)


def stacked(pieces):
    return jnp.concatenate([piece.astype(F32) for piece in pieces]).astype(BF)


def under_rank(sums, turns, rank_part, ranks_ref):
    me = lax.axis_index("list")
    groups = []
    for index, turn in enumerate(turns):
        values = sums[index * rank_part : (index + 1) * rank_part]
        level = (me ^ turn) * rank_part + lax.broadcasted_iota(jnp.int32, values.shape, 0)
        groups.append(jnp.where(level < ranks_ref[...], values, 0.0))
    return groups


def basis_groups(side, cut, refs):
    pieces = [ref[side, :, cut] for ref in refs[:2]]
    return stacked(pieces + [ref[index, :, cut] for ref in refs[2:] for index in range(2)])


def coefficient_kernel(bases_ref, across_ref, block_ref, beside_ref, ranks_ref, out_ref):
    me = lax.axis_index("list")
    rows = block_ref.shape[0]
    total = 0.0
    for part, operand_ref in ((me, block_ref), (me ^ 1, beside_ref)):
        cut = pl.ds(pl.multiple_of(part * rows, rows), rows)
        bases = basis_groups(0, cut, (bases_ref, across_ref))
        total += jnp.dot(bases, operand_ref[...], preferred_element_type=F32)
    groups = under_rank(total, (0, 2), bases_ref.shape[1], ranks_ref)
    out_ref[...] = jnp.concatenate(groups).astype(out_ref.dtype)


def tile_swap(block, turn):
    return lax.ppermute(block, "tile", [(i, i ^ turn) for i in range(lax.axis_size("tile"))])


def middle_swap(block):
    tiles, parts = lax.axis_size("tile"), lax.axis_size("list")
    route = []
    for tile in range(tiles):
        for part in range(parts):
            to = (tile - 1 + 2 * (tile % 2), part)
            if tile in (0, tiles - 1):
                to = (tile, part ^ 1)
            route.append((tile * parts + part, to[0] * parts + to[1]))
    return lax.ppermute(block, ("tile", "list"), route)


def far_swap(block):
    tiles, parts = lax.axis_size("tile"), lax.axis_size("list")
    route = [
        (tile * parts + part, (tile ^ (2 + part % 2)) * parts + part)
        for tile in range(tiles)
        for part in range(parts)
    ]
    return lax.ppermute(block, ("tile", "list"), route)


def list_swap(block, bit):
    return lax.ppermute(block, "list", [(i, i ^ bit) for i in range(lax.axis_size("list"))])


def near_choice(columns, tile, me, refs):
    chosen = refs[0][...]
    for turn in (1, 2, 3):
        chosen = jnp.where(columns == tile ^ turn, refs[turn][...], chosen)
    return chosen


def far_choice(columns, tile, me, refs):
    own_ref, message_ref, far_ref = refs
    half = own_ref.shape[0] // 2
    first = jnp.where(columns == tile, own_ref[:half, :], 0)
    first = jnp.where(columns == tile ^ 1, message_ref[message_ref.shape[0] - half :, :], first)
    far = columns == tile ^ (2 + lax.rem(me, 2))
    return jnp.concatenate(
        [jnp.where(far, far_ref[:half, :], first), jnp.where(far, far_ref[half:, :], 0)]
    )


def image_kernel(choice, turns, near_ref, columns_ref, bases_refs, operand_refs, out_refs):
    block_refs, coefficient_refs = operand_refs[:3], operand_refs[3:]
    count = lax.axis_size("tile")
    tile = lax.axis_index("tile")
    me = lax.axis_index("list")
    rows = near_ref.shape[2]
    chosen = choice(columns_ref[...], tile, me, coefficient_refs)
    odd = lax.rem(tile, 2)
    inside = (tile > 0) & (tile < count - 1)
    blocks = [
        (1, block_refs[0][...]),
        (2 - 2 * odd, block_refs[1][:rows, :]),
        (2 * odd, jnp.where(inside, block_refs[2][...], 0)),
    ]
    totals = []
    for turn, out_ref in zip(turns, out_refs):
        part = me ^ turn
        cut = pl.ds(pl.multiple_of(part * rows, rows), rows)
        left = basis_groups(1, cut, bases_refs)
        total = lax.dot_general(
            left, chosen, (((0,), (0,)), ((), ())), preferred_element_type=F32
        )
        for side, block in blocks:
            total += jnp.dot(near_ref[side, cut, :], block, preferred_element_type=F32)
        out_ref[...] = total
        totals.append((cut, total.astype(BF)))
    return totals


def right_products(totals, bases_refs):
    return sum(
        jnp.dot(basis_groups(0, cut, bases_refs), total, preferred_element_type=F32)
        for cut, total in totals
    )


def first_kernel(turns, near_ref, columns_ref, bases_ref, across_ref, other_ref, *refs):
    operand_refs, refs = refs[:7], refs[7:]
    last = 0 in turns
    sums_before, refs = (refs[:1], refs[1:]) if 3 not in turns else ((), refs)
    ranks_ref, refs = (refs[0], refs[1:]) if last else (None, refs)
    bases_refs = (bases_ref, across_ref)
    totals = image_kernel(
        near_choice, turns, near_ref, columns_ref, bases_refs, operand_refs, refs
    )
    sums = right_products(totals, (*bases_refs, other_ref))
    for ref in sums_before:
        sums += ref[...]
    if not last:
        refs[-1][...] = sums
        return
    groups = under_rank(sums, (0, 2, 1, 3), bases_ref.shape[1], ranks_ref)
    refs[-2][...] = jnp.concatenate(groups)
    refs[-1][...] = jnp.concatenate(groups[2:] + groups[:2])


def second_kernel(turns, near_ref, columns_ref, bases_ref, across_ref, other_ref, *refs):
    bases_refs = (bases_ref, across_ref, other_ref)
    image_kernel(far_choice, turns, near_ref, columns_ref, bases_refs, refs[:6], refs[6:])


def one_slot(probes, right_bases, left_bases, near_tiles, tile_ranks, column_rows, row_columns):
    rows, probe_count = probes.shape
    rank_part = right_bases.shape[2]
    near = near_tiles[0].transpose(1, 0, 2)
    flops = 2 * near.size * probe_count
    part = ((rows, probe_count), F32)
    ranks = 4 * rank_part

    bases = jnp.stack([right_bases[0, 0], left_bases[0, 0]])
    bases, probes = lax.optimization_barrier((bases, probes))
    across = list_swap(bases, 2)
    block = probes.astype(BF)
    beside = [block, tile_swap(block, 1), middle_swap(block)]
    (own,) = kernel_call(
        coefficient_kernel,
        [((ranks // 2, probe_count), BF)],
        (bases, across, block, list_swap(block, 1), tile_ranks),
        8 * flops,
    )
    coefficients = [own] + [tile_swap(own, turn) for turn in (1, 2, 3)]
    right, _ = lax.optimization_barrier((jnp.stack([bases[0], across[0]]), own))
    fixed = (near, row_columns, bases, across)
    operands = (*fixed, list_swap(right, 1), *beside, *coefficients)
    small = ((ranks, probe_count), F32)

    def first(turns, outs, more=()):
        kernel = functools.partial(first_kernel, turns)
        return kernel_call(kernel, outs, (*operands, *more), len(turns) * flops // 4)

    send, sums = first((3,), [part, small])
    arrived = list_swap(send, 1)
    crossing, send, keep, own, other = first(
        (2, 1, 0), [part] * 3 + [small] * 2, (sums, tile_ranks)
    )
    crossed = list_swap((crossing + arrived).astype(BF), 2)
    own = (own + list_swap(other, 1)).astype(BF)
    far = far_swap(own)
    block = (keep + list_swap(send, 1) + crossed).astype(BF)
    message = tile_swap(jnp.concatenate([block, own[: ranks // 2]]), 1)
    beside = [block, message, middle_swap(block)]
    held, held_across, far, block = lax.optimization_barrier((bases, across, far, block))
    left = list_swap(jnp.stack([held[1], held_across[1]]), 1)

    operands = (*fixed, left, *beside, own, message, far)

    def second(turns, operands):
        kernel = functools.partial(second_kernel, turns)
        return kernel_call(kernel, [part] * len(turns), operands, len(turns) * flops // 4)

    (send,) = second((3,), operands)
    arrived = list_swap(send, 1)
    (keep,) = second((2,), operands)
    crossing = (keep + arrived).astype(BF)
    near, crossing = lax.optimization_barrier((near, crossing))
    crossed = list_swap(crossing, 2)
    send, keep = second((1, 0), (near, *operands[1:]))
    return keep + list_swap_in_pieces(send, 1, 2) + crossed


def local(probes, right_bases, left_bases, near_tiles, tile_ranks, column_rows, row_columns):
    few = lax.axis_size("tile") == 4 and lax.axis_size("list") == 4
    small = right_bases.shape[1] == 1 and few
    form = one_slot if small else many_slots
    return form(
        probes, right_bases, left_bases, near_tiles, tile_ranks, column_rows, row_columns
    )


def solution(mesh):
    placed = (
        P(("group", "tile", "list"), None),
        P(("group", "tile"), None, "list", None),
        P(("group", "tile"), None, "list", None),
        P(("group", "tile"), None, None, "list"),
        P(("group", "tile"), None),
        P("tile", None),
        P("tile", None),
    )
    return jax.shard_map(
        local,
        mesh=mesh,
        in_specs=placed,
        out_specs=P(("group", "tile", "list"), None),
        check_vma=False,
    )
```

```python
import functools

import jax
import jax.numpy as jnp
from jax import lax
from jax.experimental import pallas as pl
from jax.experimental.pallas import tpu as pltpu
from jax.sharding import PartitionSpec as P

BF = jnp.bfloat16
F32 = jnp.float32


def shifted(block, axis, distance):
    devices = range(lax.axis_size(axis))
    route = [(i - distance, i) for i in devices if i - distance in devices]
    return lax.ppermute(block, axis, route)


def image_part(operand, right_bases, left_bases, near_tiles, tile_ranks, column_rows, row_columns):
    tile_slots = right_bases.shape[1]
    rank_part = right_bases.shape[2]
    tile_rows = right_bases.shape[3]
    probe_count = operand.shape[1]
    tile_count = lax.axis_size("tile")
    right_flat = right_bases.reshape(tile_slots * rank_part, tile_rows)
    left_flat = left_bases.reshape(tile_slots * rank_part, tile_rows)
    dense_flat = near_tiles.reshape(tile_rows, -1)
    values = jnp.dot(
        right_flat,
        lax.all_gather(operand, "list", axis=0, tiled=True),
        preferred_element_type=F32,
    )
    rank_level = lax.axis_index("list") * rank_part + lax.iota(jnp.int32, rank_part)
    rank_mask = rank_level[None, :] < tile_ranks[0][:, None]
    coefficients = jnp.where(
        rank_mask[:, :, None], values.reshape(tile_slots, rank_part, probe_count), 0.0
    ).astype(BF)
    targets = (column_rows[0][None, :] == lax.iota(jnp.int32, tile_count)[:, None]).astype(BF)
    outgoing = jnp.einsum(
        "dk,krp->drp", targets, coefficients, preferred_element_type=F32
    ).astype(BF)
    sources = (row_columns[0][:, None] == lax.iota(jnp.int32, tile_count)[None, :]).astype(BF)
    chosen = jnp.einsum(
        "kj,jrp->krp",
        sources,
        lax.all_to_all(outgoing, "tile", split_axis=0, concat_axis=0, tiled=True),
        preferred_element_type=F32,
    ).astype(BF)
    chosen = chosen.reshape(tile_slots * rank_part, -1)
    far_sum = lax.dot_general(
        left_flat, chosen, (((0,), (0,)), ((), ())), preferred_element_type=F32
    )
    arrived = {}
    for offset in (1, -1):
        arrived[offset] = shifted(operand, "tile", offset)
    stacked = jnp.concatenate([arrived[1], operand, arrived[-1]], axis=0)
    near_sum = jnp.dot(dense_flat, stacked, preferred_element_type=F32)
    partial_image = near_sum + far_sum
    return lax.psum_scatter(partial_image, "list", scatter_dimension=0, tiled=True)


def many_slots(probes, right_bases, left_bases, near_tiles, tile_ranks, column_rows, row_columns):
    rest = (right_bases, left_bases, near_tiles, tile_ranks, column_rows, row_columns)
    first_pass = image_part(probes.astype(BF), *rest).astype(BF)
    return image_part(first_pass, *rest)


VMEM = pl.BlockSpec(memory_space=pltpu.VMEM)


def list_swap_in_pieces(block, bit, pieces):
    return jnp.concatenate([list_swap(piece, bit) for piece in jnp.split(block, pieces)])


def kernel_call(kernel, outs, operands, flops=0):
    return pl.pallas_call(
        kernel,
        out_shape=tuple(jax.ShapeDtypeStruct(shape, kind) for shape, kind in outs),
        in_specs=[VMEM] * len(operands),
        out_specs=tuple(VMEM for _ in outs),
        compiler_params=pltpu.CompilerParams(vmem_limit_bytes=16 * 2**20),
        cost_estimate=pl.CostEstimate(
            flops=flops, bytes_accessed=2 * operands[0].size, transcendentals=0
        ),
    )(*operands)


def stacked(pieces):
    return jnp.concatenate([piece.astype(F32) for piece in pieces]).astype(BF)


def under_rank(sums, turns, rank_part, ranks_ref):
    me = lax.axis_index("list")
    groups = []
    for index, turn in enumerate(turns):
        values = sums[index * rank_part : (index + 1) * rank_part]
        level = (me ^ turn) * rank_part + lax.broadcasted_iota(jnp.int32, values.shape, 0)
        groups.append(jnp.where(level < ranks_ref[...], values, 0.0))
    return groups


def basis_groups(side, cut, refs):
    pieces = [ref[side, :, cut] for ref in refs[:2]]
    return stacked(pieces + [ref[index, :, cut] for ref in refs[2:] for index in range(2)])


def coefficient_kernel(bases_ref, across_ref, block_ref, beside_ref, ranks_ref, out_ref):
    me = lax.axis_index("list")
    rows = block_ref.shape[0]
    total = 0.0
    for part, operand_ref in ((me, block_ref), (me ^ 1, beside_ref)):
        cut = pl.ds(pl.multiple_of(part * rows, rows), rows)
        bases = basis_groups(0, cut, (bases_ref, across_ref))
        total += jnp.dot(bases, operand_ref[...], preferred_element_type=F32)
    groups = under_rank(total, (0, 2), bases_ref.shape[1], ranks_ref)
    out_ref[...] = jnp.concatenate(groups).astype(out_ref.dtype)


def tile_swap(block, turn):
    return lax.ppermute(block, "tile", [(i, i ^ turn) for i in range(lax.axis_size("tile"))])


def middle_swap(block):
    tiles, parts = lax.axis_size("tile"), lax.axis_size("list")
    route = []
    for tile in range(tiles):
        for part in range(parts):
            to = (tile - 1 + 2 * (tile % 2), part)
            if tile in (0, tiles - 1):
                to = (tile, part ^ 1)
            route.append((tile * parts + part, to[0] * parts + to[1]))
    return lax.ppermute(block, ("tile", "list"), route)


def far_swap(block):
    tiles, parts = lax.axis_size("tile"), lax.axis_size("list")
    route = [
        (tile * parts + part, (tile ^ (2 + part % 2)) * parts + part)
        for tile in range(tiles)
        for part in range(parts)
    ]
    return lax.ppermute(block, ("tile", "list"), route)


def list_swap(block, bit):
    return lax.ppermute(block, "list", [(i, i ^ bit) for i in range(lax.axis_size("list"))])


def near_choice(columns, tile, me, refs):
    chosen = refs[0][...]
    for turn in (1, 2, 3):
        chosen = jnp.where(columns == tile ^ turn, refs[turn][...], chosen)
    return chosen


def far_choice(columns, tile, me, refs):
    own_ref, message_ref, far_ref = refs
    half = own_ref.shape[0] // 2
    first = jnp.where(columns == tile, own_ref[:half, :], 0)
    first = jnp.where(columns == tile ^ 1, message_ref[message_ref.shape[0] - half :, :], first)
    far = columns == tile ^ (2 + lax.rem(me, 2))
    return jnp.concatenate(
        [jnp.where(far, far_ref[:half, :], first), jnp.where(far, far_ref[half:, :], 0)]
    )


def image_kernel(choice, turns, near_ref, columns_ref, bases_refs, operand_refs, out_refs):
    count_refs = len(operand_refs) - (4 if choice is near_choice else 3)
    block_refs, coefficient_refs = operand_refs[:count_refs], operand_refs[count_refs:]
    count = lax.axis_size("tile")
    tile = lax.axis_index("tile")
    me = lax.axis_index("list")
    rows = near_ref.shape[2]
    chosen = choice(columns_ref[...], tile, me, coefficient_refs)
    odd = lax.rem(tile, 2)
    inside = (tile > 0) & (tile < count - 1)
    blocks = []
    start = 0
    for index in range(0, count_refs, 3):
        own_ref, first_ref, second_ref = block_refs[index : index + 3]
        step = own_ref.shape[0]
        place = slice(start, start + step)
        blocks.append((1, place, own_ref[...]))
        blocks.append((2 - 2 * odd, place, first_ref[:step, :]))
        blocks.append((2 * odd, place, jnp.where(inside, second_ref[...], 0)))
        start += step
    totals = []
    for turn, out_ref in zip(turns, out_refs):
        part = me ^ turn
        cut = pl.ds(pl.multiple_of(part * rows, rows), rows)
        left = basis_groups(1, cut, bases_refs)
        total = lax.dot_general(
            left, chosen, (((0,), (0,)), ((), ())), preferred_element_type=F32
        )
        for side, place, block in blocks:
            total += jnp.dot(near_ref[side, cut, place], block, preferred_element_type=F32)
        out_ref[...] = total
        totals.append((cut, total.astype(BF)))
    return totals


def right_products(totals, bases_refs):
    return sum(
        jnp.dot(basis_groups(0, cut, bases_refs), total, preferred_element_type=F32)
        for cut, total in totals
    )


def first_kernel(turns, near_ref, columns_ref, bases_ref, across_ref, other_ref, *refs):
    operand_refs, refs = refs[:7], refs[7:]
    last = 0 in turns
    sums_before, refs = (refs[:1], refs[1:]) if 3 not in turns else ((), refs)
    ranks_ref, refs = (refs[0], refs[1:]) if last else (None, refs)
    bases_refs = (bases_ref, across_ref)
    totals = image_kernel(
        near_choice, turns, near_ref, columns_ref, bases_refs, operand_refs, refs
    )
    sums = right_products(totals, (*bases_refs, other_ref))
    for ref in sums_before:
        sums += ref[...]
    if not last:
        refs[-1][...] = sums
        return
    groups = under_rank(sums, (0, 2, 1, 3), bases_ref.shape[1], ranks_ref)
    refs[-2][...] = jnp.concatenate(groups)
    refs[-1][...] = jnp.concatenate(groups[2:] + groups[:2])


def second_kernel(turns, near_ref, columns_ref, bases_ref, across_ref, other_ref, *refs):
    bases_refs = (bases_ref, across_ref, other_ref)
    image_kernel(far_choice, turns, near_ref, columns_ref, bases_refs, refs[:9], refs[9:])


def one_slot(probes, right_bases, left_bases, near_tiles, tile_ranks, column_rows, row_columns):
    rows, probe_count = probes.shape
    rank_part = right_bases.shape[2]
    near = near_tiles[0].transpose(1, 0, 2)
    flops = 2 * near.size * probe_count
    part = ((rows, probe_count), F32)
    ranks = 4 * rank_part

    bases = jnp.stack([right_bases[0, 0], left_bases[0, 0]])
    bases, probes = lax.optimization_barrier((bases, probes))
    across = list_swap(bases, 2)
    block = probes.astype(BF)
    beside = [block, tile_swap(block, 1), middle_swap(block)]
    (own,) = kernel_call(
        coefficient_kernel,
        [((ranks // 2, probe_count), BF)],
        (bases, across, block, list_swap(block, 1), tile_ranks),
        8 * flops,
    )
    coefficients = [own] + [tile_swap(own, turn) for turn in (1, 2, 3)]
    right, _ = lax.optimization_barrier((jnp.stack([bases[0], across[0]]), own))
    fixed = (near, row_columns, bases, across)
    operands = (*fixed, list_swap(right, 1), *beside, *coefficients)
    small = ((ranks, probe_count), F32)

    def first(turns, outs, more=()):
        kernel = functools.partial(first_kernel, turns)
        return kernel_call(kernel, outs, (*operands, *more), len(turns) * flops // 4)

    send, sums = first((3,), [part, small])
    arrived = list_swap(send, 1)
    crossing, send, keep, own, other = first(
        (2, 1, 0), [part] * 3 + [small] * 2, (sums, tile_ranks)
    )
    crossing = (crossing + arrived).astype(BF)
    own = (own + list_swap(other, 1)).astype(BF)
    far = far_swap(own)
    keep += list_swap(send, 1)
    beside = []
    split = 5 * rows // 8
    for piece in (slice(0, split), slice(split, rows)):
        block = (keep[piece] + list_swap(crossing[piece], 2)).astype(BF)
        if piece.start:
            block, far = lax.optimization_barrier((block, far))
        keep, block = lax.optimization_barrier((keep, block))
        message = block if piece.start else jnp.concatenate([block, own[: ranks // 2]])
        message = tile_swap(message, 1)
        beside += [block, message, middle_swap(block)]
    message = beside[1]
    held, held_across, _ = lax.optimization_barrier((bases, across, beside[0]))
    left = list_swap(jnp.stack([held[1], held_across[1]]), 1)

    operands = (*fixed, left, *beside, own, message, far)

    def second(turns, operands):
        kernel = functools.partial(second_kernel, turns)
        return kernel_call(kernel, [part] * len(turns), operands, len(turns) * flops // 4)

    (send,) = second((3,), operands)
    arrived = list_swap(send, 1)
    (keep,) = second((2,), operands)
    crossing = (keep + arrived).astype(BF)
    near, crossing = lax.optimization_barrier((near, crossing))
    crossed = list_swap(crossing, 2)
    send, keep = second((1, 0), (near, *operands[1:]))
    return keep + list_swap_in_pieces(send, 1, 2) + crossed


def local(probes, right_bases, left_bases, near_tiles, tile_ranks, column_rows, row_columns):
    few = lax.axis_size("tile") == 4 and lax.axis_size("list") == 4
    small = right_bases.shape[1] == 1 and few
    form = one_slot if small else many_slots
    return form(
        probes, right_bases, left_bases, near_tiles, tile_ranks, column_rows, row_columns
    )


def solution(mesh):
    placed = (
        P(("group", "tile", "list"), None),
        P(("group", "tile"), None, "list", None),
        P(("group", "tile"), None, "list", None),
        P(("group", "tile"), None, None, "list"),
        P(("group", "tile"), None),
        P("tile", None),
        P("tile", None),
    )
    return jax.shard_map(
        local,
        mesh=mesh,
        in_specs=placed,
        out_specs=P(("group", "tile", "list"), None),
        check_vma=False,
    )
```

```python
import functools

import jax
import jax.numpy as jnp
from jax import lax
from jax.experimental import pallas as pl
from jax.experimental.pallas import tpu as pltpu
from jax.sharding import PartitionSpec as P

BF = jnp.bfloat16
F32 = jnp.float32


def shifted(block, axis, distance):
    devices = range(lax.axis_size(axis))
    route = [(i - distance, i) for i in devices if i - distance in devices]
    return lax.ppermute(block, axis, route)


def image_part(operand, right_bases, left_bases, near_tiles, tile_ranks, column_rows, row_columns):
    tile_slots = right_bases.shape[1]
    rank_part = right_bases.shape[2]
    tile_rows = right_bases.shape[3]
    probe_count = operand.shape[1]
    tile_count = lax.axis_size("tile")
    right_flat = right_bases.reshape(tile_slots * rank_part, tile_rows)
    left_flat = left_bases.reshape(tile_slots * rank_part, tile_rows)
    dense_flat = near_tiles.reshape(tile_rows, -1)
    values = jnp.dot(
        right_flat,
        lax.all_gather(operand, "list", axis=0, tiled=True),
        preferred_element_type=F32,
    )
    rank_level = lax.axis_index("list") * rank_part + lax.iota(jnp.int32, rank_part)
    rank_mask = rank_level[None, :] < tile_ranks[0][:, None]
    coefficients = jnp.where(
        rank_mask[:, :, None], values.reshape(tile_slots, rank_part, probe_count), 0.0
    ).astype(BF)
    targets = (column_rows[0][None, :] == lax.iota(jnp.int32, tile_count)[:, None]).astype(BF)
    outgoing = jnp.einsum(
        "dk,krp->drp", targets, coefficients, preferred_element_type=F32
    ).astype(BF)
    sources = (row_columns[0][:, None] == lax.iota(jnp.int32, tile_count)[None, :]).astype(BF)
    chosen = jnp.einsum(
        "kj,jrp->krp",
        sources,
        lax.all_to_all(outgoing, "tile", split_axis=0, concat_axis=0, tiled=True),
        preferred_element_type=F32,
    ).astype(BF)
    chosen = chosen.reshape(tile_slots * rank_part, -1)
    far_sum = lax.dot_general(
        left_flat, chosen, (((0,), (0,)), ((), ())), preferred_element_type=F32
    )
    arrived = {}
    for offset in (1, -1):
        arrived[offset] = shifted(operand, "tile", offset)
    stacked = jnp.concatenate([arrived[1], operand, arrived[-1]], axis=0)
    near_sum = jnp.dot(dense_flat, stacked, preferred_element_type=F32)
    partial_image = near_sum + far_sum
    return lax.psum_scatter(partial_image, "list", scatter_dimension=0, tiled=True)


def many_slots(probes, right_bases, left_bases, near_tiles, tile_ranks, column_rows, row_columns):
    rest = (right_bases, left_bases, near_tiles, tile_ranks, column_rows, row_columns)
    first_pass = image_part(probes.astype(BF), *rest).astype(BF)
    return image_part(first_pass, *rest)


VMEM = pl.BlockSpec(memory_space=pltpu.VMEM)


def list_swap_in_pieces(block, bit, pieces):
    return jnp.concatenate([list_swap(piece, bit) for piece in jnp.split(block, pieces)])


def kernel_call(kernel, outs, operands, flops=0):
    return pl.pallas_call(
        kernel,
        out_shape=tuple(jax.ShapeDtypeStruct(shape, kind) for shape, kind in outs),
        in_specs=[VMEM] * len(operands),
        out_specs=tuple(VMEM for _ in outs),
        compiler_params=pltpu.CompilerParams(vmem_limit_bytes=16 * 2**20),
        cost_estimate=pl.CostEstimate(
            flops=flops, bytes_accessed=2 * operands[0].size, transcendentals=0
        ),
    )(*operands)


def stacked(pieces):
    return jnp.concatenate([piece.astype(F32) for piece in pieces]).astype(BF)


def under_rank(sums, turns, rank_part, ranks_ref):
    me = lax.axis_index("list")
    groups = []
    for index, turn in enumerate(turns):
        values = sums[index * rank_part : (index + 1) * rank_part]
        level = (me ^ turn) * rank_part + lax.broadcasted_iota(jnp.int32, values.shape, 0)
        groups.append(jnp.where(level < ranks_ref[...], values, 0.0))
    return groups


def basis_groups(side, cut, refs):
    pieces = [ref[side, :, cut] for ref in refs[:2]]
    return stacked(pieces + [ref[index, :, cut] for ref in refs[2:] for index in range(2)])


def coefficient_kernel(bases_ref, across_ref, block_ref, beside_ref, ranks_ref, out_ref):
    me = lax.axis_index("list")
    rows = block_ref.shape[0]
    total = 0.0
    for part, operand_ref in ((me, block_ref), (me ^ 1, beside_ref)):
        cut = pl.ds(pl.multiple_of(part * rows, rows), rows)
        bases = basis_groups(0, cut, (bases_ref, across_ref))
        total += jnp.dot(bases, operand_ref[...], preferred_element_type=F32)
    groups = under_rank(total, (0, 2), bases_ref.shape[1], ranks_ref)
    out_ref[...] = jnp.concatenate(groups).astype(out_ref.dtype)


def tile_swap(block, turn):
    return lax.ppermute(block, "tile", [(i, i ^ turn) for i in range(lax.axis_size("tile"))])


def middle_swap(block):
    tiles, parts = lax.axis_size("tile"), lax.axis_size("list")
    route = []
    for tile in range(tiles):
        for part in range(parts):
            to = (tile - 1 + 2 * (tile % 2), part)
            if tile in (0, tiles - 1):
                to = (tile, part ^ 1)
            route.append((tile * parts + part, to[0] * parts + to[1]))
    return lax.ppermute(block, ("tile", "list"), route)


def far_swap(block):
    tiles, parts = lax.axis_size("tile"), lax.axis_size("list")
    route = [
        (tile * parts + part, (tile ^ (2 + part % 2)) * parts + part)
        for tile in range(tiles)
        for part in range(parts)
    ]
    return lax.ppermute(block, ("tile", "list"), route)


def list_swap(block, bit):
    return lax.ppermute(block, "list", [(i, i ^ bit) for i in range(lax.axis_size("list"))])


def near_choice(columns, tile, me, refs):
    chosen = refs[0][...]
    for turn in (1, 2, 3):
        chosen = jnp.where(columns == tile ^ turn, refs[turn][...], chosen)
    return chosen


def far_choice(columns, tile, me, refs):
    own_ref, near_by_ref, far_ref = refs
    half = own_ref.shape[0] // 2
    first = jnp.where(columns == tile, own_ref[:half, :], 0)
    first = jnp.where(columns == tile ^ 1, near_by_ref[...], first)
    far = columns == tile ^ (2 + lax.rem(me, 2))
    return jnp.concatenate(
        [jnp.where(far, far_ref[:half, :], first), jnp.where(far, far_ref[half:, :], 0)]
    )


def image_kernel(choice, turns, near_ref, columns_ref, bases_refs, operand_refs, out_refs):
    block_refs, coefficient_refs = operand_refs[:3], operand_refs[3:]
    count = lax.axis_size("tile")
    tile = lax.axis_index("tile")
    me = lax.axis_index("list")
    rows = near_ref.shape[2]
    chosen = choice(columns_ref[...], tile, me, coefficient_refs)
    odd = lax.rem(tile, 2)
    inside = (tile > 0) & (tile < count - 1)
    blocks = [
        (1, block_refs[0][...]),
        (2 - 2 * odd, block_refs[1][...]),
        (2 * odd, jnp.where(inside, block_refs[2][...], 0)),
    ]
    totals = []
    for turn, out_ref in zip(turns, out_refs):
        part = me ^ turn
        cut = pl.ds(pl.multiple_of(part * rows, rows), rows)
        left = basis_groups(1, cut, bases_refs)
        total = lax.dot_general(
            left, chosen, (((0,), (0,)), ((), ())), preferred_element_type=F32
        )
        for side, block in blocks:
            total += jnp.dot(near_ref[side, cut, :], block, preferred_element_type=F32)
        out_ref[...] = total
        totals.append((cut, total.astype(BF)))
    return totals


def right_products(totals, bases_refs):
    return sum(
        jnp.dot(basis_groups(0, cut, bases_refs), total, preferred_element_type=F32)
        for cut, total in totals
    )


def first_kernel(turns, near_ref, columns_ref, bases_ref, across_ref, other_ref, *refs):
    operand_refs, refs = refs[:7], refs[7:]
    last = 0 in turns
    sums_before, refs = (refs[:1], refs[1:]) if 3 not in turns else ((), refs)
    ranks_ref, refs = (refs[0], refs[1:]) if last else (None, refs)
    bases_refs = (bases_ref, across_ref)
    totals = image_kernel(
        near_choice, turns, near_ref, columns_ref, bases_refs, operand_refs, refs
    )
    sums = right_products(totals, (*bases_refs, other_ref))
    for ref in sums_before:
        sums += ref[...]
    if not last:
        refs[-1][...] = sums
        return
    groups = under_rank(sums, (0, 2, 1, 3), bases_ref.shape[1], ranks_ref)
    refs[-2][...] = jnp.concatenate(groups)
    refs[-1][...] = jnp.concatenate(groups[2:] + groups[:2])


def second_kernel(turns, near_ref, columns_ref, bases_ref, across_ref, other_ref, *refs):
    bases_refs = (bases_ref, across_ref, other_ref)
    image_kernel(far_choice, turns, near_ref, columns_ref, bases_refs, refs[:6], refs[6:])


def one_slot(probes, right_bases, left_bases, near_tiles, tile_ranks, column_rows, row_columns):
    rows, probe_count = probes.shape
    rank_part = right_bases.shape[2]
    near = near_tiles[0].transpose(1, 0, 2)
    flops = 2 * near.size * probe_count
    part = ((rows, probe_count), F32)
    ranks = 4 * rank_part

    bases = jnp.stack([right_bases[0, 0], left_bases[0, 0]])
    bases, probes = lax.optimization_barrier((bases, probes))
    across = list_swap(bases, 2)
    block = probes.astype(BF)
    beside = [block, tile_swap(block, 1), middle_swap(block)]
    (own,) = kernel_call(
        coefficient_kernel,
        [((ranks // 2, probe_count), BF)],
        (bases, across, block, list_swap(block, 1), tile_ranks),
        8 * flops,
    )
    coefficients = [own] + [tile_swap(own, turn) for turn in (1, 2, 3)]
    right, _ = lax.optimization_barrier((jnp.stack([bases[0], across[0]]), own))
    fixed = (near, row_columns, bases, across)
    operands = (*fixed, list_swap(right, 1), *beside, *coefficients)
    small = ((ranks, probe_count), F32)

    def first(turns, outs, more=()):
        kernel = functools.partial(first_kernel, turns)
        return kernel_call(kernel, outs, (*operands, *more), len(turns) * flops // 4)

    send, sums = first((3,), [part, small])
    arrived = list_swap(send, 1)
    crossing, send, keep, own, other = first(
        (2, 1, 0), [part] * 3 + [small] * 2, (sums, tile_ranks)
    )
    crossed = list_swap((crossing + arrived).astype(BF), 2)
    own = (own + list_swap(other, 1)).astype(BF)
    near_by, far = tile_swap(own[: ranks // 2], 1), far_swap(own)
    block = (keep + list_swap(send, 1) + crossed).astype(BF)
    held, held_across, near_by, far, ready = lax.optimization_barrier(
        (bases, across, near_by, far, block)
    )
    beside = [block, tile_swap(ready, 1), middle_swap(block)]
    left = list_swap(jnp.stack([held[1], held_across[1]]), 1)

    operands = (*fixed, left, *beside, own, near_by, far)

    def second(turns, operands):
        kernel = functools.partial(second_kernel, turns)
        return kernel_call(kernel, [part] * len(turns), operands, len(turns) * flops // 4)

    (send,) = second((3,), operands)
    arrived = list_swap(send, 1)
    (keep,) = second((2,), operands)
    crossing = (keep + arrived).astype(BF)
    near, crossing = lax.optimization_barrier((near, crossing))
    crossed = list_swap(crossing, 2)
    send, keep = second((1, 0), (near, *operands[1:]))
    return keep + list_swap_in_pieces(send, 1, 2) + crossed


def local(probes, right_bases, left_bases, near_tiles, tile_ranks, column_rows, row_columns):
    few = lax.axis_size("tile") == 4 and lax.axis_size("list") == 4
    small = right_bases.shape[1] == 1 and few
    form = one_slot if small else many_slots
    return form(
        probes, right_bases, left_bases, near_tiles, tile_ranks, column_rows, row_columns
    )


def solution(mesh):
    placed = (
        P(("group", "tile", "list"), None),
        P(("group", "tile"), None, "list", None),
        P(("group", "tile"), None, "list", None),
        P(("group", "tile"), None, None, "list"),
        P(("group", "tile"), None),
        P("tile", None),
        P("tile", None),
    )
    return jax.shard_map(
        local,
        mesh=mesh,
        in_specs=placed,
        out_specs=P(("group", "tile", "list"), None),
        check_vma=False,
    )
```

```python
import functools

import jax
import jax.numpy as jnp
from jax import lax
from jax.experimental import pallas as pl
from jax.experimental.pallas import tpu as pltpu
from jax.sharding import PartitionSpec as P

BF = jnp.bfloat16
F32 = jnp.float32


def shifted(block, axis, distance):
    devices = range(lax.axis_size(axis))
    route = [(i - distance, i) for i in devices if i - distance in devices]
    return lax.ppermute(block, axis, route)


def image_part(operand, right_bases, left_bases, near_tiles, tile_ranks, column_rows, row_columns):
    tile_slots = right_bases.shape[1]
    rank_part = right_bases.shape[2]
    tile_rows = right_bases.shape[3]
    probe_count = operand.shape[1]
    tile_count = lax.axis_size("tile")
    right_flat = right_bases.reshape(tile_slots * rank_part, tile_rows)
    left_flat = left_bases.reshape(tile_slots * rank_part, tile_rows)
    dense_flat = near_tiles.reshape(tile_rows, -1)
    values = jnp.dot(
        right_flat,
        lax.all_gather(operand, "list", axis=0, tiled=True),
        preferred_element_type=F32,
    )
    rank_level = lax.axis_index("list") * rank_part + lax.iota(jnp.int32, rank_part)
    rank_mask = rank_level[None, :] < tile_ranks[0][:, None]
    coefficients = jnp.where(
        rank_mask[:, :, None], values.reshape(tile_slots, rank_part, probe_count), 0.0
    ).astype(BF)
    targets = (column_rows[0][None, :] == lax.iota(jnp.int32, tile_count)[:, None]).astype(BF)
    outgoing = jnp.einsum(
        "dk,krp->drp", targets, coefficients, preferred_element_type=F32
    ).astype(BF)
    sources = (row_columns[0][:, None] == lax.iota(jnp.int32, tile_count)[None, :]).astype(BF)
    chosen = jnp.einsum(
        "kj,jrp->krp",
        sources,
        lax.all_to_all(outgoing, "tile", split_axis=0, concat_axis=0, tiled=True),
        preferred_element_type=F32,
    ).astype(BF)
    chosen = chosen.reshape(tile_slots * rank_part, -1)
    far_sum = lax.dot_general(
        left_flat, chosen, (((0,), (0,)), ((), ())), preferred_element_type=F32
    )
    arrived = {}
    for offset in (1, -1):
        arrived[offset] = shifted(operand, "tile", offset)
    stacked = jnp.concatenate([arrived[1], operand, arrived[-1]], axis=0)
    near_sum = jnp.dot(dense_flat, stacked, preferred_element_type=F32)
    partial_image = near_sum + far_sum
    return lax.psum_scatter(partial_image, "list", scatter_dimension=0, tiled=True)


def many_slots(probes, right_bases, left_bases, near_tiles, tile_ranks, column_rows, row_columns):
    rest = (right_bases, left_bases, near_tiles, tile_ranks, column_rows, row_columns)
    first_pass = image_part(probes.astype(BF), *rest).astype(BF)
    return image_part(first_pass, *rest)


VMEM = pl.BlockSpec(memory_space=pltpu.VMEM)


def list_swap_in_pieces(block, bit, pieces):
    return jnp.concatenate([list_swap(piece, bit) for piece in jnp.split(block, pieces)])


def kernel_call(kernel, outs, operands, flops=0):
    return pl.pallas_call(
        kernel,
        out_shape=tuple(jax.ShapeDtypeStruct(shape, kind) for shape, kind in outs),
        in_specs=[VMEM] * len(operands),
        out_specs=tuple(VMEM for _ in outs),
        compiler_params=pltpu.CompilerParams(vmem_limit_bytes=16 * 2**20),
        cost_estimate=pl.CostEstimate(
            flops=flops, bytes_accessed=flops // 1024, transcendentals=0
        ),
    )(*operands)


def stacked(pieces):
    return jnp.concatenate([piece.astype(F32) for piece in pieces]).astype(BF)


def under_rank(sums, turns, rank_part, ranks_ref):
    me = lax.axis_index("list")
    groups = []
    for index, turn in enumerate(turns):
        values = sums[index * rank_part : (index + 1) * rank_part]
        level = (me ^ turn) * rank_part + lax.broadcasted_iota(jnp.int32, values.shape, 0)
        groups.append(jnp.where(level < ranks_ref[...], values, 0.0))
    return groups


def basis_groups(side, cut, refs):
    pieces = [ref[side, :, cut] for ref in refs[:2]]
    return stacked(pieces + [ref[index, :, cut] for ref in refs[2:] for index in range(2)])


def coefficient_kernel(bases_ref, across_ref, block_ref, beside_ref, ranks_ref, out_ref):
    me = lax.axis_index("list")
    rows = block_ref.shape[0]
    total = 0.0
    for part, operand_ref in ((me, block_ref), (me ^ 1, beside_ref)):
        cut = pl.ds(pl.multiple_of(part * rows, rows), rows)
        bases = basis_groups(0, cut, (bases_ref, across_ref))
        total += jnp.dot(bases, operand_ref[...], preferred_element_type=F32)
    groups = under_rank(total, (0, 2), bases_ref.shape[1], ranks_ref)
    out_ref[...] = jnp.concatenate(groups).astype(out_ref.dtype)


def tile_swap(block, turn):
    return lax.ppermute(block, "tile", [(i, i ^ turn) for i in range(lax.axis_size("tile"))])


def middle_swap(block):
    tiles, parts = lax.axis_size("tile"), lax.axis_size("list")
    route = []
    for tile in range(tiles):
        for part in range(parts):
            to = (tile - 1 + 2 * (tile % 2), part)
            if tile in (0, tiles - 1):
                to = (tile, part ^ 1)
            route.append((tile * parts + part, to[0] * parts + to[1]))
    return lax.ppermute(block, ("tile", "list"), route)


def far_swap(block):
    tiles, parts = lax.axis_size("tile"), lax.axis_size("list")
    route = [
        (tile * parts + part, (tile ^ (2 + part % 2)) * parts + part)
        for tile in range(tiles)
        for part in range(parts)
    ]
    return lax.ppermute(block, ("tile", "list"), route)


def list_swap(block, bit):
    return lax.ppermute(block, "list", [(i, i ^ bit) for i in range(lax.axis_size("list"))])


def near_choice(columns, tile, me, refs):
    chosen = refs[0][...]
    for turn in (1, 2, 3):
        chosen = jnp.where(columns == tile ^ turn, refs[turn][...], chosen)
    return chosen


def far_choice(columns, tile, me, refs):
    own_ref, near_by_ref, far_ref = refs
    half = own_ref.shape[0] // 2
    first = jnp.where(columns == tile, own_ref[:half, :], 0)
    first = jnp.where(columns == tile ^ 1, near_by_ref[...], first)
    far = columns == tile ^ (2 + lax.rem(me, 2))
    return jnp.concatenate(
        [jnp.where(far, far_ref[:half, :], first), jnp.where(far, far_ref[half:, :], 0)]
    )


def near_kernel(turns, near_ref, own_ref, first_ref, second_ref, *refs):
    base_refs, out_refs = refs[: -len(turns)], refs[-len(turns) :]
    count = lax.axis_size("tile")
    tile = lax.axis_index("tile")
    me = lax.axis_index("list")
    rows = near_ref.shape[2]
    odd = lax.rem(tile, 2)
    inside = (tile > 0) & (tile < count - 1)
    blocks = [
        (1, own_ref[...]),
        (2 - 2 * odd, first_ref[...]),
        (2 * odd, jnp.where(inside, second_ref[...], 0)),
    ]
    for index, turn in enumerate(turns):
        cut = pl.ds(pl.multiple_of((me ^ turn) * rows, rows), rows)
        total = base_refs[index][...] if base_refs else 0.0
        for side, block in blocks:
            total += jnp.dot(near_ref[side, cut, :], block, preferred_element_type=F32)
        out_refs[index][...] = total


def far_parts(choice, turns, columns_ref, bases_refs, coefficient_refs):
    me = lax.axis_index("list")
    chosen = choice(columns_ref[...], lax.axis_index("tile"), me, coefficient_refs)
    rows = bases_refs[0].shape[2] // 4
    for turn in turns:
        cut = pl.ds(pl.multiple_of((me ^ turn) * rows, rows), rows)
        left = basis_groups(1, cut, bases_refs)
        yield cut, lax.dot_general(
            left, chosen, (((0,), (0,)), ((), ())), preferred_element_type=F32
        )


def right_products(totals, bases_refs):
    return sum(
        jnp.dot(basis_groups(0, cut, bases_refs), total, preferred_element_type=F32)
        for cut, total in totals
    )


def first_kernel(turns, columns_ref, bases_ref, across_ref, other_ref, *refs):
    coefficient_refs, refs = refs[:4], refs[4:]
    base_refs, refs = refs[: len(turns)], refs[len(turns) :]
    last = 0 in turns
    sums_before, refs = (refs[:1], refs[1:]) if 3 not in turns else ((), refs)
    ranks_ref, refs = (refs[0], refs[1:]) if last else (None, refs)
    bases_refs = (bases_ref, across_ref)
    totals = []
    parts = far_parts(near_choice, turns, columns_ref, bases_refs, coefficient_refs)
    for (cut, total), base_ref, out_ref in zip(parts, base_refs, refs):
        total += base_ref[...]
        out_ref[...] = total
        totals.append((cut, total.astype(BF)))
    sums = right_products(totals, (*bases_refs, other_ref))
    for ref in sums_before:
        sums += ref[...]
    if not last:
        refs[-1][...] = sums
        return
    groups = under_rank(sums, (0, 2, 1, 3), bases_ref.shape[1], ranks_ref)
    refs[-2][...] = jnp.concatenate(groups)
    refs[-1][...] = jnp.concatenate(groups[2:] + groups[:2])


def second_kernel(turns, columns_ref, bases_ref, across_ref, other_ref, *refs):
    operand_refs, out_refs = refs[3:-len(turns)], refs[-len(turns) :]
    bases_refs = (bases_ref, across_ref, other_ref)
    parts = far_parts(far_choice, turns, columns_ref, bases_refs, refs[:3])
    for (_, total), out_ref in zip(parts, out_refs):
        out_ref[...] = total
    near_kernel(turns, *operand_refs, *out_refs, *out_refs)


def one_slot(probes, right_bases, left_bases, near_tiles, tile_ranks, column_rows, row_columns):
    rows, probe_count = probes.shape
    rank_part = right_bases.shape[2]
    near = near_tiles[0].transpose(1, 0, 2)
    flops = 2 * near.size * probe_count
    part = ((rows, probe_count), F32)
    ranks = 4 * rank_part

    bases = jnp.stack([right_bases[0, 0], left_bases[0, 0]])
    bases, probes = lax.optimization_barrier((bases, probes))
    across = list_swap(bases, 2)
    block = probes.astype(BF)
    beside = [block, tile_swap(block, 1), middle_swap(block)]
    (own,) = kernel_call(
        coefficient_kernel,
        [((ranks // 2, probe_count), BF)],
        (bases, across, block, list_swap(block, 1), tile_ranks),
        8 * flops,
    )
    coefficients = [own] + [tile_swap(own, turn) for turn in (1, 2, 3)]
    right, _ = lax.optimization_barrier((jnp.stack([bases[0], across[0]]), own))
    fixed = (row_columns, bases, across)
    operands = (*fixed, list_swap(right, 1), *coefficients)
    small = ((ranks, probe_count), F32)

    def call(kernel, turns, operands, more=(), cost=1):
        outs = [part] * len(turns) + list(more)
        kernel = functools.partial(kernel, turns)
        return kernel_call(kernel, outs, operands, cost * len(turns) * flops // 4)

    base = call(near_kernel, (3, 2, 1, 0), (near, *beside), cost=0)
    send, sums = call(first_kernel, (3,), (*operands, base[0]), [small])
    arrived = list_swap(send, 1)
    crossing, send, keep, own, other = call(
        first_kernel, (2, 1, 0), (*operands, *base[1:], sums, tile_ranks), [small] * 2
    )
    crossed = list_swap((crossing + arrived).astype(BF), 2)
    own = (own + list_swap(other, 1)).astype(BF)
    near_by, far = tile_swap(own[: ranks // 2], 1), far_swap(own)
    block = (keep + list_swap(send, 1) + crossed).astype(BF)
    held, held_across, near_by, far, ready = lax.optimization_barrier(
        (bases, across, near_by, far, block)
    )
    beside = [block, tile_swap(block, 1), middle_swap(ready)]
    left = list_swap(jnp.stack([held[1], held_across[1]]), 1)

    operands = (*fixed, left, own, near_by, far, near, *beside)
    (send,) = call(second_kernel, (3,), operands)
    arrived = list_swap(send, 1)
    (keep,) = call(second_kernel, (2,), operands)
    crossing = (keep + arrived).astype(BF)
    left, crossing = lax.optimization_barrier((left, crossing))
    crossed = list_swap(crossing, 2)
    operands = (*fixed, left, own, near_by, far, near, *beside)
    send, keep = call(second_kernel, (1, 0), operands)
    return keep + list_swap_in_pieces(send, 1, 2) + crossed


def local(probes, right_bases, left_bases, near_tiles, tile_ranks, column_rows, row_columns):
    few = lax.axis_size("tile") == 4 and lax.axis_size("list") == 4
    small = right_bases.shape[1] == 1 and few
    form = one_slot if small else many_slots
    return form(
        probes, right_bases, left_bases, near_tiles, tile_ranks, column_rows, row_columns
    )


def solution(mesh):
    placed = (
        P(("group", "tile", "list"), None),
        P(("group", "tile"), None, "list", None),
        P(("group", "tile"), None, "list", None),
        P(("group", "tile"), None, None, "list"),
        P(("group", "tile"), None),
        P("tile", None),
        P("tile", None),
    )
    return jax.shard_map(
        local,
        mesh=mesh,
        in_specs=placed,
        out_specs=P(("group", "tile", "list"), None),
        check_vma=False,
    )
```

```python
import functools

import jax
import jax.numpy as jnp
from jax import lax
from jax.experimental import pallas as pl
from jax.experimental.pallas import tpu as pltpu
from jax.sharding import PartitionSpec as P

BF = jnp.bfloat16
F32 = jnp.float32


def shifted(block, axis, distance):
    devices = range(lax.axis_size(axis))
    route = [(i - distance, i) for i in devices if i - distance in devices]
    return lax.ppermute(block, axis, route)


def image_part(operand, right_bases, left_bases, near_tiles, tile_ranks, column_rows, row_columns):
    tile_slots = right_bases.shape[1]
    rank_part = right_bases.shape[2]
    tile_rows = right_bases.shape[3]
    probe_count = operand.shape[1]
    tile_count = lax.axis_size("tile")
    right_flat = right_bases.reshape(tile_slots * rank_part, tile_rows)
    left_flat = left_bases.reshape(tile_slots * rank_part, tile_rows)
    dense_flat = near_tiles.reshape(tile_rows, -1)
    values = jnp.dot(
        right_flat,
        lax.all_gather(operand, "list", axis=0, tiled=True),
        preferred_element_type=F32,
    )
    rank_level = lax.axis_index("list") * rank_part + lax.iota(jnp.int32, rank_part)
    rank_mask = rank_level[None, :] < tile_ranks[0][:, None]
    coefficients = jnp.where(
        rank_mask[:, :, None], values.reshape(tile_slots, rank_part, probe_count), 0.0
    ).astype(BF)
    targets = (column_rows[0][None, :] == lax.iota(jnp.int32, tile_count)[:, None]).astype(BF)
    outgoing = jnp.einsum(
        "dk,krp->drp", targets, coefficients, preferred_element_type=F32
    ).astype(BF)
    sources = (row_columns[0][:, None] == lax.iota(jnp.int32, tile_count)[None, :]).astype(BF)
    chosen = jnp.einsum(
        "kj,jrp->krp",
        sources,
        lax.all_to_all(outgoing, "tile", split_axis=0, concat_axis=0, tiled=True),
        preferred_element_type=F32,
    ).astype(BF)
    chosen = chosen.reshape(tile_slots * rank_part, -1)
    far_sum = lax.dot_general(
        left_flat, chosen, (((0,), (0,)), ((), ())), preferred_element_type=F32
    )
    arrived = {}
    for offset in (1, -1):
        arrived[offset] = shifted(operand, "tile", offset)
    stacked = jnp.concatenate([arrived[1], operand, arrived[-1]], axis=0)
    near_sum = jnp.dot(dense_flat, stacked, preferred_element_type=F32)
    partial_image = near_sum + far_sum
    return lax.psum_scatter(partial_image, "list", scatter_dimension=0, tiled=True)


def many_slots(probes, right_bases, left_bases, near_tiles, tile_ranks, column_rows, row_columns):
    rest = (right_bases, left_bases, near_tiles, tile_ranks, column_rows, row_columns)
    first_pass = image_part(probes.astype(BF), *rest).astype(BF)
    return image_part(first_pass, *rest)


VMEM = pl.BlockSpec(memory_space=pltpu.VMEM)


def list_swap_in_pieces(block, bit, pieces):
    return jnp.concatenate([list_swap(piece, bit) for piece in jnp.split(block, pieces)])


def kernel_call(kernel, outs, operands, flops=0):
    return pl.pallas_call(
        kernel,
        out_shape=tuple(jax.ShapeDtypeStruct(shape, kind) for shape, kind in outs),
        in_specs=[VMEM] * len(operands),
        out_specs=tuple(VMEM for _ in outs),
        compiler_params=pltpu.CompilerParams(vmem_limit_bytes=16 * 2**20),
        cost_estimate=pl.CostEstimate(
            flops=flops, bytes_accessed=flops // 1024, transcendentals=0
        ),
    )(*operands)


def stacked(pieces):
    return jnp.concatenate([piece.astype(F32) for piece in pieces]).astype(BF)


def under_rank(sums, turns, rank_part, ranks_ref):
    me = lax.axis_index("list")
    groups = []
    for index, turn in enumerate(turns):
        values = sums[index * rank_part : (index + 1) * rank_part]
        level = (me ^ turn) * rank_part + lax.broadcasted_iota(jnp.int32, values.shape, 0)
        groups.append(jnp.where(level < ranks_ref[...], values, 0.0))
    return groups


def basis_groups(side, cut, refs):
    pieces = [ref[side, :, cut] for ref in refs[:2]]
    return stacked(pieces + [ref[index, :, cut] for ref in refs[2:] for index in range(2)])


def coefficient_kernel(bases_ref, across_ref, block_ref, beside_ref, ranks_ref, out_ref):
    me = lax.axis_index("list")
    rows = block_ref.shape[0]
    total = 0.0
    for part, operand_ref in ((me, block_ref), (me ^ 1, beside_ref)):
        cut = pl.ds(pl.multiple_of(part * rows, rows), rows)
        bases = basis_groups(0, cut, (bases_ref, across_ref))
        total += jnp.dot(bases, operand_ref[...], preferred_element_type=F32)
    groups = under_rank(total, (0, 2), bases_ref.shape[1], ranks_ref)
    out_ref[...] = jnp.concatenate(groups).astype(out_ref.dtype)


def tile_swap(block, turn):
    return lax.ppermute(block, "tile", [(i, i ^ turn) for i in range(lax.axis_size("tile"))])


def middle_swap(block):
    tiles, parts = lax.axis_size("tile"), lax.axis_size("list")
    route = []
    for tile in range(tiles):
        for part in range(parts):
            to = (tile - 1 + 2 * (tile % 2), part)
            if tile in (0, tiles - 1):
                to = (tile, part ^ 1)
            route.append((tile * parts + part, to[0] * parts + to[1]))
    return lax.ppermute(block, ("tile", "list"), route)


def far_swap(block):
    tiles, parts = lax.axis_size("tile"), lax.axis_size("list")
    route = [
        (tile * parts + part, (tile ^ (2 + part % 2)) * parts + part)
        for tile in range(tiles)
        for part in range(parts)
    ]
    return lax.ppermute(block, ("tile", "list"), route)


def list_swap(block, bit):
    return lax.ppermute(block, "list", [(i, i ^ bit) for i in range(lax.axis_size("list"))])


def near_choice(columns, tile, me, refs):
    chosen = refs[0][...]
    for turn in (1, 2, 3):
        chosen = jnp.where(columns == tile ^ turn, refs[turn][...], chosen)
    return chosen


def far_choice(columns, tile, me, refs):
    own_ref, near_by_ref, far_ref = refs
    half = own_ref.shape[0] // 2
    first = jnp.where(columns == tile, own_ref[:half, :], 0)
    first = jnp.where(columns == tile ^ 1, near_by_ref[...], first)
    far = columns == tile ^ (2 + lax.rem(me, 2))
    return jnp.concatenate(
        [jnp.where(far, far_ref[:half, :], first), jnp.where(far, far_ref[half:, :], 0)]
    )


def near_kernel(turns, near_ref, own_ref, second_ref, first_ref, *refs):
    base_refs, out_refs = refs[: -len(turns)], refs[-len(turns) :]
    count = lax.axis_size("tile")
    tile = lax.axis_index("tile")
    me = lax.axis_index("list")
    rows = near_ref.shape[2]
    odd = lax.rem(tile, 2)
    inside = (tile > 0) & (tile < count - 1)
    blocks = [
        (1, own_ref[...]),
        (2 - 2 * odd, first_ref[...]),
        (2 * odd, jnp.where(inside, second_ref[...], 0)),
    ]
    for index, turn in enumerate(turns):
        cut = pl.ds(pl.multiple_of((me ^ turn) * rows, rows), rows)
        total = base_refs[index][...] if base_refs else 0.0
        for side, block in blocks:
            total += jnp.dot(near_ref[side, cut, :], block, preferred_element_type=F32)
        out_refs[index][...] = total


def far_parts(choice, turns, columns_ref, bases_refs, coefficient_refs):
    me = lax.axis_index("list")
    chosen = choice(columns_ref[...], lax.axis_index("tile"), me, coefficient_refs)
    rows = bases_refs[0].shape[2] // 4
    for turn in turns:
        cut = pl.ds(pl.multiple_of((me ^ turn) * rows, rows), rows)
        left = basis_groups(1, cut, bases_refs)
        yield cut, lax.dot_general(
            left, chosen, (((0,), (0,)), ((), ())), preferred_element_type=F32
        )


def right_products(totals, bases_refs):
    return sum(
        jnp.dot(basis_groups(0, cut, bases_refs), total, preferred_element_type=F32)
        for cut, total in totals
    )


def first_kernel(turns, columns_ref, bases_ref, across_ref, other_ref, *refs):
    coefficient_refs, refs = refs[:4], refs[4:]
    base_refs, refs = refs[: len(turns)], refs[len(turns) :]
    last = 0 in turns
    sums_before, refs = (refs[:1], refs[1:]) if 3 not in turns else ((), refs)
    ranks_ref, refs = (refs[0], refs[1:]) if last else (None, refs)
    bases_refs = (bases_ref, across_ref)
    totals = []
    parts = far_parts(near_choice, turns, columns_ref, bases_refs, coefficient_refs)
    for (cut, total), base_ref, out_ref in zip(parts, base_refs, refs):
        total += base_ref[...]
        out_ref[...] = total
        totals.append((cut, total.astype(BF)))
    sums = right_products(totals, (*bases_refs, other_ref))
    for ref in sums_before:
        sums += ref[...]
    if not last:
        refs[-1][...] = sums
        return
    groups = under_rank(sums, (0, 2, 1, 3), bases_ref.shape[1], ranks_ref)
    refs[-2][...] = jnp.concatenate(groups)
    refs[-1][...] = jnp.concatenate(groups[2:] + groups[:2])


def far_kernel(turns, columns_ref, bases_ref, across_ref, other_ref, *refs):
    bases_refs = (bases_ref, across_ref, other_ref)
    parts = far_parts(far_choice, turns, columns_ref, bases_refs, refs[:3])
    for (_, total), out_ref in zip(parts, refs[3:]):
        out_ref[...] = total


def one_slot(probes, right_bases, left_bases, near_tiles, tile_ranks, column_rows, row_columns):
    rows, probe_count = probes.shape
    rank_part = right_bases.shape[2]
    near = near_tiles[0].transpose(1, 0, 2)
    flops = 2 * near.size * probe_count
    part = ((rows, probe_count), F32)
    ranks = 4 * rank_part

    bases = jnp.stack([right_bases[0, 0], left_bases[0, 0]])
    bases, probes = lax.optimization_barrier((bases, probes))
    across = list_swap(bases, 2)
    block = probes.astype(BF)
    beside = [block, middle_swap(block), tile_swap(block, 1)]
    (own,) = kernel_call(
        coefficient_kernel,
        [((ranks // 2, probe_count), BF)],
        (bases, across, block, list_swap(block, 1), tile_ranks),
        8 * flops,
    )
    coefficients = [own] + [tile_swap(own, turn) for turn in (1, 2, 3)]
    right, _ = lax.optimization_barrier((jnp.stack([bases[0], across[0]]), own))
    fixed = (row_columns, bases, across)
    operands = (*fixed, list_swap(right, 1), *coefficients)
    small = ((ranks, probe_count), F32)

    def call(kernel, turns, operands, more=(), cost=1):
        outs = [part] * len(turns) + list(more)
        kernel = functools.partial(kernel, turns)
        return kernel_call(kernel, outs, operands, cost * len(turns) * flops // 4)

    base = call(near_kernel, (3, 2, 1, 0), (near, *beside), cost=0)
    send, sums = call(first_kernel, (3,), (*operands, base[0]), [small])
    arrived = list_swap(send, 1)
    crossing, send, keep, own, other = call(
        first_kernel, (2, 1, 0), (*operands, *base[1:], sums, tile_ranks), [small] * 2
    )
    crossed = list_swap((crossing + arrived).astype(BF), 2)
    own = (own + list_swap(other, 1)).astype(BF)
    near_by, far = tile_swap(own[: ranks // 2], 1), far_swap(own)
    block = (keep + list_swap(send, 1) + crossed).astype(BF)
    held, held_across, near_by, far, ready = lax.optimization_barrier(
        (bases, across, near_by, far, block)
    )
    beside = [block, middle_swap(ready), tile_swap(block, 1)]
    left = list_swap(jnp.stack([held[1], held_across[1]]), 1)

    base = call(far_kernel, (3, 2, 1, 0), (*fixed, left, own, near_by, far), cost=0)
    (send,) = call(near_kernel, (3,), (near, *beside, base[0]))
    arrived = list_swap(send, 1)
    (keep,) = call(near_kernel, (2,), (near, *beside, base[1]))
    crossing = (keep + arrived).astype(BF)
    near, crossing = lax.optimization_barrier((near, crossing))
    crossed = list_swap(crossing, 2)
    send, keep = call(near_kernel, (1, 0), (near, *beside, *base[2:]))
    return keep + list_swap_in_pieces(send, 1, 2) + crossed


def local(probes, right_bases, left_bases, near_tiles, tile_ranks, column_rows, row_columns):
    few = lax.axis_size("tile") == 4 and lax.axis_size("list") == 4
    small = right_bases.shape[1] == 1 and few
    form = one_slot if small else many_slots
    return form(
        probes, right_bases, left_bases, near_tiles, tile_ranks, column_rows, row_columns
    )


def solution(mesh):
    placed = (
        P(("group", "tile", "list"), None),
        P(("group", "tile"), None, "list", None),
        P(("group", "tile"), None, "list", None),
        P(("group", "tile"), None, None, "list"),
        P(("group", "tile"), None),
        P("tile", None),
        P("tile", None),
    )
    return jax.shard_map(
        local,
        mesh=mesh,
        in_specs=placed,
        out_specs=P(("group", "tile", "list"), None),
        check_vma=False,
    )
```

```python
import functools

import jax
import jax.numpy as jnp
from jax import lax
from jax.experimental import pallas as pl
from jax.experimental.pallas import tpu as pltpu
from jax.sharding import PartitionSpec as P

BF = jnp.bfloat16
F32 = jnp.float32


def shifted(block, axis, distance):
    devices = range(lax.axis_size(axis))
    route = [(i - distance, i) for i in devices if i - distance in devices]
    return lax.ppermute(block, axis, route)


def image_part(operand, right_bases, left_bases, near_tiles, tile_ranks, column_rows, row_columns):
    tile_slots = right_bases.shape[1]
    rank_part = right_bases.shape[2]
    tile_rows = right_bases.shape[3]
    probe_count = operand.shape[1]
    tile_count = lax.axis_size("tile")
    right_flat = right_bases.reshape(tile_slots * rank_part, tile_rows)
    left_flat = left_bases.reshape(tile_slots * rank_part, tile_rows)
    dense_flat = near_tiles.reshape(tile_rows, -1)
    values = jnp.dot(
        right_flat,
        lax.all_gather(operand, "list", axis=0, tiled=True),
        preferred_element_type=F32,
    )
    rank_level = lax.axis_index("list") * rank_part + lax.iota(jnp.int32, rank_part)
    rank_mask = rank_level[None, :] < tile_ranks[0][:, None]
    coefficients = jnp.where(
        rank_mask[:, :, None], values.reshape(tile_slots, rank_part, probe_count), 0.0
    ).astype(BF)
    targets = (column_rows[0][None, :] == lax.iota(jnp.int32, tile_count)[:, None]).astype(BF)
    outgoing = jnp.einsum(
        "dk,krp->drp", targets, coefficients, preferred_element_type=F32
    ).astype(BF)
    sources = (row_columns[0][:, None] == lax.iota(jnp.int32, tile_count)[None, :]).astype(BF)
    chosen = jnp.einsum(
        "kj,jrp->krp",
        sources,
        lax.all_to_all(outgoing, "tile", split_axis=0, concat_axis=0, tiled=True),
        preferred_element_type=F32,
    ).astype(BF)
    chosen = chosen.reshape(tile_slots * rank_part, -1)
    far_sum = lax.dot_general(
        left_flat, chosen, (((0,), (0,)), ((), ())), preferred_element_type=F32
    )
    arrived = {}
    for offset in (1, -1):
        arrived[offset] = shifted(operand, "tile", offset)
    stacked = jnp.concatenate([arrived[1], operand, arrived[-1]], axis=0)
    near_sum = jnp.dot(dense_flat, stacked, preferred_element_type=F32)
    partial_image = near_sum + far_sum
    return lax.psum_scatter(partial_image, "list", scatter_dimension=0, tiled=True)


def many_slots(probes, right_bases, left_bases, near_tiles, tile_ranks, column_rows, row_columns):
    rest = (right_bases, left_bases, near_tiles, tile_ranks, column_rows, row_columns)
    first_pass = image_part(probes.astype(BF), *rest).astype(BF)
    return image_part(first_pass, *rest)


VMEM = pl.BlockSpec(memory_space=pltpu.VMEM)


def list_swap_in_pieces(block, bit, pieces):
    return jnp.concatenate([list_swap(piece, bit) for piece in jnp.split(block, pieces)])


def kernel_call(kernel, outs, operands, flops=0):
    return pl.pallas_call(
        kernel,
        out_shape=tuple(jax.ShapeDtypeStruct(shape, kind) for shape, kind in outs),
        in_specs=[VMEM] * len(operands),
        out_specs=tuple(VMEM for _ in outs),
        compiler_params=pltpu.CompilerParams(vmem_limit_bytes=16 * 2**20),
        cost_estimate=pl.CostEstimate(
            flops=flops, bytes_accessed=flops // 1024, transcendentals=0
        ),
    )(*operands)


def stacked(pieces):
    return jnp.concatenate([piece.astype(F32) for piece in pieces]).astype(BF)


def under_rank(sums, turns, rank_part, ranks_ref):
    me = lax.axis_index("list")
    groups = []
    for index, turn in enumerate(turns):
        values = sums[index * rank_part : (index + 1) * rank_part]
        level = (me ^ turn) * rank_part + lax.broadcasted_iota(jnp.int32, values.shape, 0)
        groups.append(jnp.where(level < ranks_ref[...], values, 0.0))
    return groups


def basis_groups(side, cut, refs):
    pieces = [ref[side, :, cut] for ref in refs[:2]]
    return stacked(pieces + [ref[index, :, cut] for ref in refs[2:] for index in range(2)])


def coefficient_kernel(bases_ref, across_ref, block_ref, beside_ref, ranks_ref, out_ref):
    me = lax.axis_index("list")
    rows = block_ref.shape[0]
    total = 0.0
    for part, operand_ref in ((me, block_ref), (me ^ 1, beside_ref)):
        cut = pl.ds(pl.multiple_of(part * rows, rows), rows)
        bases = basis_groups(0, cut, (bases_ref, across_ref))
        total += jnp.dot(bases, operand_ref[...], preferred_element_type=F32)
    groups = under_rank(total, (0, 2), bases_ref.shape[1], ranks_ref)
    out_ref[...] = jnp.concatenate(groups).astype(out_ref.dtype)


def tile_swap(block, turn):
    return lax.ppermute(block, "tile", [(i, i ^ turn) for i in range(lax.axis_size("tile"))])


def middle_swap(block):
    tiles, parts = lax.axis_size("tile"), lax.axis_size("list")
    route = []
    for tile in range(tiles):
        for part in range(parts):
            to = (tile - 1 + 2 * (tile % 2), part)
            if tile in (0, tiles - 1):
                to = (tile, part ^ 1)
            route.append((tile * parts + part, to[0] * parts + to[1]))
    return lax.ppermute(block, ("tile", "list"), route)


def far_swap(block):
    tiles, parts = lax.axis_size("tile"), lax.axis_size("list")
    route = [
        (tile * parts + part, (tile ^ (2 + part % 2)) * parts + part)
        for tile in range(tiles)
        for part in range(parts)
    ]
    return lax.ppermute(block, ("tile", "list"), route)


def list_swap(block, bit):
    return lax.ppermute(block, "list", [(i, i ^ bit) for i in range(lax.axis_size("list"))])


def near_choice(columns, tile, me, refs):
    chosen = refs[0][...]
    for turn in (1, 2, 3):
        chosen = jnp.where(columns == tile ^ turn, refs[turn][...], chosen)
    return chosen


def far_choice(columns, tile, me, refs):
    own_ref, near_by_ref, far_ref = refs
    half = own_ref.shape[0] // 2
    first = jnp.where(columns == tile, own_ref[:half, :], 0)
    first = jnp.where(columns == tile ^ 1, near_by_ref[...], first)
    far = columns == tile ^ (2 + lax.rem(me, 2))
    return jnp.concatenate(
        [jnp.where(far, far_ref[:half, :], first), jnp.where(far, far_ref[half:, :], 0)]
    )


def near_kernel(turns, near_ref, own_ref, second_ref, first_ref, *refs):
    base_refs, out_refs = refs[: -len(turns)], refs[-len(turns) :]
    count = lax.axis_size("tile")
    tile = lax.axis_index("tile")
    me = lax.axis_index("list")
    rows = near_ref.shape[2]
    odd = lax.rem(tile, 2)
    inside = (tile > 0) & (tile < count - 1)
    blocks = [
        (1, own_ref[...]),
        (2 - 2 * odd, first_ref[...]),
        (2 * odd, jnp.where(inside, second_ref[...], 0)),
    ]
    for index, turn in enumerate(turns):
        cut = pl.ds(pl.multiple_of((me ^ turn) * rows, rows), rows)
        total = base_refs[index][...] if base_refs else 0.0
        for side, block in blocks:
            total += jnp.dot(near_ref[side, cut, :], block, preferred_element_type=F32)
        out_refs[index][...] = total.astype(out_refs[index].dtype)


def far_parts(choice, turns, columns_ref, bases_refs, coefficient_refs):
    me = lax.axis_index("list")
    chosen = choice(columns_ref[...], lax.axis_index("tile"), me, coefficient_refs)
    rows = bases_refs[0].shape[2] // 4
    for turn in turns:
        cut = pl.ds(pl.multiple_of((me ^ turn) * rows, rows), rows)
        left = basis_groups(1, cut, bases_refs)
        yield cut, lax.dot_general(
            left, chosen, (((0,), (0,)), ((), ())), preferred_element_type=F32
        )


def right_products(totals, bases_refs):
    return sum(
        jnp.dot(basis_groups(0, cut, bases_refs), total, preferred_element_type=F32)
        for cut, total in totals
    )


def first_kernel(turns, columns_ref, bases_ref, across_ref, other_ref, *refs):
    coefficient_refs, refs = refs[:4], refs[4:]
    base_refs, refs = refs[: len(turns)], refs[len(turns) :]
    last = 0 in turns
    sums_before, refs = (refs[:1], refs[1:]) if 3 not in turns else ((), refs)
    ranks_ref, refs = (refs[0], refs[1:]) if last else (None, refs)
    bases_refs = (bases_ref, across_ref)
    totals = []
    parts = far_parts(near_choice, turns, columns_ref, bases_refs, coefficient_refs)
    for (cut, total), base_ref, out_ref in zip(parts, base_refs, refs):
        total += base_ref[...]
        out_ref[...] = total.astype(out_ref.dtype)
        totals.append((cut, total.astype(BF)))
    sums = right_products(totals, (*bases_refs, other_ref))
    for ref in sums_before:
        sums += ref[...]
    if not last:
        refs[-1][...] = sums
        return
    groups = under_rank(sums, (0, 2, 1, 3), bases_ref.shape[1], ranks_ref)
    refs[-2][...] = jnp.concatenate(groups)
    refs[-1][...] = jnp.concatenate(groups[2:] + groups[:2])


def far_kernel(turns, columns_ref, bases_ref, across_ref, other_ref, *refs):
    bases_refs = (bases_ref, across_ref, other_ref)
    parts = far_parts(far_choice, turns, columns_ref, bases_refs, refs[:3])
    for (_, total), out_ref in zip(parts, refs[3:]):
        out_ref[...] = total


def one_slot(probes, right_bases, left_bases, near_tiles, tile_ranks, column_rows, row_columns):
    rows, probe_count = probes.shape
    rank_part = right_bases.shape[2]
    near = near_tiles[0].transpose(1, 0, 2)
    flops = 2 * near.size * probe_count
    ranks = 4 * rank_part

    bases = jnp.stack([right_bases[0, 0], left_bases[0, 0]])
    bases, probes = lax.optimization_barrier((bases, probes))
    across = list_swap(bases, 2)
    block = probes.astype(BF)
    beside = [block, middle_swap(block), tile_swap(block, 1)]
    (own,) = kernel_call(
        coefficient_kernel,
        [((ranks // 2, probe_count), BF)],
        (bases, across, block, list_swap(block, 1), tile_ranks),
        8 * flops,
    )
    coefficients = [own] + [tile_swap(own, turn) for turn in (1, 2, 3)]
    right, _ = lax.optimization_barrier((jnp.stack([bases[0], across[0]]), own))
    fixed = (row_columns, bases, across)
    operands = (*fixed, list_swap(right, 1), *coefficients)
    small = ((ranks, probe_count), F32)

    def call(kernel, turns, operands, more=(), cost=1, kind=F32):
        outs = [((rows, probe_count), kind)] * len(turns) + list(more)
        kernel = functools.partial(kernel, turns)
        return kernel_call(kernel, outs, operands, cost * len(turns) * flops // 4)

    base = call(near_kernel, (3, 2, 1, 0), (near, *beside), cost=0)
    send, sums = call(first_kernel, (3,), (*operands, base[0]), [small], kind=BF)
    arrived = list_swap(send, 1)
    crossing, send, keep, own, other = call(
        first_kernel, (2, 1, 0), (*operands, *base[1:], sums, tile_ranks), [small] * 2
    )
    crossed = list_swap((crossing + arrived).astype(BF), 2)
    own = (own + list_swap(other, 1)).astype(BF)
    near_by, far = tile_swap(own[: ranks // 2], 1), far_swap(own)
    block = (keep + list_swap(send, 1) + crossed).astype(BF)
    held, held_across, near_by, far, ready = lax.optimization_barrier(
        (bases, across, near_by, far, block)
    )
    beside = [block, middle_swap(ready), tile_swap(block, 1)]
    left = list_swap(jnp.stack([held[1], held_across[1]]), 1)

    base = call(far_kernel, (3, 2, 1, 0), (*fixed, left, own, near_by, far), cost=0)
    (send,) = call(near_kernel, (3,), (near, *beside, base[0]), kind=BF)
    arrived = list_swap(send, 1)
    (keep,) = call(near_kernel, (2,), (near, *beside, base[1]))
    crossing = (keep + arrived).astype(BF)
    near, crossing = lax.optimization_barrier((near, crossing))
    crossed = list_swap(crossing, 2)
    send, keep = call(near_kernel, (1, 0), (near, *beside, *base[2:]))
    return keep + list_swap_in_pieces(send, 1, 2) + crossed


def local(probes, right_bases, left_bases, near_tiles, tile_ranks, column_rows, row_columns):
    few = lax.axis_size("tile") == 4 and lax.axis_size("list") == 4
    small = right_bases.shape[1] == 1 and few
    form = one_slot if small else many_slots
    return form(
        probes, right_bases, left_bases, near_tiles, tile_ranks, column_rows, row_columns
    )


def solution(mesh):
    placed = (
        P(("group", "tile", "list"), None),
        P(("group", "tile"), None, "list", None),
        P(("group", "tile"), None, "list", None),
        P(("group", "tile"), None, None, "list"),
        P(("group", "tile"), None),
        P("tile", None),
        P("tile", None),
    )
    return jax.shard_map(
        local,
        mesh=mesh,
        in_specs=placed,
        out_specs=P(("group", "tile", "list"), None),
        check_vma=False,
    )
```

```python
import functools

import jax
import jax.numpy as jnp
from jax import lax
from jax.experimental import pallas as pl
from jax.experimental.pallas import tpu as pltpu
from jax.sharding import PartitionSpec as P

BF = jnp.bfloat16
F32 = jnp.float32


def shifted(block, axis, distance):
    devices = range(lax.axis_size(axis))
    route = [(i - distance, i) for i in devices if i - distance in devices]
    return lax.ppermute(block, axis, route)


def image_part(operand, right_bases, left_bases, near_tiles, tile_ranks, column_rows, row_columns):
    tile_slots = right_bases.shape[1]
    rank_part = right_bases.shape[2]
    tile_rows = right_bases.shape[3]
    probe_count = operand.shape[1]
    tile_count = lax.axis_size("tile")
    right_flat = right_bases.reshape(tile_slots * rank_part, tile_rows)
    left_flat = left_bases.reshape(tile_slots * rank_part, tile_rows)
    dense_flat = near_tiles.reshape(tile_rows, -1)
    values = jnp.dot(
        right_flat,
        lax.all_gather(operand, "list", axis=0, tiled=True),
        preferred_element_type=F32,
    )
    rank_level = lax.axis_index("list") * rank_part + lax.iota(jnp.int32, rank_part)
    rank_mask = rank_level[None, :] < tile_ranks[0][:, None]
    coefficients = jnp.where(
        rank_mask[:, :, None], values.reshape(tile_slots, rank_part, probe_count), 0.0
    ).astype(BF)
    targets = (column_rows[0][None, :] == lax.iota(jnp.int32, tile_count)[:, None]).astype(BF)
    outgoing = jnp.einsum(
        "dk,krp->drp", targets, coefficients, preferred_element_type=F32
    ).astype(BF)
    sources = (row_columns[0][:, None] == lax.iota(jnp.int32, tile_count)[None, :]).astype(BF)
    chosen = jnp.einsum(
        "kj,jrp->krp",
        sources,
        lax.all_to_all(outgoing, "tile", split_axis=0, concat_axis=0, tiled=True),
        preferred_element_type=F32,
    ).astype(BF)
    chosen = chosen.reshape(tile_slots * rank_part, -1)
    far_sum = lax.dot_general(
        left_flat, chosen, (((0,), (0,)), ((), ())), preferred_element_type=F32
    )
    arrived = {}
    for offset in (1, -1):
        arrived[offset] = shifted(operand, "tile", offset)
    stacked = jnp.concatenate([arrived[1], operand, arrived[-1]], axis=0)
    near_sum = jnp.dot(dense_flat, stacked, preferred_element_type=F32)
    partial_image = near_sum + far_sum
    return lax.psum_scatter(partial_image, "list", scatter_dimension=0, tiled=True)


def many_slots(probes, right_bases, left_bases, near_tiles, tile_ranks, column_rows, row_columns):
    rest = (right_bases, left_bases, near_tiles, tile_ranks, column_rows, row_columns)
    first_pass = image_part(probes.astype(BF), *rest).astype(BF)
    return image_part(first_pass, *rest)


VMEM = pl.BlockSpec(memory_space=pltpu.VMEM)


def list_swap_in_pieces(block, bit, pieces):
    return jnp.concatenate([list_swap(piece, bit) for piece in jnp.split(block, pieces)])


def kernel_call(kernel, outs, operands, flops=0):
    return pl.pallas_call(
        kernel,
        out_shape=tuple(jax.ShapeDtypeStruct(shape, kind) for shape, kind in outs),
        in_specs=[VMEM] * len(operands),
        out_specs=tuple(VMEM for _ in outs),
        compiler_params=pltpu.CompilerParams(vmem_limit_bytes=16 * 2**20),
        cost_estimate=pl.CostEstimate(
            flops=flops, bytes_accessed=flops // 1024, transcendentals=0
        ),
    )(*operands)


def round_kernel(probes_ref, out_ref):
    out_ref[...] = probes_ref[...].astype(out_ref.dtype)


def join_kernel(right_ref, left_ref, out_ref):
    out_ref[0] = right_ref[0, 0]
    out_ref[1] = left_ref[0, 0]


def stacked(pieces):
    return jnp.concatenate([piece.astype(F32) for piece in pieces]).astype(BF)


def under_rank(sums, turns, rank_part, ranks_ref):
    me = lax.axis_index("list")
    groups = []
    for index, turn in enumerate(turns):
        values = sums[index * rank_part : (index + 1) * rank_part]
        level = (me ^ turn) * rank_part + lax.broadcasted_iota(jnp.int32, values.shape, 0)
        groups.append(jnp.where(level < ranks_ref[...], values, 0.0))
    return groups


def basis_groups(side, cut, refs):
    pieces = [ref[side, :, cut] for ref in refs[:2]]
    return stacked(pieces + [ref[index, :, cut] for ref in refs[2:] for index in range(2)])


def coefficient_kernel(bases_ref, across_ref, block_ref, beside_ref, ranks_ref, out_ref):
    me = lax.axis_index("list")
    rows = block_ref.shape[0]
    total = 0.0
    for part, operand_ref in ((me, block_ref), (me ^ 1, beside_ref)):
        cut = pl.ds(pl.multiple_of(part * rows, rows), rows)
        bases = basis_groups(0, cut, (bases_ref, across_ref))
        total += jnp.dot(bases, operand_ref[...], preferred_element_type=F32)
    groups = under_rank(total, (0, 2), bases_ref.shape[1], ranks_ref)
    out_ref[...] = jnp.concatenate(groups).astype(out_ref.dtype)


def tile_swap(block, turn):
    return lax.ppermute(block, "tile", [(i, i ^ turn) for i in range(lax.axis_size("tile"))])


def middle_swap(block):
    tiles, parts = lax.axis_size("tile"), lax.axis_size("list")
    route = []
    for tile in range(tiles):
        for part in range(parts):
            to = (tile - 1 + 2 * (tile % 2), part)
            if tile in (0, tiles - 1):
                to = (tile, part ^ 1)
            route.append((tile * parts + part, to[0] * parts + to[1]))
    return lax.ppermute(block, ("tile", "list"), route)


def far_swap(block):
    tiles, parts = lax.axis_size("tile"), lax.axis_size("list")
    route = [
        (tile * parts + part, (tile ^ (2 + part % 2)) * parts + part)
        for tile in range(tiles)
        for part in range(parts)
    ]
    return lax.ppermute(block, ("tile", "list"), route)


def list_swap(block, bit):
    return lax.ppermute(block, "list", [(i, i ^ bit) for i in range(lax.axis_size("list"))])


def near_choice(columns, tile, me, refs):
    chosen = refs[0][...]
    for turn in (1, 2, 3):
        chosen = jnp.where(columns == tile ^ turn, refs[turn][...], chosen)
    return chosen


def far_choice(columns, tile, me, refs):
    own_ref, near_by_ref, far_ref = refs
    half = own_ref.shape[0] // 2
    first = jnp.where(columns == tile, own_ref[:half, :], 0)
    first = jnp.where(columns == tile ^ 1, near_by_ref[...], first)
    far = columns == tile ^ (2 + lax.rem(me, 2))
    return jnp.concatenate(
        [jnp.where(far, far_ref[:half, :], first), jnp.where(far, far_ref[half:, :], 0)]
    )


def near_kernel(turns, near_ref, own_ref, second_ref, first_ref, *refs):
    base_refs, out_refs = refs[: -len(turns)], refs[-len(turns) :]
    count = lax.axis_size("tile")
    tile = lax.axis_index("tile")
    me = lax.axis_index("list")
    rows = near_ref.shape[2]
    odd = lax.rem(tile, 2)
    inside = (tile > 0) & (tile < count - 1)
    blocks = [
        (1, own_ref[...]),
        (2 - 2 * odd, first_ref[...]),
        (2 * odd, jnp.where(inside, second_ref[...], 0)),
    ]
    for index, turn in enumerate(turns):
        cut = pl.ds(pl.multiple_of((me ^ turn) * rows, rows), rows)
        total = base_refs[index][...] if base_refs else 0.0
        for side, block in blocks:
            total += jnp.dot(near_ref[side, cut, :], block, preferred_element_type=F32)
        out_refs[index][...] = total


def far_parts(choice, turns, columns_ref, bases_refs, coefficient_refs):
    me = lax.axis_index("list")
    chosen = choice(columns_ref[...], lax.axis_index("tile"), me, coefficient_refs)
    rows = bases_refs[0].shape[2] // 4
    for turn in turns:
        cut = pl.ds(pl.multiple_of((me ^ turn) * rows, rows), rows)
        left = basis_groups(1, cut, bases_refs)
        yield cut, lax.dot_general(
            left, chosen, (((0,), (0,)), ((), ())), preferred_element_type=F32
        )


def right_products(totals, bases_refs):
    return sum(
        jnp.dot(basis_groups(0, cut, bases_refs), total, preferred_element_type=F32)
        for cut, total in totals
    )


def first_kernel(turns, columns_ref, bases_ref, across_ref, other_ref, *refs):
    coefficient_refs, refs = refs[:4], refs[4:]
    base_refs, refs = refs[: len(turns)], refs[len(turns) :]
    last = 0 in turns
    sums_before, refs = (refs[:1], refs[1:]) if 3 not in turns else ((), refs)
    ranks_ref, refs = (refs[0], refs[1:]) if last else (None, refs)
    bases_refs = (bases_ref, across_ref)
    totals = []
    parts = far_parts(near_choice, turns, columns_ref, bases_refs, coefficient_refs)
    for (cut, total), base_ref, out_ref in zip(parts, base_refs, refs):
        total += base_ref[...]
        out_ref[...] = total
        totals.append((cut, total.astype(BF)))
    sums = right_products(totals, (*bases_refs, other_ref))
    for ref in sums_before:
        sums += ref[...]
    if not last:
        refs[-1][...] = sums
        return
    groups = under_rank(sums, (0, 2, 1, 3), bases_ref.shape[1], ranks_ref)
    refs[-2][...] = jnp.concatenate(groups)
    refs[-1][...] = jnp.concatenate(groups[2:] + groups[:2])


def far_kernel(turns, columns_ref, bases_ref, across_ref, other_ref, *refs):
    bases_refs = (bases_ref, across_ref, other_ref)
    parts = far_parts(far_choice, turns, columns_ref, bases_refs, refs[:3])
    for (_, total), out_ref in zip(parts, refs[3:]):
        out_ref[...] = total


def one_slot(probes, right_bases, left_bases, near_tiles, tile_ranks, column_rows, row_columns):
    rows, probe_count = probes.shape
    rank_part = right_bases.shape[2]
    near = near_tiles[0].transpose(1, 0, 2)
    flops = 2 * near.size * probe_count
    part = ((rows, probe_count), F32)
    ranks = 4 * rank_part

    (block,) = kernel_call(round_kernel, [(probes.shape, BF)], (probes,), 8 * flops)
    block, right, left = lax.optimization_barrier((block, right_bases, left_bases))
    (bases,) = kernel_call(join_kernel, [((2, *right_bases.shape[2:]), BF)], (right, left))
    across = list_swap(bases, 2)
    beside = [block, middle_swap(block), tile_swap(block, 1)]
    (own,) = kernel_call(
        coefficient_kernel,
        [((ranks // 2, probe_count), BF)],
        (bases, across, block, list_swap(block, 1), tile_ranks),
        8 * flops,
    )
    coefficients = [own] + [tile_swap(own, turn) for turn in (1, 2, 3)]
    right, _ = lax.optimization_barrier((jnp.stack([bases[0], across[0]]), own))
    fixed = (row_columns, bases, across)
    operands = (*fixed, list_swap(right, 1), *coefficients)
    small = ((ranks, probe_count), F32)

    def call(kernel, turns, operands, more=(), cost=1):
        outs = [part] * len(turns) + list(more)
        kernel = functools.partial(kernel, turns)
        return kernel_call(kernel, outs, operands, cost * len(turns) * flops // 4)

    base = call(near_kernel, (3, 2, 1, 0), (near, *beside), cost=0)
    send, sums = call(first_kernel, (3,), (*operands, base[0]), [small])
    arrived = list_swap(send, 1)
    crossing, send, keep, own, other = call(
        first_kernel, (2, 1, 0), (*operands, *base[1:], sums, tile_ranks), [small] * 2
    )
    crossed = list_swap((crossing + arrived).astype(BF), 2)
    own = (own + list_swap(other, 1)).astype(BF)
    near_by, far = tile_swap(own[: ranks // 2], 1), far_swap(own)
    block = (keep + list_swap(send, 1) + crossed).astype(BF)
    held, held_across, near_by, far, ready = lax.optimization_barrier(
        (bases, across, near_by, far, block)
    )
    beside = [block, middle_swap(ready), tile_swap(block, 1)]
    left = list_swap(jnp.stack([held[1], held_across[1]]), 1)

    base = call(far_kernel, (3, 2, 1, 0), (*fixed, left, own, near_by, far), cost=0)
    (send,) = call(near_kernel, (3,), (near, *beside, base[0]))
    arrived = list_swap(send, 1)
    (keep,) = call(near_kernel, (2,), (near, *beside, base[1]))
    crossing = (keep + arrived).astype(BF)
    near, crossing = lax.optimization_barrier((near, crossing))
    crossed = list_swap(crossing, 2)
    send, keep = call(near_kernel, (1, 0), (near, *beside, *base[2:]))
    return keep + list_swap_in_pieces(send, 1, 2) + crossed


def local(probes, right_bases, left_bases, near_tiles, tile_ranks, column_rows, row_columns):
    few = lax.axis_size("tile") == 4 and lax.axis_size("list") == 4
    small = right_bases.shape[1] == 1 and few
    form = one_slot if small else many_slots
    return form(
        probes, right_bases, left_bases, near_tiles, tile_ranks, column_rows, row_columns
    )


def solution(mesh):
    placed = (
        P(("group", "tile", "list"), None),
        P(("group", "tile"), None, "list", None),
        P(("group", "tile"), None, "list", None),
        P(("group", "tile"), None, None, "list"),
        P(("group", "tile"), None),
        P("tile", None),
        P("tile", None),
    )
    return jax.shard_map(
        local,
        mesh=mesh,
        in_specs=placed,
        out_specs=P(("group", "tile", "list"), None),
        check_vma=False,
    )
```

```python
import functools

import jax
import jax.numpy as jnp
from jax import lax
from jax.experimental import pallas as pl
from jax.experimental.pallas import tpu as pltpu
from jax.sharding import PartitionSpec as P

BF = jnp.bfloat16
F32 = jnp.float32


def shifted(block, axis, distance):
    devices = range(lax.axis_size(axis))
    route = [(i - distance, i) for i in devices if i - distance in devices]
    return lax.ppermute(block, axis, route)


def image_part(operand, right_bases, left_bases, near_tiles, tile_ranks, column_rows, row_columns):
    tile_slots = right_bases.shape[1]
    rank_part = right_bases.shape[2]
    tile_rows = right_bases.shape[3]
    probe_count = operand.shape[1]
    tile_count = lax.axis_size("tile")
    right_flat = right_bases.reshape(tile_slots * rank_part, tile_rows)
    left_flat = left_bases.reshape(tile_slots * rank_part, tile_rows)
    dense_flat = near_tiles.reshape(tile_rows, -1)
    values = jnp.dot(
        right_flat,
        lax.all_gather(operand, "list", axis=0, tiled=True),
        preferred_element_type=F32,
    )
    rank_level = lax.axis_index("list") * rank_part + lax.iota(jnp.int32, rank_part)
    rank_mask = rank_level[None, :] < tile_ranks[0][:, None]
    coefficients = jnp.where(
        rank_mask[:, :, None], values.reshape(tile_slots, rank_part, probe_count), 0.0
    ).astype(BF)
    targets = (column_rows[0][None, :] == lax.iota(jnp.int32, tile_count)[:, None]).astype(BF)
    outgoing = jnp.einsum(
        "dk,krp->drp", targets, coefficients, preferred_element_type=F32
    ).astype(BF)
    sources = (row_columns[0][:, None] == lax.iota(jnp.int32, tile_count)[None, :]).astype(BF)
    chosen = jnp.einsum(
        "kj,jrp->krp",
        sources,
        lax.all_to_all(outgoing, "tile", split_axis=0, concat_axis=0, tiled=True),
        preferred_element_type=F32,
    ).astype(BF)
    chosen = chosen.reshape(tile_slots * rank_part, -1)
    far_sum = lax.dot_general(
        left_flat, chosen, (((0,), (0,)), ((), ())), preferred_element_type=F32
    )
    arrived = {}
    for offset in (1, -1):
        arrived[offset] = shifted(operand, "tile", offset)
    stacked = jnp.concatenate([arrived[1], operand, arrived[-1]], axis=0)
    near_sum = jnp.dot(dense_flat, stacked, preferred_element_type=F32)
    partial_image = near_sum + far_sum
    return lax.psum_scatter(partial_image, "list", scatter_dimension=0, tiled=True)


def many_slots(probes, right_bases, left_bases, near_tiles, tile_ranks, column_rows, row_columns):
    rest = (right_bases, left_bases, near_tiles, tile_ranks, column_rows, row_columns)
    first_pass = image_part(probes.astype(BF), *rest).astype(BF)
    return image_part(first_pass, *rest)


VMEM = pl.BlockSpec(memory_space=pltpu.VMEM)


def list_swap_in_pieces(block, bit, pieces):
    return jnp.concatenate([list_swap(piece, bit) for piece in jnp.split(block, pieces)])


def kernel_call(kernel, outs, operands, flops=0):
    return pl.pallas_call(
        kernel,
        out_shape=tuple(jax.ShapeDtypeStruct(shape, kind) for shape, kind in outs),
        in_specs=[VMEM] * len(operands),
        out_specs=tuple(VMEM for _ in outs),
        compiler_params=pltpu.CompilerParams(vmem_limit_bytes=16 * 2**20),
        cost_estimate=pl.CostEstimate(
            flops=flops, bytes_accessed=flops // 1024, transcendentals=0
        ),
    )(*operands)


def round_kernel(probes_ref, out_ref):
    out_ref[...] = probes_ref[...].astype(out_ref.dtype)


def join_kernel(right_ref, left_ref, out_ref):
    out_ref[0] = right_ref[0, 0]
    out_ref[1] = left_ref[0, 0]


def stacked(pieces):
    return jnp.concatenate([piece.astype(F32) for piece in pieces]).astype(BF)


def under_rank(sums, turns, rank_part, ranks_ref):
    me = lax.axis_index("list")
    groups = []
    for index, turn in enumerate(turns):
        values = sums[index * rank_part : (index + 1) * rank_part]
        level = (me ^ turn) * rank_part + lax.broadcasted_iota(jnp.int32, values.shape, 0)
        groups.append(jnp.where(level < ranks_ref[...], values, 0.0))
    return groups


def basis_groups(side, cut, refs):
    pieces = [ref[side, :, cut] for ref in refs[:2]]
    return stacked(pieces + [ref[index, :, cut] for ref in refs[2:] for index in range(2)])


def coefficient_kernel(bases_ref, across_ref, block_ref, beside_ref, ranks_ref, out_ref):
    me = lax.axis_index("list")
    rows = block_ref.shape[0]
    total = 0.0
    for part, operand_ref in ((me, block_ref), (me ^ 1, beside_ref)):
        cut = pl.ds(pl.multiple_of(part * rows, rows), rows)
        bases = basis_groups(0, cut, (bases_ref, across_ref))
        total += jnp.dot(bases, operand_ref[...], preferred_element_type=F32)
    groups = under_rank(total, (0, 2), bases_ref.shape[1], ranks_ref)
    out_ref[...] = jnp.concatenate(groups).astype(out_ref.dtype)


def tile_swap(block, turn):
    return lax.ppermute(block, "tile", [(i, i ^ turn) for i in range(lax.axis_size("tile"))])


def middle_swap(block):
    tiles, parts = lax.axis_size("tile"), lax.axis_size("list")
    route = []
    for tile in range(tiles):
        for part in range(parts):
            to = (tile - 1 + 2 * (tile % 2), part)
            if tile in (0, tiles - 1):
                to = (tile, part ^ 1)
            route.append((tile * parts + part, to[0] * parts + to[1]))
    return lax.ppermute(block, ("tile", "list"), route)


def far_swap(block):
    tiles, parts = lax.axis_size("tile"), lax.axis_size("list")
    route = [
        (tile * parts + part, (tile ^ (2 + part % 2)) * parts + part)
        for tile in range(tiles)
        for part in range(parts)
    ]
    return lax.ppermute(block, ("tile", "list"), route)


def list_swap(block, bit):
    return lax.ppermute(block, "list", [(i, i ^ bit) for i in range(lax.axis_size("list"))])


def near_choice(columns, tile, me, refs):
    chosen = refs[0][...]
    for turn in (1, 2, 3):
        chosen = jnp.where(columns == tile ^ turn, refs[turn][...], chosen)
    return chosen


def far_choice(columns, tile, me, refs):
    own_ref, near_by_ref, far_ref = refs
    half = own_ref.shape[0] // 2
    first = jnp.where(columns == tile, own_ref[:half, :], 0)
    first = jnp.where(columns == tile ^ 1, near_by_ref[...], first)
    far = columns == tile ^ (2 + lax.rem(me, 2))
    return jnp.concatenate(
        [jnp.where(far, far_ref[:half, :], first), jnp.where(far, far_ref[half:, :], 0)]
    )


def near_kernel(turns, near_ref, own_ref, second_ref, first_ref, *refs):
    base_refs, out_refs = refs[: -len(turns)], refs[-len(turns) :]
    count = lax.axis_size("tile")
    tile = lax.axis_index("tile")
    me = lax.axis_index("list")
    rows = near_ref.shape[2]
    odd = lax.rem(tile, 2)
    inside = (tile > 0) & (tile < count - 1)
    blocks = [
        (1, own_ref[...]),
        (2 - 2 * odd, first_ref[...]),
        (2 * odd, jnp.where(inside, second_ref[...], 0)),
    ]
    for index, turn in enumerate(turns):
        cut = pl.ds(pl.multiple_of((me ^ turn) * rows, rows), rows)
        total = base_refs[index][...] if base_refs else 0.0
        for side, block in blocks:
            total += jnp.dot(near_ref[side, cut, :], block, preferred_element_type=F32)
        out_refs[index][...] = total


def far_parts(choice, turns, columns_ref, bases_refs, coefficient_refs):
    me = lax.axis_index("list")
    chosen = choice(columns_ref[...], lax.axis_index("tile"), me, coefficient_refs)
    rows = bases_refs[0].shape[2] // 4
    for turn in turns:
        cut = pl.ds(pl.multiple_of((me ^ turn) * rows, rows), rows)
        left = basis_groups(1, cut, bases_refs)
        yield cut, lax.dot_general(
            left, chosen, (((0,), (0,)), ((), ())), preferred_element_type=F32
        )


def right_products(totals, bases_refs):
    return sum(
        jnp.dot(basis_groups(0, cut, bases_refs), total, preferred_element_type=F32)
        for cut, total in totals
    )


def first_kernel(turns, columns_ref, bases_ref, across_ref, other_ref, *refs):
    coefficient_refs, refs = refs[:4], refs[4:]
    base_refs, refs = refs[: len(turns)], refs[len(turns) :]
    last = 0 in turns
    sums_before, refs = (refs[:1], refs[1:]) if 3 not in turns else ((), refs)
    ranks_ref, refs = (refs[0], refs[1:]) if last else (None, refs)
    bases_refs = (bases_ref, across_ref)
    totals = []
    parts = far_parts(near_choice, turns, columns_ref, bases_refs, coefficient_refs)
    for (cut, total), base_ref, out_ref in zip(parts, base_refs, refs):
        total += base_ref[...]
        out_ref[...] = total
        totals.append((cut, total.astype(BF)))
    sums = right_products(totals, (*bases_refs, other_ref))
    for ref in sums_before:
        sums += ref[...]
    if not last:
        refs[-1][...] = sums
        return
    groups = under_rank(sums, (0, 2, 1, 3), bases_ref.shape[1], ranks_ref)
    refs[-2][...] = jnp.concatenate(groups)
    refs[-1][...] = jnp.concatenate(groups[2:] + groups[:2])


def far_kernel(turns, columns_ref, bases_ref, across_ref, other_ref, *refs):
    bases_refs = (bases_ref, across_ref, other_ref)
    parts = far_parts(far_choice, turns, columns_ref, bases_refs, refs[:3])
    for (_, total), out_ref in zip(parts, refs[3:]):
        out_ref[...] = total


def one_slot(probes, right_bases, left_bases, near_tiles, tile_ranks, column_rows, row_columns):
    rows, probe_count = probes.shape
    rank_part = right_bases.shape[2]
    near = near_tiles[0].transpose(1, 0, 2)
    flops = 2 * near.size * probe_count
    part = ((rows, probe_count), F32)
    ranks = 4 * rank_part

    (block,) = kernel_call(round_kernel, [(probes.shape, BF)], (probes,), 8 * flops)
    block, right, left = lax.optimization_barrier((block, right_bases, left_bases))
    (bases,) = kernel_call(join_kernel, [((2, *right_bases.shape[2:]), BF)], (right, left))
    right_across = list_swap(right_bases[0], 2)
    beside = [block, middle_swap(block), tile_swap(block, 1)]
    (own,) = kernel_call(
        coefficient_kernel,
        [((ranks // 2, probe_count), BF)],
        (bases, right_across, block, list_swap(block, 1), tile_ranks),
        8 * flops,
    )
    coefficients = [own] + [tile_swap(own, turn) for turn in (1, 2, 3)]
    right, _ = lax.optimization_barrier((jnp.stack([bases[0], right_across[0]]), own))
    across = jnp.concatenate([right_across, list_swap(left_bases[0], 2)])
    fixed = (row_columns, bases, across)
    operands = (*fixed, list_swap(right, 1), *coefficients)
    small = ((ranks, probe_count), F32)

    def call(kernel, turns, operands, more=(), cost=1):
        outs = [part] * len(turns) + list(more)
        kernel = functools.partial(kernel, turns)
        return kernel_call(kernel, outs, operands, cost * len(turns) * flops // 4)

    base = call(near_kernel, (3, 2, 1, 0), (near, *beside), cost=0)
    send, sums = call(first_kernel, (3,), (*operands, base[0]), [small])
    arrived = list_swap(send, 1)
    crossing, send, keep, own, other = call(
        first_kernel, (2, 1, 0), (*operands, *base[1:], sums, tile_ranks), [small] * 2
    )
    crossed = list_swap((crossing + arrived).astype(BF), 2)
    own = (own + list_swap(other, 1)).astype(BF)
    near_by, far = tile_swap(own[: ranks // 2], 1), far_swap(own)
    block = (keep + list_swap(send, 1) + crossed).astype(BF)
    held, held_across, near_by, far, ready = lax.optimization_barrier(
        (bases, across, near_by, far, block)
    )
    beside = [block, middle_swap(ready), tile_swap(block, 1)]
    left = list_swap(jnp.stack([held[1], held_across[1]]), 1)

    base = call(far_kernel, (3, 2, 1, 0), (*fixed, left, own, near_by, far), cost=0)
    (send,) = call(near_kernel, (3,), (near, *beside, base[0]))
    arrived = list_swap(send, 1)
    (keep,) = call(near_kernel, (2,), (near, *beside, base[1]))
    crossing = (keep + arrived).astype(BF)
    near, crossing = lax.optimization_barrier((near, crossing))
    crossed = list_swap(crossing, 2)
    send, keep = call(near_kernel, (1, 0), (near, *beside, *base[2:]))
    return keep + list_swap_in_pieces(send, 1, 2) + crossed


def local(probes, right_bases, left_bases, near_tiles, tile_ranks, column_rows, row_columns):
    few = lax.axis_size("tile") == 4 and lax.axis_size("list") == 4
    small = right_bases.shape[1] == 1 and few
    form = one_slot if small else many_slots
    return form(
        probes, right_bases, left_bases, near_tiles, tile_ranks, column_rows, row_columns
    )


def solution(mesh):
    placed = (
        P(("group", "tile", "list"), None),
        P(("group", "tile"), None, "list", None),
        P(("group", "tile"), None, "list", None),
        P(("group", "tile"), None, None, "list"),
        P(("group", "tile"), None),
        P("tile", None),
        P("tile", None),
    )
    return jax.shard_map(
        local,
        mesh=mesh,
        in_specs=placed,
        out_specs=P(("group", "tile", "list"), None),
        check_vma=False,
    )
```

```python
import functools

import jax
import jax.numpy as jnp
from jax import lax
from jax.experimental import pallas as pl
from jax.experimental.pallas import tpu as pltpu
from jax.sharding import PartitionSpec as P

BF = jnp.bfloat16
F32 = jnp.float32


def shifted(block, axis, distance):
    devices = range(lax.axis_size(axis))
    route = [(i - distance, i) for i in devices if i - distance in devices]
    return lax.ppermute(block, axis, route)


def image_part(operand, right_bases, left_bases, near_tiles, tile_ranks, column_rows, row_columns):
    tile_slots = right_bases.shape[1]
    rank_part = right_bases.shape[2]
    tile_rows = right_bases.shape[3]
    probe_count = operand.shape[1]
    tile_count = lax.axis_size("tile")
    right_flat = right_bases.reshape(tile_slots * rank_part, tile_rows)
    left_flat = left_bases.reshape(tile_slots * rank_part, tile_rows)
    dense_flat = near_tiles.reshape(tile_rows, -1)
    values = jnp.dot(
        right_flat,
        lax.all_gather(operand, "list", axis=0, tiled=True),
        preferred_element_type=F32,
    )
    rank_level = lax.axis_index("list") * rank_part + lax.iota(jnp.int32, rank_part)
    rank_mask = rank_level[None, :] < tile_ranks[0][:, None]
    coefficients = jnp.where(
        rank_mask[:, :, None], values.reshape(tile_slots, rank_part, probe_count), 0.0
    ).astype(BF)
    targets = (column_rows[0][None, :] == lax.iota(jnp.int32, tile_count)[:, None]).astype(BF)
    outgoing = jnp.einsum(
        "dk,krp->drp", targets, coefficients, preferred_element_type=F32
    ).astype(BF)
    sources = (row_columns[0][:, None] == lax.iota(jnp.int32, tile_count)[None, :]).astype(BF)
    chosen = jnp.einsum(
        "kj,jrp->krp",
        sources,
        lax.all_to_all(outgoing, "tile", split_axis=0, concat_axis=0, tiled=True),
        preferred_element_type=F32,
    ).astype(BF)
    chosen = chosen.reshape(tile_slots * rank_part, -1)
    far_sum = lax.dot_general(
        left_flat, chosen, (((0,), (0,)), ((), ())), preferred_element_type=F32
    )
    arrived = {}
    for offset in (1, -1):
        arrived[offset] = shifted(operand, "tile", offset)
    stacked = jnp.concatenate([arrived[1], operand, arrived[-1]], axis=0)
    near_sum = jnp.dot(dense_flat, stacked, preferred_element_type=F32)
    partial_image = near_sum + far_sum
    return lax.psum_scatter(partial_image, "list", scatter_dimension=0, tiled=True)


def many_slots(probes, right_bases, left_bases, near_tiles, tile_ranks, column_rows, row_columns):
    rest = (right_bases, left_bases, near_tiles, tile_ranks, column_rows, row_columns)
    first_pass = image_part(probes.astype(BF), *rest).astype(BF)
    return image_part(first_pass, *rest)


VMEM = pl.BlockSpec(memory_space=pltpu.VMEM)


def list_swap_in_pieces(block, bit, pieces):
    return jnp.concatenate([list_swap(piece, bit) for piece in jnp.split(block, pieces)])


def kernel_call(kernel, outs, operands, flops=0):
    return pl.pallas_call(
        kernel,
        out_shape=tuple(jax.ShapeDtypeStruct(shape, kind) for shape, kind in outs),
        in_specs=[VMEM] * len(operands),
        out_specs=tuple(VMEM for _ in outs),
        compiler_params=pltpu.CompilerParams(vmem_limit_bytes=16 * 2**20),
        cost_estimate=pl.CostEstimate(
            flops=flops, bytes_accessed=flops // 1024, transcendentals=0
        ),
    )(*operands)


def round_kernel(probes_ref, out_ref):
    out_ref[...] = probes_ref[...].astype(out_ref.dtype)


def join_kernel(right_ref, left_ref, out_ref):
    out_ref[0] = right_ref[0, 0]
    out_ref[1] = left_ref[0, 0]


def stacked(pieces):
    return jnp.concatenate([piece.astype(F32) for piece in pieces]).astype(BF)


def under_rank(sums, turns, rank_part, ranks_ref):
    me = lax.axis_index("list")
    groups = []
    for index, turn in enumerate(turns):
        values = sums[index * rank_part : (index + 1) * rank_part]
        level = (me ^ turn) * rank_part + lax.broadcasted_iota(jnp.int32, values.shape, 0)
        groups.append(jnp.where(level < ranks_ref[...], values, 0.0))
    return groups


def basis_groups(side, cut, refs):
    pieces = [ref[side, :, cut] for ref in refs[:2]]
    return stacked(pieces + [ref[index, :, cut] for ref in refs[2:] for index in range(2)])


def coefficient_kernel(bases_ref, across_ref, block_ref, beside_ref, ranks_ref, out_ref):
    me = lax.axis_index("list")
    rows = block_ref.shape[0]
    total = 0.0
    for part, operand_ref in ((me, block_ref), (me ^ 1, beside_ref)):
        cut = pl.ds(pl.multiple_of(part * rows, rows), rows)
        bases = basis_groups(0, cut, (bases_ref, across_ref))
        total += jnp.dot(bases, operand_ref[...], preferred_element_type=F32)
    groups = under_rank(total, (0, 2), bases_ref.shape[1], ranks_ref)
    out_ref[...] = jnp.concatenate(groups).astype(out_ref.dtype)


def tile_swap(block, turn):
    return lax.ppermute(block, "tile", [(i, i ^ turn) for i in range(lax.axis_size("tile"))])


def middle_swap(block):
    tiles, parts = lax.axis_size("tile"), lax.axis_size("list")
    route = []
    for tile in range(tiles):
        for part in range(parts):
            to = (tile - 1 + 2 * (tile % 2), part)
            if tile in (0, tiles - 1):
                to = (tile, part ^ 1)
            route.append((tile * parts + part, to[0] * parts + to[1]))
    return lax.ppermute(block, ("tile", "list"), route)


def far_swap(block):
    tiles, parts = lax.axis_size("tile"), lax.axis_size("list")
    route = [
        (tile * parts + part, (tile ^ (2 + part % 2)) * parts + part)
        for tile in range(tiles)
        for part in range(parts)
    ]
    return lax.ppermute(block, ("tile", "list"), route)


def list_swap(block, bit):
    return lax.ppermute(block, "list", [(i, i ^ bit) for i in range(lax.axis_size("list"))])


def near_choice(columns, tile, me, refs):
    chosen = refs[0][...]
    for turn in (1, 2, 3):
        chosen = jnp.where(columns == tile ^ turn, refs[turn][...], chosen)
    return chosen


def far_choice(columns, tile, me, refs):
    own_ref, near_by_ref, far_ref = refs
    half = own_ref.shape[0] // 2
    first = jnp.where(columns == tile, own_ref[:half, :], 0)
    first = jnp.where(columns == tile ^ 1, near_by_ref[...], first)
    far = columns == tile ^ (2 + lax.rem(me, 2))
    return jnp.concatenate(
        [jnp.where(far, far_ref[:half, :], first), jnp.where(far, far_ref[half:, :], 0)]
    )


def near_kernel(turns, near_ref, own_ref, first_ref, second_ref, *refs):
    base_refs, out_refs = refs[: -len(turns)], refs[-len(turns) :]
    count = lax.axis_size("tile")
    tile = lax.axis_index("tile")
    me = lax.axis_index("list")
    rows = near_ref.shape[2]
    odd = lax.rem(tile, 2)
    inside = (tile > 0) & (tile < count - 1)
    blocks = [
        (1, own_ref[...]),
        (2 - 2 * odd, first_ref[...]),
        (2 * odd, jnp.where(inside, second_ref[...], 0)),
    ]
    for index, turn in enumerate(turns):
        cut = pl.ds(pl.multiple_of((me ^ turn) * rows, rows), rows)
        total = base_refs[index][...] if base_refs else 0.0
        for side, block in blocks:
            total += jnp.dot(near_ref[side, cut, :], block, preferred_element_type=F32)
        out_refs[index][...] = total


def far_parts(choice, turns, columns_ref, bases_refs, coefficient_refs):
    me = lax.axis_index("list")
    chosen = choice(columns_ref[...], lax.axis_index("tile"), me, coefficient_refs)
    rows = bases_refs[0].shape[2] // 4
    for turn in turns:
        cut = pl.ds(pl.multiple_of((me ^ turn) * rows, rows), rows)
        left = basis_groups(1, cut, bases_refs)
        yield cut, lax.dot_general(
            left, chosen, (((0,), (0,)), ((), ())), preferred_element_type=F32
        )


def right_products(totals, bases_refs):
    return sum(
        jnp.dot(basis_groups(0, cut, bases_refs), total, preferred_element_type=F32)
        for cut, total in totals
    )


def first_kernel(turns, columns_ref, bases_ref, across_ref, other_ref, *refs):
    coefficient_refs, refs = refs[:4], refs[4:]
    base_refs, refs = refs[: len(turns)], refs[len(turns) :]
    last = 0 in turns
    sums_before, refs = (refs[:1], refs[1:]) if 3 not in turns else ((), refs)
    ranks_ref, refs = (refs[0], refs[1:]) if last else (None, refs)
    bases_refs = (bases_ref, across_ref)
    totals = []
    parts = far_parts(near_choice, turns, columns_ref, bases_refs, coefficient_refs)
    for (cut, total), base_ref, out_ref in zip(parts, base_refs, refs):
        total += base_ref[...]
        out_ref[...] = total
        totals.append((cut, total.astype(BF)))
    sums = right_products(totals, (*bases_refs, other_ref))
    for ref in sums_before:
        sums += ref[...]
    if not last:
        refs[-1][...] = sums
        return
    groups = under_rank(sums, (0, 2, 1, 3), bases_ref.shape[1], ranks_ref)
    refs[-2][...] = jnp.concatenate(groups)
    refs[-1][...] = jnp.concatenate(groups[2:] + groups[:2])


def far_kernel(turns, columns_ref, bases_ref, across_ref, other_ref, *refs):
    bases_refs = (bases_ref, across_ref, other_ref)
    parts = far_parts(far_choice, turns, columns_ref, bases_refs, refs[:3])
    for (_, total), out_ref in zip(parts, refs[3:]):
        out_ref[...] = total


def one_slot(probes, right_bases, left_bases, near_tiles, tile_ranks, column_rows, row_columns):
    rows, probe_count = probes.shape
    rank_part = right_bases.shape[2]
    near = near_tiles[0].transpose(1, 0, 2)
    flops = 2 * near.size * probe_count
    part = ((rows, probe_count), F32)
    ranks = 4 * rank_part

    (block,) = kernel_call(round_kernel, [(probes.shape, BF)], (probes,), 8 * flops)
    block, right, left = lax.optimization_barrier((block, right_bases, left_bases))
    (bases,) = kernel_call(join_kernel, [((2, *right_bases.shape[2:]), BF)], (right, left))
    across = list_swap(bases, 2)
    beside = [block, tile_swap(block, 1), middle_swap(block)]
    (own,) = kernel_call(
        coefficient_kernel,
        [((ranks // 2, probe_count), BF)],
        (bases, across, block, list_swap(block, 1), tile_ranks),
        8 * flops,
    )
    coefficients = [own] + [tile_swap(own, turn) for turn in (1, 2, 3)]
    right, _ = lax.optimization_barrier((jnp.stack([bases[0], across[0]]), own))
    fixed = (row_columns, bases, across)
    operands = (*fixed, list_swap(right, 1), *coefficients)
    small = ((ranks, probe_count), F32)

    def call(kernel, turns, operands, more=(), cost=1):
        outs = [part] * len(turns) + list(more)
        kernel = functools.partial(kernel, turns)
        return kernel_call(kernel, outs, operands, cost * len(turns) * flops // 4)

    base = call(near_kernel, (3, 2, 1, 0), (near, *beside), cost=0)
    send, sums = call(first_kernel, (3,), (*operands, base[0]), [small])
    arrived = list_swap(send, 1)
    crossing, send, keep, own, other = call(
        first_kernel, (2, 1, 0), (*operands, *base[1:], sums, tile_ranks), [small] * 2
    )
    crossed = list_swap((crossing + arrived).astype(BF), 2)
    own = (own + list_swap(other, 1)).astype(BF)
    near_by, far = tile_swap(own[: ranks // 2], 1), far_swap(own)
    block = (keep + list_swap(send, 1) + crossed).astype(BF)
    held, held_across, near_by, far, ready = lax.optimization_barrier(
        (bases, across, near_by, far, block)
    )
    beside = [block, tile_swap(block, 1), middle_swap(ready)]
    left = list_swap(jnp.stack([held[1], held_across[1]]), 1)

    base = call(far_kernel, (3, 2, 1, 0), (*fixed, left, own, near_by, far), cost=0)
    (send,) = call(near_kernel, (3,), (near, *beside, base[0]))
    arrived = list_swap(send, 1)
    (keep,) = call(near_kernel, (2,), (near, *beside, base[1]))
    crossing = (keep + arrived).astype(BF)
    near, crossing = lax.optimization_barrier((near, crossing))
    crossed = list_swap(crossing, 2)
    send, keep = call(near_kernel, (1, 0), (near, *beside, *base[2:]))
    return keep + list_swap_in_pieces(send, 1, 2) + crossed


def local(probes, right_bases, left_bases, near_tiles, tile_ranks, column_rows, row_columns):
    few = lax.axis_size("tile") == 4 and lax.axis_size("list") == 4
    small = right_bases.shape[1] == 1 and few
    form = one_slot if small else many_slots
    return form(
        probes, right_bases, left_bases, near_tiles, tile_ranks, column_rows, row_columns
    )


def solution(mesh):
    placed = (
        P(("group", "tile", "list"), None),
        P(("group", "tile"), None, "list", None),
        P(("group", "tile"), None, "list", None),
        P(("group", "tile"), None, None, "list"),
        P(("group", "tile"), None),
        P("tile", None),
        P("tile", None),
    )
    return jax.shard_map(
        local,
        mesh=mesh,
        in_specs=placed,
        out_specs=P(("group", "tile", "list"), None),
        check_vma=False,
    )
```

```python
import functools

import jax
import jax.numpy as jnp
from jax import lax
from jax.experimental import pallas as pl
from jax.experimental.pallas import tpu as pltpu
from jax.sharding import PartitionSpec as P

BF = jnp.bfloat16
F32 = jnp.float32


def shifted(block, axis, distance):
    devices = range(lax.axis_size(axis))
    route = [(i - distance, i) for i in devices if i - distance in devices]
    return lax.ppermute(block, axis, route)


def image_part(operand, right_bases, left_bases, near_tiles, tile_ranks, column_rows, row_columns):
    tile_slots = right_bases.shape[1]
    rank_part = right_bases.shape[2]
    tile_rows = right_bases.shape[3]
    probe_count = operand.shape[1]
    tile_count = lax.axis_size("tile")
    right_flat = right_bases.reshape(tile_slots * rank_part, tile_rows)
    left_flat = left_bases.reshape(tile_slots * rank_part, tile_rows)
    dense_flat = near_tiles.reshape(tile_rows, -1)
    values = jnp.dot(
        right_flat,
        lax.all_gather(operand, "list", axis=0, tiled=True),
        preferred_element_type=F32,
    )
    rank_level = lax.axis_index("list") * rank_part + lax.iota(jnp.int32, rank_part)
    rank_mask = rank_level[None, :] < tile_ranks[0][:, None]
    coefficients = jnp.where(
        rank_mask[:, :, None], values.reshape(tile_slots, rank_part, probe_count), 0.0
    ).astype(BF)
    targets = (column_rows[0][None, :] == lax.iota(jnp.int32, tile_count)[:, None]).astype(BF)
    outgoing = jnp.einsum(
        "dk,krp->drp", targets, coefficients, preferred_element_type=F32
    ).astype(BF)
    sources = (row_columns[0][:, None] == lax.iota(jnp.int32, tile_count)[None, :]).astype(BF)
    chosen = jnp.einsum(
        "kj,jrp->krp",
        sources,
        lax.all_to_all(outgoing, "tile", split_axis=0, concat_axis=0, tiled=True),
        preferred_element_type=F32,
    ).astype(BF)
    chosen = chosen.reshape(tile_slots * rank_part, -1)
    far_sum = lax.dot_general(
        left_flat, chosen, (((0,), (0,)), ((), ())), preferred_element_type=F32
    )
    arrived = {}
    for offset in (1, -1):
        arrived[offset] = shifted(operand, "tile", offset)
    stacked = jnp.concatenate([arrived[1], operand, arrived[-1]], axis=0)
    near_sum = jnp.dot(dense_flat, stacked, preferred_element_type=F32)
    partial_image = near_sum + far_sum
    return lax.psum_scatter(partial_image, "list", scatter_dimension=0, tiled=True)


def many_slots(probes, right_bases, left_bases, near_tiles, tile_ranks, column_rows, row_columns):
    rest = (right_bases, left_bases, near_tiles, tile_ranks, column_rows, row_columns)
    first_pass = image_part(probes.astype(BF), *rest).astype(BF)
    return image_part(first_pass, *rest)


VMEM = pl.BlockSpec(memory_space=pltpu.VMEM)


def list_swap_in_pieces(block, bit, pieces):
    return jnp.concatenate([list_swap(piece, bit) for piece in jnp.split(block, pieces)])


def kernel_call(kernel, outs, operands, flops=0):
    return pl.pallas_call(
        kernel,
        out_shape=tuple(jax.ShapeDtypeStruct(shape, kind) for shape, kind in outs),
        in_specs=[VMEM] * len(operands),
        out_specs=tuple(VMEM for _ in outs),
        compiler_params=pltpu.CompilerParams(vmem_limit_bytes=16 * 2**20),
        cost_estimate=pl.CostEstimate(
            flops=flops, bytes_accessed=flops // 1024, transcendentals=0
        ),
    )(*operands)


def round_kernel(probes_ref, out_ref):
    out_ref[...] = probes_ref[...].astype(out_ref.dtype)


def join_kernel(right_ref, left_ref, out_ref):
    out_ref[0] = right_ref[0, 0]
    out_ref[1] = left_ref[0, 0]


def stacked(pieces):
    return jnp.concatenate([piece.astype(F32) for piece in pieces]).astype(BF)


def under_rank(sums, turns, rank_part, ranks_ref):
    me = lax.axis_index("list")
    groups = []
    for index, turn in enumerate(turns):
        values = sums[index * rank_part : (index + 1) * rank_part]
        level = (me ^ turn) * rank_part + lax.broadcasted_iota(jnp.int32, values.shape, 0)
        groups.append(jnp.where(level < ranks_ref[...], values, 0.0))
    return groups


def basis_groups(side, cut, refs):
    pieces = [ref[side, :, cut] for ref in refs[:2]]
    return stacked(pieces + [ref[index, :, cut] for ref in refs[2:] for index in range(2)])


def coefficient_kernel(bases_ref, across_ref, block_ref, beside_ref, ranks_ref, out_ref):
    me = lax.axis_index("list")
    rows = block_ref.shape[0]
    total = 0.0
    for part, operand_ref in ((me, block_ref), (me ^ 1, beside_ref)):
        cut = pl.ds(pl.multiple_of(part * rows, rows), rows)
        bases = basis_groups(0, cut, (bases_ref, across_ref))
        total += jnp.dot(bases, operand_ref[...], preferred_element_type=F32)
    groups = under_rank(total, (0, 2), bases_ref.shape[1], ranks_ref)
    out_ref[...] = jnp.concatenate(groups).astype(out_ref.dtype)


def tile_swap(block, turn):
    return lax.ppermute(block, "tile", [(i, i ^ turn) for i in range(lax.axis_size("tile"))])


def middle_swap(block):
    tiles, parts = lax.axis_size("tile"), lax.axis_size("list")
    route = []
    for tile in range(tiles):
        for part in range(parts):
            to = (tile - 1 + 2 * (tile % 2), part)
            if tile in (0, tiles - 1):
                to = (tile, part ^ 1)
            route.append((tile * parts + part, to[0] * parts + to[1]))
    return lax.ppermute(block, ("tile", "list"), route)


def far_swap(block):
    tiles, parts = lax.axis_size("tile"), lax.axis_size("list")
    route = [
        (tile * parts + part, (tile ^ (2 + part % 2)) * parts + part)
        for tile in range(tiles)
        for part in range(parts)
    ]
    return lax.ppermute(block, ("tile", "list"), route)


def list_swap(block, bit):
    return lax.ppermute(block, "list", [(i, i ^ bit) for i in range(lax.axis_size("list"))])


def near_choice(columns, tile, me, refs):
    chosen = refs[0][...]
    for turn in (1, 2, 3):
        chosen = jnp.where(columns == tile ^ turn, refs[turn][...], chosen)
    return chosen


def far_choice(columns, tile, me, refs):
    own_ref, near_by_ref, far_ref = refs
    half = own_ref.shape[0] // 2
    first = jnp.where(columns == tile, own_ref[:half, :], 0)
    first = jnp.where(columns == tile ^ 1, near_by_ref[...], first)
    far = columns == tile ^ (2 + lax.rem(me, 2))
    return jnp.concatenate(
        [jnp.where(far, far_ref[:half, :], first), jnp.where(far, far_ref[half:, :], 0)]
    )


def near_kernel(turns, near_ref, own_ref, first_ref, second_ref, *refs):
    base_refs, out_refs = refs[: -len(turns)], refs[-len(turns) :]
    count = lax.axis_size("tile")
    tile = lax.axis_index("tile")
    me = lax.axis_index("list")
    rows = near_ref.shape[2]
    odd = lax.rem(tile, 2)
    inside = (tile > 0) & (tile < count - 1)
    blocks = [
        (1, own_ref[...]),
        (2 - 2 * odd, first_ref[...]),
        (2 * odd, jnp.where(inside, second_ref[...], 0)),
    ]
    for index, turn in enumerate(turns):
        cut = pl.ds(pl.multiple_of((me ^ turn) * rows, rows), rows)
        total = base_refs[index][...] if base_refs else 0.0
        for side, block in blocks:
            total += jnp.dot(near_ref[side, cut, :], block, preferred_element_type=F32)
        out_refs[index][...] = total


def far_parts(choice, turns, columns_ref, bases_refs, coefficient_refs):
    me = lax.axis_index("list")
    chosen = choice(columns_ref[...], lax.axis_index("tile"), me, coefficient_refs)
    rows = bases_refs[0].shape[2] // 4
    for turn in turns:
        cut = pl.ds(pl.multiple_of((me ^ turn) * rows, rows), rows)
        left = basis_groups(1, cut, bases_refs)
        yield cut, lax.dot_general(
            left, chosen, (((0,), (0,)), ((), ())), preferred_element_type=F32
        )


def right_products(totals, bases_refs):
    return sum(
        jnp.dot(basis_groups(0, cut, bases_refs), total, preferred_element_type=F32)
        for cut, total in totals
    )


def first_kernel(turns, columns_ref, bases_ref, across_ref, other_ref, *refs):
    coefficient_refs, refs = refs[:4], refs[4:]
    base_refs, refs = refs[: len(turns)], refs[len(turns) :]
    last = 0 in turns
    (before_ref, ranks_ref), refs = (refs[:2], refs[2:]) if last else ((None, None), refs)
    bases_refs = (bases_ref, across_ref)
    totals = []
    parts = far_parts(near_choice, turns, columns_ref, bases_refs, coefficient_refs)
    for (cut, total), base_ref, out_ref in zip(parts, base_refs, refs):
        total += base_ref[...]
        out_ref[...] = total
        totals.append((cut, total.astype(BF)))
    if not last:
        return
    rows = before_ref.shape[0]
    cut = pl.ds(pl.multiple_of((lax.axis_index("list") ^ 3) * rows, rows), rows)
    totals.append((cut, before_ref[...].astype(BF)))
    sums = right_products(totals, (*bases_refs, other_ref))
    groups = under_rank(sums, (0, 2, 1, 3), bases_ref.shape[1], ranks_ref)
    refs[-2][...] = jnp.concatenate(groups)
    refs[-1][...] = jnp.concatenate(groups[2:] + groups[:2])


def far_kernel(turns, columns_ref, bases_ref, across_ref, other_ref, *refs):
    bases_refs = (bases_ref, across_ref, other_ref)
    parts = far_parts(far_choice, turns, columns_ref, bases_refs, refs[:3])
    for (_, total), out_ref in zip(parts, refs[3:]):
        out_ref[...] = total


def one_slot(probes, right_bases, left_bases, near_tiles, tile_ranks, column_rows, row_columns):
    rows, probe_count = probes.shape
    rank_part = right_bases.shape[2]
    near = near_tiles[0].transpose(1, 0, 2)
    flops = 2 * near.size * probe_count
    part = ((rows, probe_count), F32)
    ranks = 4 * rank_part

    (block,) = kernel_call(round_kernel, [(probes.shape, BF)], (probes,), 8 * flops)
    block, right, left = lax.optimization_barrier((block, right_bases, left_bases))
    (bases,) = kernel_call(join_kernel, [((2, *right_bases.shape[2:]), BF)], (right, left))
    across = list_swap(bases, 2)
    beside = [block, tile_swap(block, 1), middle_swap(block)]
    (own,) = kernel_call(
        coefficient_kernel,
        [((ranks // 2, probe_count), BF)],
        (bases, across, block, list_swap(block, 1), tile_ranks),
        8 * flops,
    )
    coefficients = [own] + [tile_swap(own, turn) for turn in (1, 2, 3)]
    right, _ = lax.optimization_barrier((jnp.stack([bases[0], across[0]]), own))
    fixed = (row_columns, bases, across)
    operands = (*fixed, list_swap(right, 1), *coefficients)
    small = ((ranks, probe_count), F32)

    def call(kernel, turns, operands, more=(), cost=1):
        outs = [part] * len(turns) + list(more)
        kernel = functools.partial(kernel, turns)
        return kernel_call(kernel, outs, operands, cost * len(turns) * flops // 4)

    base = call(near_kernel, (3, 2, 1, 0), (near, *beside), cost=0)
    (send,) = call(first_kernel, (3,), (*operands, base[0]))
    arrived = list_swap(send, 1)
    crossing, send, keep, own, other = call(
        first_kernel, (2, 1, 0), (*operands, *base[1:], send, tile_ranks), [small] * 2
    )
    crossed = list_swap((crossing + arrived).astype(BF), 2)
    own = (own + list_swap(other, 1)).astype(BF)
    near_by, far = tile_swap(own[: ranks // 2], 1), far_swap(own)
    block = (keep + list_swap(send, 1) + crossed).astype(BF)
    held, held_across, near_by, far, ready = lax.optimization_barrier(
        (bases, across, near_by, far, block)
    )
    beside = [block, tile_swap(block, 1), middle_swap(ready)]
    left = list_swap(jnp.stack([held[1], held_across[1]]), 1)

    base = call(far_kernel, (3, 2, 1, 0), (*fixed, left, own, near_by, far), cost=0)
    (send,) = call(near_kernel, (3,), (near, *beside, base[0]))
    arrived = list_swap(send, 1)
    (keep,) = call(near_kernel, (2,), (near, *beside, base[1]))
    crossing = (keep + arrived).astype(BF)
    near, crossing = lax.optimization_barrier((near, crossing))
    crossed = list_swap(crossing, 2)
    send, keep = call(near_kernel, (1, 0), (near, *beside, *base[2:]))
    return keep + list_swap_in_pieces(send, 1, 2) + crossed


def local(probes, right_bases, left_bases, near_tiles, tile_ranks, column_rows, row_columns):
    few = lax.axis_size("tile") == 4 and lax.axis_size("list") == 4
    small = right_bases.shape[1] == 1 and few
    form = one_slot if small else many_slots
    return form(
        probes, right_bases, left_bases, near_tiles, tile_ranks, column_rows, row_columns
    )


def solution(mesh):
    placed = (
        P(("group", "tile", "list"), None),
        P(("group", "tile"), None, "list", None),
        P(("group", "tile"), None, "list", None),
        P(("group", "tile"), None, None, "list"),
        P(("group", "tile"), None),
        P("tile", None),
        P("tile", None),
    )
    return jax.shard_map(
        local,
        mesh=mesh,
        in_specs=placed,
        out_specs=P(("group", "tile", "list"), None),
        check_vma=False,
    )
```

```python
import functools

import jax
import jax.numpy as jnp
from jax import lax
from jax.experimental import pallas as pl
from jax.experimental.pallas import tpu as pltpu
from jax.sharding import PartitionSpec as P

BF = jnp.bfloat16
F32 = jnp.float32


def shifted(block, axis, distance):
    devices = range(lax.axis_size(axis))
    route = [(i - distance, i) for i in devices if i - distance in devices]
    return lax.ppermute(block, axis, route)


def image_part(operand, right_bases, left_bases, near_tiles, tile_ranks, column_rows, row_columns):
    tile_slots = right_bases.shape[1]
    rank_part = right_bases.shape[2]
    tile_rows = right_bases.shape[3]
    probe_count = operand.shape[1]
    tile_count = lax.axis_size("tile")
    right_flat = right_bases.reshape(tile_slots * rank_part, tile_rows)
    left_flat = left_bases.reshape(tile_slots * rank_part, tile_rows)
    dense_flat = near_tiles.reshape(tile_rows, -1)
    values = jnp.dot(
        right_flat,
        lax.all_gather(operand, "list", axis=0, tiled=True),
        preferred_element_type=F32,
    )
    rank_level = lax.axis_index("list") * rank_part + lax.iota(jnp.int32, rank_part)
    rank_mask = rank_level[None, :] < tile_ranks[0][:, None]
    coefficients = jnp.where(
        rank_mask[:, :, None], values.reshape(tile_slots, rank_part, probe_count), 0.0
    ).astype(BF)
    targets = (column_rows[0][None, :] == lax.iota(jnp.int32, tile_count)[:, None]).astype(BF)
    outgoing = jnp.einsum(
        "dk,krp->drp", targets, coefficients, preferred_element_type=F32
    ).astype(BF)
    sources = (row_columns[0][:, None] == lax.iota(jnp.int32, tile_count)[None, :]).astype(BF)
    chosen = jnp.einsum(
        "kj,jrp->krp",
        sources,
        lax.all_to_all(outgoing, "tile", split_axis=0, concat_axis=0, tiled=True),
        preferred_element_type=F32,
    ).astype(BF)
    chosen = chosen.reshape(tile_slots * rank_part, -1)
    far_sum = lax.dot_general(
        left_flat, chosen, (((0,), (0,)), ((), ())), preferred_element_type=F32
    )
    arrived = {}
    for offset in (1, -1):
        arrived[offset] = shifted(operand, "tile", offset)
    stacked = jnp.concatenate([arrived[1], operand, arrived[-1]], axis=0)
    near_sum = jnp.dot(dense_flat, stacked, preferred_element_type=F32)
    partial_image = near_sum + far_sum
    return lax.psum_scatter(partial_image, "list", scatter_dimension=0, tiled=True)


def many_slots(probes, right_bases, left_bases, near_tiles, tile_ranks, column_rows, row_columns):
    rest = (right_bases, left_bases, near_tiles, tile_ranks, column_rows, row_columns)
    first_pass = image_part(probes.astype(BF), *rest).astype(BF)
    return image_part(first_pass, *rest)


VMEM = pl.BlockSpec(memory_space=pltpu.VMEM)


def list_swap_in_pieces(block, bit, pieces):
    return jnp.concatenate([list_swap(piece, bit) for piece in jnp.split(block, pieces)])


def kernel_call(kernel, outs, operands, flops=0):
    return pl.pallas_call(
        kernel,
        out_shape=tuple(jax.ShapeDtypeStruct(shape, kind) for shape, kind in outs),
        in_specs=[VMEM] * len(operands),
        out_specs=tuple(VMEM for _ in outs),
        compiler_params=pltpu.CompilerParams(vmem_limit_bytes=16 * 2**20),
        cost_estimate=pl.CostEstimate(
            flops=flops, bytes_accessed=flops // 1024, transcendentals=0
        ),
    )(*operands)


def round_kernel(probes_ref, out_ref):
    out_ref[...] = probes_ref[...].astype(out_ref.dtype)


def join_kernel(right_ref, left_ref, out_ref):
    out_ref[0] = right_ref[0, 0]
    out_ref[1] = left_ref[0, 0]


def stacked(pieces):
    return jnp.concatenate([piece.astype(F32) for piece in pieces]).astype(BF)


def under_rank(sums, turns, rank_part, ranks_ref):
    me = lax.axis_index("list")
    groups = []
    for index, turn in enumerate(turns):
        values = sums[index * rank_part : (index + 1) * rank_part]
        level = (me ^ turn) * rank_part + lax.broadcasted_iota(jnp.int32, values.shape, 0)
        groups.append(jnp.where(level < ranks_ref[...], values, 0.0))
    return groups


def basis_groups(side, cut, refs):
    pieces = [ref[side, :, cut] for ref in refs[:2]]
    return stacked(pieces + [ref[index, :, cut] for ref in refs[2:] for index in range(2)])


def coefficient_kernel(bases_ref, across_ref, block_ref, beside_ref, ranks_ref, out_ref):
    me = lax.axis_index("list")
    rows = block_ref.shape[0]
    total = 0.0
    for part, operand_ref in ((me, block_ref), (me ^ 1, beside_ref)):
        cut = pl.ds(pl.multiple_of(part * rows, rows), rows)
        bases = basis_groups(0, cut, (bases_ref, across_ref))
        total += jnp.dot(bases, operand_ref[...], preferred_element_type=F32)
    groups = under_rank(total, (0, 2), bases_ref.shape[1], ranks_ref)
    out_ref[...] = jnp.concatenate(groups).astype(out_ref.dtype)


def tile_swap(block, turn):
    return lax.ppermute(block, "tile", [(i, i ^ turn) for i in range(lax.axis_size("tile"))])


def middle_swap(block):
    tiles, parts = lax.axis_size("tile"), lax.axis_size("list")
    route = []
    for tile in range(tiles):
        for part in range(parts):
            to = (tile - 1 + 2 * (tile % 2), part)
            if tile in (0, tiles - 1):
                to = (tile, part ^ 1)
            route.append((tile * parts + part, to[0] * parts + to[1]))
    return lax.ppermute(block, ("tile", "list"), route)


def far_swap(block):
    tiles, parts = lax.axis_size("tile"), lax.axis_size("list")
    route = [
        (tile * parts + part, (tile ^ (2 + part % 2)) * parts + part)
        for tile in range(tiles)
        for part in range(parts)
    ]
    return lax.ppermute(block, ("tile", "list"), route)


def list_swap(block, bit):
    return lax.ppermute(block, "list", [(i, i ^ bit) for i in range(lax.axis_size("list"))])


def near_choice(columns, tile, me, refs):
    chosen = refs[0][...]
    for turn in (1, 2, 3):
        chosen = jnp.where(columns == tile ^ turn, refs[turn][...], chosen)
    return chosen


def far_choice(columns, tile, me, refs):
    own_ref, near_by_ref, far_ref = refs
    half = own_ref.shape[0] // 2
    first = jnp.where(columns == tile, own_ref[:half, :], 0)
    first = jnp.where(columns == tile ^ 1, near_by_ref[...], first)
    far = columns == tile ^ (2 + lax.rem(me, 2))
    return jnp.concatenate(
        [jnp.where(far, far_ref[:half, :], first), jnp.where(far, far_ref[half:, :], 0)]
    )


def near_kernel(turns, near_ref, own_ref, second_ref, first_ref, *refs):
    base_refs, out_refs = refs[: -len(turns)], refs[-len(turns) :]
    count = lax.axis_size("tile")
    tile = lax.axis_index("tile")
    me = lax.axis_index("list")
    rows = near_ref.shape[2]
    odd = lax.rem(tile, 2)
    inside = (tile > 0) & (tile < count - 1)
    blocks = [
        (1, own_ref[...]),
        (2 - 2 * odd, first_ref[...]),
        (2 * odd, jnp.where(inside, second_ref[...], 0)),
    ]
    for index, turn in enumerate(turns):
        cut = pl.ds(pl.multiple_of((me ^ turn) * rows, rows), rows)
        total = base_refs[index][...] if base_refs else 0.0
        for side, block in blocks:
            total += jnp.dot(near_ref[side, cut, :], block, preferred_element_type=F32)
        out_refs[index][...] = total


def far_parts(choice, turns, columns_ref, bases_refs, coefficient_refs):
    me = lax.axis_index("list")
    chosen = choice(columns_ref[...], lax.axis_index("tile"), me, coefficient_refs)
    rows = bases_refs[0].shape[2] // 4
    for turn in turns:
        cut = pl.ds(pl.multiple_of((me ^ turn) * rows, rows), rows)
        left = basis_groups(1, cut, bases_refs)
        yield cut, lax.dot_general(
            left, chosen, (((0,), (0,)), ((), ())), preferred_element_type=F32
        )


def right_products(totals, bases_refs):
    return sum(
        jnp.dot(basis_groups(0, cut, bases_refs), total, preferred_element_type=F32)
        for cut, total in totals
    )


def first_kernel(turns, columns_ref, bases_ref, across_ref, other_ref, *refs):
    coefficient_refs, refs = refs[:4], refs[4:]
    base_refs, refs = refs[: len(turns)], refs[len(turns) :]
    last = 0 in turns
    (before_ref, ranks_ref), refs = (refs[:2], refs[2:]) if last else ((None, None), refs)
    bases_refs = (bases_ref, across_ref)
    totals = []
    parts = far_parts(near_choice, turns, columns_ref, bases_refs, coefficient_refs)
    for (cut, total), base_ref, out_ref in zip(parts, base_refs, refs):
        total += base_ref[...]
        out_ref[...] = total
        totals.append((cut, total.astype(BF)))
    if not last:
        return
    rows = before_ref.shape[0]
    cut = pl.ds(pl.multiple_of((lax.axis_index("list") ^ 3) * rows, rows), rows)
    totals.append((cut, before_ref[...].astype(BF)))
    sums = right_products(totals, (*bases_refs, other_ref))
    groups = under_rank(sums, (0, 2, 1, 3), bases_ref.shape[1], ranks_ref)
    refs[-2][...] = jnp.concatenate(groups)
    refs[-1][...] = jnp.concatenate(groups[2:] + groups[:2])


def far_kernel(turns, columns_ref, bases_ref, across_ref, other_ref, *refs):
    bases_refs = (bases_ref, across_ref, other_ref)
    parts = far_parts(far_choice, turns, columns_ref, bases_refs, refs[:3])
    for (_, total), out_ref in zip(parts, refs[3:]):
        out_ref[...] = total


def one_slot(probes, right_bases, left_bases, near_tiles, tile_ranks, column_rows, row_columns):
    rows, probe_count = probes.shape
    rank_part = right_bases.shape[2]
    near = near_tiles[0].transpose(1, 0, 2)
    flops = 2 * near.size * probe_count
    part = ((rows, probe_count), F32)
    ranks = 4 * rank_part

    (block,) = kernel_call(round_kernel, [(probes.shape, BF)], (probes,), 8 * flops)
    block, right, left = lax.optimization_barrier((block, right_bases, left_bases))
    (bases,) = kernel_call(join_kernel, [((2, *right_bases.shape[2:]), BF)], (right, left))
    across = list_swap(bases, 2)
    beside = [block, middle_swap(block), tile_swap(block, 1)]
    (own,) = kernel_call(
        coefficient_kernel,
        [((ranks // 2, probe_count), BF)],
        (bases, across, block, list_swap(block, 1), tile_ranks),
        8 * flops,
    )
    coefficients = [own] + [tile_swap(own, turn) for turn in (1, 2, 3)]
    right, _ = lax.optimization_barrier((jnp.stack([bases[0], across[0]]), own))
    fixed = (row_columns, bases, across)
    operands = (*fixed, list_swap(right, 1), *coefficients)
    small = ((ranks, probe_count), F32)

    def call(kernel, turns, operands, more=(), cost=1):
        outs = [part] * len(turns) + list(more)
        kernel = functools.partial(kernel, turns)
        return kernel_call(kernel, outs, operands, cost * len(turns) * flops // 4)

    base = call(near_kernel, (3, 2, 1, 0), (near, *beside), cost=0)
    (send,) = call(first_kernel, (3,), (*operands, base[0]))
    arrived = list_swap(send, 1)
    crossing, send, keep, own, other = call(
        first_kernel, (2, 1, 0), (*operands, *base[1:], send, tile_ranks), [small] * 2
    )
    crossed = list_swap((crossing + arrived).astype(BF), 2)
    own = (own + list_swap(other, 1)).astype(BF)
    near_by, far = tile_swap(own[: ranks // 2], 1), far_swap(own)
    block = (keep + list_swap(send, 1) + crossed).astype(BF)
    held, held_across, near_by, far, _ = lax.optimization_barrier(
        (bases, across, near_by, far, block)
    )
    beside = [block, middle_swap(block), tile_swap(block, 1)]
    left = list_swap(jnp.stack([held[1], held_across[1]]), 1)

    base = call(far_kernel, (3, 2, 1, 0), (*fixed, left, own, near_by, far), cost=0)
    (send,) = call(near_kernel, (3,), (near, *beside, base[0]))
    arrived = list_swap(send, 1)
    (keep,) = call(near_kernel, (2,), (near, *beside, base[1]))
    crossing = (keep + arrived).astype(BF)
    near, crossing = lax.optimization_barrier((near, crossing))
    crossed = list_swap(crossing, 2)
    send, keep = call(near_kernel, (1, 0), (near, *beside, *base[2:]))
    return keep + list_swap_in_pieces(send, 1, 2) + crossed


def local(probes, right_bases, left_bases, near_tiles, tile_ranks, column_rows, row_columns):
    few = lax.axis_size("tile") == 4 and lax.axis_size("list") == 4
    small = right_bases.shape[1] == 1 and few
    form = one_slot if small else many_slots
    return form(
        probes, right_bases, left_bases, near_tiles, tile_ranks, column_rows, row_columns
    )


def solution(mesh):
    placed = (
        P(("group", "tile", "list"), None),
        P(("group", "tile"), None, "list", None),
        P(("group", "tile"), None, "list", None),
        P(("group", "tile"), None, None, "list"),
        P(("group", "tile"), None),
        P("tile", None),
        P("tile", None),
    )
    return jax.shard_map(
        local,
        mesh=mesh,
        in_specs=placed,
        out_specs=P(("group", "tile", "list"), None),
        check_vma=False,
    )
```
